32 devices in a mesh: ctx: 8 (over y, x, core), ch: 4 (over z).
Axes of the slice: x: 2, y: 2, z: 4, core: 2. Of those that a mesh axis runs over, the one named last changes fastest.
Arguments:
- signal: bfloat16 [2048, 2048], P('ctx', 'ch'), may hold values from -8 to 8
- cotangent: bfloat16 [2048, 2048], P('ctx', 'ch'), may hold values from -8 to 8
- residue: float32 [16, 512], replicated, may hold values from -0.125 to 0.125
- decay: float32 [16, 512], replicated, may hold values from 0.00048828125 to 0.2
Outputs:
- conv_out: bfloat16 [2048, 2048], P('ctx', 'ch')
- signal_grad: bfloat16 [2048, 2048], P('ctx', 'ch')
- residue_grad: float32 [16, 512], replicated
The draws below stay inside these ranges and needn't reach their ends.
All inputs are finite; a program needn't handle non-finite values.
Results may differ from the reference program's by a relative error of at most 0.0013.
Values sent between devices are 32-bit elements; how exact they have to be, the bound alone decides.
No kernel may reach another device: no remote copies, remote signals or barrier semaphores. Data moves between devices by JAX's collectives and lax.ppermute only.
A program may use at most 64 MiB of HBM per device.

```python
import math
import jax
import jax.numpy as jnp
from jax import lax

CH_DEV = 512
MODES = 16
TOK_DEV = 256
LENGTH = 2048
CHANNELS = 2048
N_CTX = 8
N_CH = 4


def block_pattern(key, amplitude):
    positions = (jnp.arange(LENGTH, dtype=jnp.int32) % TOK_DEV).astype(jnp.float32)
    centred = (2.0 * positions + 1.0) / TOK_DEV - 1.0
    angles = jnp.arccos(centred)[:, None]
    weights = jax.random.normal(key, (8, CHANNELS), jnp.float32) * (amplitude / 8.0 ** 0.5)
    total = jnp.zeros((LENGTH, CHANNELS), jnp.float32)
    for order in range(8):
        total = total + jnp.cos((order + 6.0) * angles) * weights[order][None, :]
    return total


def mixed_field(key):
    noise_key = jax.random.fold_in(key, 11)
    shape_key = jax.random.fold_in(key, 12)
    noise = 0.7 * jax.random.normal(noise_key, (LENGTH, CHANNELS), jnp.float32)
    amplitude = 2.0
    value = noise + block_pattern(shape_key, amplitude)
    return jnp.clip(value, -8.0, 8.0).astype(jnp.bfloat16)


def draw_signal(key, part):
    return mixed_field(jax.random.fold_in(key, 101))


def draw_cotangent(key, part):
    return mixed_field(jax.random.fold_in(key, 202))


def gaussian(stream_key, dims, deviation, reach, kind=jnp.bfloat16):
    drawn = jax.random.normal(stream_key, dims, jnp.float32) * deviation
    return jnp.minimum(jnp.maximum(drawn, -reach), reach).astype(kind)


def setup_inputs(seed: int = 0) -> dict:
    arg_keys = jax.random.split(jax.random.key(seed), 5)
    signal = draw_signal(jax.random.fold_in(arg_keys[4], 71), 0)
    cotangent = draw_cotangent(jax.random.fold_in(arg_keys[4], 71), 0)
    residue = gaussian(arg_keys[2], (MODES, CH_DEV), 0.02, 0.125, jnp.float32)
    decay = jnp.clip(jnp.exp(jax.random.uniform(arg_keys[3], (MODES, CH_DEV), jnp.float32, math.log(0.00048828125), math.log(0.2))), 0.00048828125, 0.2)
    return {"signal": signal, "cotangent": cotangent, "residue": residue, "decay": decay}


def combine_pairs(earlier, latter):
    return (earlier[0] * latter[0], earlier[1] * latter[0] + latter[1])


def local_block(signal, cotangent, residue, decay):
    values = signal.astype(jnp.float32)
    cotans = cotangent.astype(jnp.float32)

    def per_mode(totals, mode_params):
        residue_row, decay_row = mode_params
        step_decay = jnp.broadcast_to(jnp.exp(-decay_row), values.shape)
        forward_sum = lax.associative_scan(combine_pairs, (step_decay, values), axis=0)[1]
        backward_sum = lax.associative_scan(combine_pairs, (step_decay, cotans), axis=0, reverse=True)[1]
        out_acc, grad_acc = totals
        totals = (out_acc + residue_row * forward_sum, grad_acc + residue_row * backward_sum)
        return totals, (forward_sum[-1], backward_sum[0], jnp.sum(cotans * forward_sum, axis=0))

    empty_acc = jnp.zeros(values.shape, jnp.float32)
    (out_acc, grad_acc), (closing, opening, local_grad) = lax.scan(per_mode, (empty_acc, empty_acc), (residue, decay))
    return out_acc, grad_acc, closing, opening, local_grad


def finish(out_acc, grad_acc, residue, decay, incoming, outgoing):
    block_len = out_acc.shape[0]
    offsets = jnp.arange(block_len, dtype=jnp.float32)[:, None]

    def per_mode(totals, mode_params):
        residue_row, decay_row, arriving, leaving = mode_params
        first, second = totals
        first = first + residue_row * jnp.exp(-decay_row * (offsets + 1.0)) * arriving
        second = second + residue_row * jnp.exp(-decay_row * (block_len - offsets)) * leaving
        return (first, second), None

    (first, second), _ = lax.scan(per_mode, (out_acc, grad_acc), (residue, decay, incoming, outgoing))
    return first.astype(jnp.bfloat16), second.astype(jnp.bfloat16)


def reference(signal, cotangent, residue, decay):
    blocks = signal.reshape(N_CTX, TOK_DEV, N_CH, CH_DEV).transpose(0, 2, 1, 3)
    cotans = cotangent.reshape(N_CTX, TOK_DEV, N_CH, CH_DEV).transpose(0, 2, 1, 3)

    def one_block(block_pair):
        return jax.vmap(lambda first, second: local_block(first, second, residue, decay))(block_pair[0], block_pair[1])

    out_acc, grad_acc, closing, opening, local_grad = lax.map(one_block, (blocks, cotans))
    block_decay = jnp.exp(-decay * TOK_DEV)

    def advance(running, element):
        return block_decay * running + element, running

    start_state = jnp.zeros((N_CH, MODES, CH_DEV), jnp.float32)
    _, incoming = lax.scan(advance, start_state, closing)
    _, outgoing = lax.scan(advance, start_state, opening, reverse=True)
    summed = jnp.sum(local_grad + jnp.exp(-decay) * opening * incoming, axis=(0, 1))
    residue_grad = summed / (TOK_DEV * N_CTX)

    def finish_block(items):
        return jax.vmap(lambda first, second, arriving, leaving: finish(first, second, residue, decay, arriving, leaving))(*items)

    conv_out, signal_grad = lax.map(finish_block, (out_acc, grad_acc, incoming, outgoing))
    conv_out = conv_out.transpose(0, 2, 1, 3).reshape(TOK_DEV * N_CTX, N_CH * CH_DEV)
    signal_grad = signal_grad.transpose(0, 2, 1, 3).reshape(TOK_DEV * N_CTX, N_CH * CH_DEV)
    return conv_out, signal_grad, residue_grad
```

```python
import functools

import jax
import jax.numpy as jnp
from jax import lax
from jax.experimental import pallas as pl
from jax.experimental.pallas import tpu as pltpu
from jax.sharding import PartitionSpec as P

SUB = 8
LANES = 128
F32 = jnp.float32


def row(ref, *index):
    return jnp.broadcast_to(ref[index], (SUB, LANES))


def split_lanes(source, target, tile):
    lanes = pl.ds(pl.multiple_of(tile * LANES, LANES), LANES)
    target[...] = source[:, lanes].astype(F32)


def read_tokens(scratch, chunks):
    span = chunks * SUB
    return [[scratch[pl.ds(p * SUB + r, SUB, stride=span), :] for r in range(SUB)] for p in range(chunks)]


def powers(decay, pw):
    pw[0] = jnp.exp(-decay)
    pw[1] = jnp.exp(-decay * SUB)


def horner(terms, factor):
    total = terms[0]
    for term in terms[1:]:
        total = total * factor + term
    return total


def chunk_states(m, xs, gs, pw):
    a, a8 = row(pw, 0, pl.ds(m, 1)), row(pw, 1, pl.ds(m, 1))
    chunks = len(xs)
    held, back = [], [None] * chunks
    for p in range(chunks):
        own = horner(xs[p], a)
        held.append(own if p == 0 else held[-1] * a8 + own)
    opens = [horner(gs[p][::-1], a) for p in range(chunks)]
    for p in reversed(range(chunks)):
        back[p] = opens[p] if p == chunks - 1 else back[p + 1] * a8 + opens[p]
    return held, back, opens


def by_span(scratch, half, j):
    return scratch[pl.ds(half * SUB * SUB + j, SUB, stride=SUB), :]


def gather_kernel(direct, n, x_ref, g_ref, decay_ref, *refs):
    modes, channels = decay_ref.shape
    chunks = x_ref.shape[0] // (SUB * SUB)
    span = chunks * SUB
    if direct:
        place = lax.axis_index("ctx")
        share = modes // n
        *messages, own, xf, gf, pw, ends, starts, inner, closing, opening, grad, parts = refs
    else:
        closing, opening, grad, xf, gf, pw, ends, starts, inner = refs

    def tile_step(tile, _):
        lanes = pl.ds(pl.multiple_of(tile * LANES, LANES), LANES)
        split_lanes(x_ref, xf, tile)
        split_lanes(g_ref, gf, tile)
        decay = decay_ref[:, lanes]
        powers(decay, pw)
        xs, gs = read_tokens(xf, chunks), read_tokens(gf, chunks)
        for m in range(modes):
            held, back, opens = chunk_states(m, xs, gs, pw)
            rows = pl.ds(m * SUB, SUB)
            ends[rows, :] = held[-1]
            starts[rows, :] = back[0]
            inner[rows, :] = sum(opens[p] * held[p - 1] for p in range(1, chunks))
        lagged = []
        for lag in range(SUB):
            pairs = [gs[p][r] * xs[p][r - lag] for p in range(chunks) for r in range(lag, SUB)]
            lagged.append(jnp.sum(sum(pairs), axis=0, keepdims=True))
        for half in range(modes // SUB):
            some = pl.ds(half * SUB, SUB)
            a = pw[0, some, :]
            across = jnp.exp(-decay[half * SUB:(half + 1) * SUB] * span)
            arriving = jnp.zeros((SUB, LANES), F32)
            cross = jnp.zeros((SUB, LANES), F32)
            for j in range(SUB):
                cross = cross + (by_span(inner, half, j) + by_span(starts, half, j) * arriving)
                arriving = arriving * across + by_span(ends, half, j)
            leaving = horner([by_span(starts, half, j) for j in reversed(range(SUB))], across)
            near = horner([jnp.broadcast_to(v, (SUB, LANES)) for v in reversed(lagged)], a)
            closing[some, lanes] = arriving
            opening[some, lanes] = leaving
            grad[some, lanes] = near + a * cross
        return 0

    lax.fori_loop(0, channels // LANES, tile_step, 0)

    if direct:
        for owner in range(n):
            rows = slice(owner * share, (owner + 1) * share)
            parts[owner, 0:share] = closing[rows]
            parts[owner, share:2 * share] = opening[rows]
            parts[owner, 2 * share:3 * share] = grad[rows]
            parts[owner, 3 * share:4 * share] = decay_ref[rows]
        own[...] = parts[place]
        for k in range(1, n):
            message = messages[k - 1]
            message[0:modes] = jnp.where(place + k < n, closing[...], opening[...])
            message[modes:] = parts[lax.rem(place + k, n)]


def local_kernel(x_ref, g_ref, residue_ref, decay_ref, out_ref, back_ref,
                 xf, gf, pw, ends, starts, before, after, arrive, leave):
    modes, channels = decay_ref.shape
    chunks = x_ref.shape[0] // (SUB * SUB)
    span = chunks * SUB

    def tile_step(tile, _):
        lanes = pl.ds(pl.multiple_of(tile * LANES, LANES), LANES)
        split_lanes(x_ref, xf, tile)
        split_lanes(g_ref, gf, tile)
        decay = decay_ref[:, lanes]
        residue = residue_ref[:, lanes]
        powers(decay, pw)
        pw[2] = residue * pw[0]
        xs, gs = read_tokens(xf, chunks), read_tokens(gf, chunks)
        for m in range(modes):
            held, back, _ = chunk_states(m, xs, gs, pw)
            rows = pl.ds(m * SUB, SUB)
            ends[rows, :] = held[-1]
            starts[rows, :] = back[0]
            for p in range(1, chunks):
                before[m, p - 1] = held[p - 1]
                after[m, p - 1] = back[p]
        for half in range(modes // SUB):
            across = jnp.exp(-decay[half * SUB:(half + 1) * SUB] * span)
            for target, source, order in ((arrive, ends, range(SUB)), (leave, starts, range(SUB - 1, -1, -1))):
                running = jnp.zeros((SUB, LANES), F32)
                for j in order:
                    target[pl.ds(half * SUB * SUB + j, SUB, stride=SUB), :] = running
                    running = running * across + by_span(source, half, j)
        taps = []
        weight = residue
        for lag in range(SUB):
            taps.append(jnp.broadcast_to(jnp.sum(weight, axis=0, keepdims=True), (SUB, LANES)))
            weight = weight * pw[0]
        for values, carried, inside, target, forward in (
            (xs, arrive, before, out_ref, True), (gs, leave, after, back_ref, False)
        ):
            order = range(SUB) if forward else range(SUB - 1, -1, -1)
            totals = []
            for p in range(chunks):
                seq = [values[p][r] for r in order]
                totals.append([sum(taps[lag] * seq[r - lag] for lag in range(r + 1)) for r in range(SUB)])
            for m in range(modes):
                a, a8, first = (row(pw, i, pl.ds(m, 1)) for i in range(3))
                edge = carried[pl.ds(m * SUB, SUB), :]
                for q in range(chunks):
                    p = q if forward else chunks - 1 - q
                    if q == 0:
                        state = edge
                    else:
                        edge = edge * a8
                        state = edge + inside[m, p - 1 if forward else p]
                    wave = state * first
                    for r in range(SUB):
                        totals[p][r] = totals[p][r] + wave
                        if r < SUB - 1:
                            wave = wave * a
            for p in range(chunks):
                for r, at in enumerate(order):
                    target[p * SUB + at, :, lanes] = totals[p][r]
        return 0

    lax.fori_loop(0, channels // LANES, tile_step, 0)


def owner_kernel(n, scale, *refs):
    *messages, own, out_ref, held, back = refs
    place = lax.axis_index("ctx")
    share = own.shape[0] // 4
    decay = own[3 * share:]
    total = own[2 * share:3 * share]
    held[place] = own[0:share]
    back[place] = own[share:2 * share]
    for k in range(1, n):
        source = lax.rem(place - k + n, n)
        held[source] = messages[k - 1][0:share]
        back[source] = messages[k - 1][share:2 * share]
        total = total + messages[k - 1][2 * share:3 * share]
    a = jnp.exp(-decay)
    block = jnp.exp(-decay * scale[0])
    arriving = jnp.zeros_like(decay)
    cross = jnp.zeros_like(decay)
    for j in range(n):
        cross = cross + back[j] * arriving
        arriving = arriving * block + held[j]
    out_ref[...] = (total + a * cross) * (1.0 / (scale[0] * n))


def finish_kernel(direct, n, residue_ref, decay_ref, near_out, near_back, *refs):
    modes, channels = decay_ref.shape
    chunks = near_out.shape[0] // SUB
    span = chunks * SUB
    *sources, out_ref, back_ref, result, pw, arrive, leave = refs
    decay = decay_ref[...]
    if direct:
        place = lax.axis_index("ctx")
        block = jnp.exp(-decay * (span * SUB))
        incoming = jnp.zeros_like(decay)
        outgoing = jnp.zeros_like(decay)
        for k in range(n - 1, 0, -1):
            incoming = incoming * block + jnp.where(place >= k, sources[k - 1][...], 0.0)
        for k in range(1, n):
            outgoing = outgoing * block + jnp.where(place < k, sources[k - 1][...], 0.0)
    else:
        incoming, outgoing = sources[0][...], sources[1][...]
    first = residue_ref[...] * jnp.exp(-decay)
    arrive[...] = incoming * first
    leave[...] = outgoing * first

    def tile_step(tile, _):
        lanes = pl.ds(pl.multiple_of(tile * LANES, LANES), LANES)
        decay = decay_ref[:, lanes]
        powers(decay, pw)
        pw[2] = decay * (-1.0 * span)
        pw[3] = arrive[:, lanes]
        pw[4] = leave[:, lanes]
        level = lax.broadcasted_iota(jnp.int32, (SUB, LANES), 0).astype(F32)
        for near, target, forward in ((near_out, out_ref, True), (near_back, back_ref, False)):
            order = range(SUB) if forward else range(SUB - 1, -1, -1)
            spans = level if forward else SUB - 1.0 - level
            totals = [[near[p * SUB + r, :, lanes] for r in range(SUB)] for p in range(chunks)]
            for m in range(modes):
                a, a8, rate = (row(pw, i, pl.ds(m, 1)) for i in range(3))
                state = row(pw, 3 if forward else 4, pl.ds(m, 1)) * jnp.exp(rate * spans)
                for q in range(chunks):
                    p = q if forward else chunks - 1 - q
                    wave = state
                    for r in order:
                        totals[p][r] = totals[p][r] + wave
                        wave = wave * a
                    if q < chunks - 1:
                        state = state * a8
            for p in range(chunks):
                for r in range(SUB):
                    result[pl.ds(p * SUB + r, SUB, stride=span), :] = totals[p][r]
            target[:, lanes] = result[...].astype(target.dtype)
        return 0

    lax.fori_loop(0, channels // LANES, tile_step, 0)


def assemble_kernel(n, *refs):
    *pieces, out_ref, parts = refs
    place = lax.axis_index("ctx")
    share = pieces[0].shape[0]
    for k in range(n):
        parts[lax.rem(place - k + n, n)] = pieces[k][...]
    for j in range(n):
        out_ref[j * share:(j + 1) * share] = parts[j]


def vmem(*shape):
    return pltpu.VMEM(shape, F32)


def shaped(*shape):
    return jax.ShapeDtypeStruct(shape, F32)


def cost(flops, transcendentals, nbytes):
    return pl.CostEstimate(flops=flops, transcendentals=transcendentals, bytes_accessed=nbytes)


PARAMS = pltpu.CompilerParams(vmem_limit_bytes=32 * 1024 * 1024)
WHOLE = pl.BlockSpec(memory_space=pltpu.VMEM)


def carried_in(own, block_decay, reverse):
    devices, place = lax.axis_size("ctx"), lax.axis_index("ctx")
    everything = lax.all_gather(own, "ctx")

    def step(k, before):
        at = devices - 1 - k if reverse else k
        reached = at > place if reverse else at < place
        return jnp.where(reached, block_decay * before + everything[at], before)

    return lax.fori_loop(0, devices, step, jnp.zeros_like(own))


def body(signal, cotangent, residue, decay):
    tokens, channels = signal.shape
    modes = decay.shape[0]
    n, n_ch = lax.axis_size("ctx"), lax.axis_size("ch")
    chunks = tokens // (SUB * SUB)
    direct = n <= SUB and modes % n == 0
    elements = tokens * channels
    tokens_scratch = [vmem(tokens, LANES), vmem(tokens, LANES)]
    spans = vmem(modes * SUB, LANES)

    if direct:
        share = modes // n
        gathered = pl.pallas_call(
            functools.partial(gather_kernel, True, n),
            out_shape=[shaped(modes + 4 * share, channels)] * (n - 1) + [shaped(4 * share, channels)],
            scratch_shapes=tokens_scratch + [vmem(2, modes, LANES), spans, spans, spans]
            + [vmem(modes, channels)] * 3 + [vmem(n, 4 * share, channels)],
            compiler_params=PARAMS,
            cost_estimate=cost(elements * modes * 5, modes * channels * 3, elements * 6),
            name="block_states",
        )(signal, cotangent, decay)
        *messages, own = gathered
        arrived = [
            lax.ppermute(messages[k - 1], "ctx", [(i, (i + k) % n) for i in range(n)]) for k in range(1, n)
        ]
    else:
        closing, opening, local_grad = pl.pallas_call(
            functools.partial(gather_kernel, False, n),
            out_shape=[shaped(modes, channels)] * 3,
            scratch_shapes=tokens_scratch + [vmem(2, modes, LANES), spans, spans, spans],
            compiler_params=PARAMS,
            cost_estimate=cost(elements * modes * 5, modes * channels * 3, elements * 6),
            name="block_states",
        )(signal, cotangent, decay)

    near_out, near_back = pl.pallas_call(
        local_kernel,
        out_shape=[shaped(chunks * SUB, SUB, channels)] * 2,
        scratch_shapes=tokens_scratch + [vmem(3, modes, LANES), spans, spans]
        + [vmem(modes, chunks - 1, SUB, LANES)] * 2 + [spans, spans],
        compiler_params=PARAMS,
        cost_estimate=cost(elements * modes * 10, modes * channels * 3, elements * 12),
        name="local_convolutions",
    )(signal, cotangent, residue, decay)

    if direct:
        part = pl.pallas_call(
            functools.partial(owner_kernel, n, (float(tokens),)),
            out_shape=shaped(share, channels),
            grid=(1,),
            in_specs=[pl.BlockSpec((4 * share, channels), lambda i: (modes // (4 * share), 0))] * (n - 1) + [WHOLE],
            out_specs=WHOLE,
            scratch_shapes=[vmem(n, share, channels)] * 2,
            compiler_params=PARAMS,
            cost_estimate=cost(elements, modes * channels, modes * channels * 16),
            name="owned_modes",
        )(*arrived, own)
        over_groups = [part]
        for k in range(1, n_ch):
            over_groups.append(lax.ppermute(part, "ch", [(i, i ^ k) for i in range(n_ch)]))
        while len(over_groups) > 1:
            over_groups = [a + b for a, b in zip(over_groups[::2], over_groups[1::2])]
        whole = over_groups[0]
        pieces = [whole] + [
            lax.ppermute(whole, "ctx", [(i, (i + k) % n) for i in range(n)]) for k in range(1, n)
        ]
        residue_grad = pl.pallas_call(
            functools.partial(assemble_kernel, n),
            out_shape=shaped(modes, channels),
            scratch_shapes=[vmem(n, share, channels)],
            compiler_params=PARAMS,
            cost_estimate=cost(modes * channels, 0, modes * channels * 8),
            name="assemble_gradient",
        )(*pieces)
        sources = arrived
        source_specs = [pl.BlockSpec((modes, channels), lambda i: (0, 0))] * (n - 1)
    else:
        block_decay = jnp.exp(-decay * tokens)
        incoming = carried_in(closing, block_decay, False)
        outgoing = carried_in(opening, block_decay, True)
        summed = lax.psum(local_grad + jnp.exp(-decay) * opening * incoming, ("ctx", "ch"))
        residue_grad = summed / (tokens * n)
        sources = [incoming, outgoing]
        source_specs = [WHOLE] * 2

    conv_out, signal_grad = pl.pallas_call(
        functools.partial(finish_kernel, direct, n),
        out_shape=[jax.ShapeDtypeStruct((tokens, channels), signal.dtype)] * 2,
        grid=(1,),
        in_specs=[WHOLE] * 4 + source_specs,
        out_specs=[WHOLE] * 2,
        scratch_shapes=[vmem(tokens, LANES), vmem(5, modes, LANES)] + [vmem(modes, channels)] * 2,
        compiler_params=PARAMS,
        cost_estimate=cost(elements * modes * 4, modes * channels * 10, elements * 12),
        name="add_arrivals",
    )(residue, decay, near_out, near_back, *sources)
    return conv_out, signal_grad, residue_grad


def solution(mesh):
    return jax.shard_map(
        body,
        mesh=mesh,
        in_specs=(P("ctx", "ch"), P("ctx", "ch"), P(), P()),
        out_specs=(P("ctx", "ch"), P("ctx", "ch"), P()),
        check_vma=False,
    )
```

```python
import functools

import jax
import jax.numpy as jnp
from jax import lax
from jax.experimental import pallas as pl
from jax.experimental.pallas import tpu as pltpu
from jax.sharding import PartitionSpec as P

SUB = 8
LANES = 128
F32 = jnp.float32


def row(ref, *index):
    return jnp.broadcast_to(ref[index], (SUB, LANES))


def split_lanes(source, target, tile):
    lanes = pl.ds(pl.multiple_of(tile * LANES, LANES), LANES)
    target[...] = source[:, lanes].astype(F32)


def read_tokens(scratch, chunks):
    span = chunks * SUB
    return [[scratch[pl.ds(p * SUB + r, SUB, stride=span), :] for r in range(SUB)] for p in range(chunks)]


def powers(decay, pw):
    pw[0] = jnp.exp(-decay)
    pw[1] = jnp.exp(-decay * SUB)


def horner(terms, factor):
    total = terms[0]
    for term in terms[1:]:
        total = total * factor + term
    return total


def chunk_states(m, xs, gs, pw):
    a, a8 = row(pw, 0, pl.ds(m, 1)), row(pw, 1, pl.ds(m, 1))
    chunks = len(xs)
    held, back = [], [None] * chunks
    for p in range(chunks):
        own = horner(xs[p], a)
        held.append(own if p == 0 else held[-1] * a8 + own)
    opens = [horner(gs[p][::-1], a) for p in range(chunks)]
    for p in reversed(range(chunks)):
        back[p] = opens[p] if p == chunks - 1 else back[p + 1] * a8 + opens[p]
    return held, back, opens


def by_span(scratch, half, j):
    return scratch[pl.ds(half * SUB * SUB + j, SUB, stride=SUB), :]


def gather_kernel(direct, n, x_hbm, g_hbm, decay_hbm, *refs):
    *refs, x_ref, g_ref, decay_ref, sems = refs
    copies = [
        pltpu.make_async_copy(source, target, sems.at[i])
        for i, (source, target) in enumerate(((x_hbm, x_ref), (g_hbm, g_ref), (decay_hbm, decay_ref)))
    ]
    for copy in copies:
        copy.start()
    modes, channels = decay_ref.shape
    chunks = x_ref.shape[0] // (SUB * SUB)
    span = chunks * SUB
    if direct:
        place = lax.axis_index("ctx")
        share = modes // n
        messages, xf, gf, pw, ends, starts, inner, closing, opening, grad, parts = refs
    else:
        closing, opening, grad, xf, gf, pw, ends, starts, inner = refs
    for copy in copies:
        copy.wait()

    def tile_step(tile, _):
        lanes = pl.ds(pl.multiple_of(tile * LANES, LANES), LANES)
        split_lanes(x_ref, xf, tile)
        split_lanes(g_ref, gf, tile)
        decay = decay_ref[:, lanes]
        powers(decay, pw)
        xs, gs = read_tokens(xf, chunks), read_tokens(gf, chunks)
        for m in range(modes):
            held, back, opens = chunk_states(m, xs, gs, pw)
            rows = pl.ds(m * SUB, SUB)
            ends[rows, :] = held[-1]
            starts[rows, :] = back[0]
            inner[rows, :] = sum(opens[p] * held[p - 1] for p in range(1, chunks))
        lagged = []
        for lag in range(SUB):
            pairs = [gs[p][r] * xs[p][r - lag] for p in range(chunks) for r in range(lag, SUB)]
            lagged.append(jnp.sum(sum(pairs), axis=0, keepdims=True))
        for half in range(modes // SUB):
            some = pl.ds(half * SUB, SUB)
            a = pw[0, some, :]
            across = jnp.exp(-decay[half * SUB:(half + 1) * SUB] * span)
            arriving = jnp.zeros((SUB, LANES), F32)
            cross = jnp.zeros((SUB, LANES), F32)
            for j in range(SUB):
                cross = cross + (by_span(inner, half, j) + by_span(starts, half, j) * arriving)
                arriving = arriving * across + by_span(ends, half, j)
            leaving = horner([by_span(starts, half, j) for j in reversed(range(SUB))], across)
            near = horner([jnp.broadcast_to(v, (SUB, LANES)) for v in reversed(lagged)], a)
            closing[some, lanes] = arriving
            opening[some, lanes] = leaving
            grad[some, lanes] = near + a * cross
        return 0

    lax.fori_loop(0, channels // LANES, tile_step, 0)

    if direct:
        for owner in range(n):
            rows = slice(owner * share, (owner + 1) * share)
            parts[owner, 0:share] = closing[rows]
            parts[owner, share:2 * share] = opening[rows]
            parts[owner, 2 * share:3 * share] = grad[rows]
            parts[owner, 3 * share:4 * share] = decay_ref[rows]
        for k in range(n):
            messages[k, 0:modes] = jnp.where(k > place, closing[...], opening[...])
            messages[k, modes:] = parts[k]


def local_kernel(x_ref, g_ref, residue_ref, decay_ref, out_ref, back_ref,
                 xf, gf, pw, ends, starts, before, after, arrive, leave):
    modes, channels = decay_ref.shape
    chunks = x_ref.shape[0] // (SUB * SUB)
    span = chunks * SUB

    def tile_step(tile, _):
        lanes = pl.ds(pl.multiple_of(tile * LANES, LANES), LANES)
        split_lanes(x_ref, xf, tile)
        split_lanes(g_ref, gf, tile)
        decay = decay_ref[:, lanes]
        residue = residue_ref[:, lanes]
        powers(decay, pw)
        pw[2] = residue * pw[0]
        xs, gs = read_tokens(xf, chunks), read_tokens(gf, chunks)
        for m in range(modes):
            held, back, _ = chunk_states(m, xs, gs, pw)
            rows = pl.ds(m * SUB, SUB)
            ends[rows, :] = held[-1]
            starts[rows, :] = back[0]
            for p in range(1, chunks):
                before[m, p - 1] = held[p - 1]
                after[m, p - 1] = back[p]
        for half in range(modes // SUB):
            across = jnp.exp(-decay[half * SUB:(half + 1) * SUB] * span)
            for target, source, order in ((arrive, ends, range(SUB)), (leave, starts, range(SUB - 1, -1, -1))):
                running = jnp.zeros((SUB, LANES), F32)
                for j in order:
                    target[pl.ds(half * SUB * SUB + j, SUB, stride=SUB), :] = running
                    running = running * across + by_span(source, half, j)
        taps = []
        weight = residue
        for lag in range(SUB):
            taps.append(jnp.broadcast_to(jnp.sum(weight, axis=0, keepdims=True), (SUB, LANES)))
            weight = weight * pw[0]
        for values, carried, inside, target, forward in (
            (xs, arrive, before, out_ref, True), (gs, leave, after, back_ref, False)
        ):
            order = range(SUB) if forward else range(SUB - 1, -1, -1)
            totals = []
            for p in range(chunks):
                seq = [values[p][r] for r in order]
                totals.append([sum(taps[lag] * seq[r - lag] for lag in range(r + 1)) for r in range(SUB)])
            for m in range(modes):
                a, a8, first = (row(pw, i, pl.ds(m, 1)) for i in range(3))
                edge = carried[pl.ds(m * SUB, SUB), :]
                for q in range(chunks):
                    p = q if forward else chunks - 1 - q
                    if q == 0:
                        state = edge
                    else:
                        edge = edge * a8
                        state = edge + inside[m, p - 1 if forward else p]
                    wave = state * first
                    for r in range(SUB):
                        totals[p][r] = totals[p][r] + wave
                        if r < SUB - 1:
                            wave = wave * a
            for p in range(chunks):
                for r, at in enumerate(order):
                    target[p * SUB + at, :, lanes] = totals[p][r]
        return 0

    lax.fori_loop(0, channels // LANES, tile_step, 0)


def owner_kernel(scale, arrived, out_ref):
    n, rows, _ = arrived.shape
    share = rows // 4
    decay = arrived[0, 3 * share:]
    a = jnp.exp(-decay)
    block = jnp.exp(-decay * scale)
    arriving = jnp.zeros_like(decay)
    cross = jnp.zeros_like(decay)
    total = jnp.zeros_like(decay)
    for j in range(n):
        cross = cross + arrived[j, share:2 * share] * arriving
        arriving = arriving * block + arrived[j, 0:share]
        total = total + arrived[j, 2 * share:3 * share]
    out_ref[...] = (total + a * cross) * (1.0 / (scale * n))


def finish_kernel(direct, n, residue_ref, decay_ref, near_out, near_back, *refs):
    modes, channels = decay_ref.shape
    chunks = near_out.shape[0] // SUB
    span = chunks * SUB
    *sources, out_ref, back_ref, result, pw, arrive, leave = refs
    decay = decay_ref[...]
    if direct:
        place = lax.axis_index("ctx")
        block = jnp.exp(-decay * (span * SUB))
        incoming = jnp.zeros_like(decay)
        outgoing = jnp.zeros_like(decay)
        arrived, = sources
        for k in range(n):
            incoming = jnp.where(k < place, incoming * block + arrived[k], incoming)
        for k in reversed(range(n)):
            outgoing = jnp.where(k > place, outgoing * block + arrived[k], outgoing)
    else:
        incoming, outgoing = sources[0][...], sources[1][...]
    first = residue_ref[...] * jnp.exp(-decay)
    arrive[...] = incoming * first
    leave[...] = outgoing * first

    def tile_step(tile, _):
        lanes = pl.ds(pl.multiple_of(tile * LANES, LANES), LANES)
        decay = decay_ref[:, lanes]
        powers(decay, pw)
        pw[2] = decay * (-1.0 * span)
        pw[3] = arrive[:, lanes]
        pw[4] = leave[:, lanes]
        level = lax.broadcasted_iota(jnp.int32, (SUB, LANES), 0).astype(F32)
        for near, target, forward in ((near_out, out_ref, True), (near_back, back_ref, False)):
            order = range(SUB) if forward else range(SUB - 1, -1, -1)
            spans = level if forward else SUB - 1.0 - level
            totals = [[near[p * SUB + r, :, lanes] for r in range(SUB)] for p in range(chunks)]
            for m in range(modes):
                a, a8, rate = (row(pw, i, pl.ds(m, 1)) for i in range(3))
                state = row(pw, 3 if forward else 4, pl.ds(m, 1)) * jnp.exp(rate * spans)
                for q in range(chunks):
                    p = q if forward else chunks - 1 - q
                    wave = state
                    for r in order:
                        totals[p][r] = totals[p][r] + wave
                        wave = wave * a
                    if q < chunks - 1:
                        state = state * a8
            for p in range(chunks):
                for r in range(SUB):
                    result[pl.ds(p * SUB + r, SUB, stride=span), :] = totals[p][r]
            target[:, lanes] = result[...].astype(target.dtype)
        return 0

    lax.fori_loop(0, channels // LANES, tile_step, 0)


def assemble_kernel(n, pieces, out_ref):
    share = pieces.shape[1]
    groups = pieces.shape[0] // n
    for owner in range(n):
        terms = [pieces[owner * groups + k] for k in range(groups)]
        out_ref[owner * share:(owner + 1) * share] = sum(terms[1:], terms[0])


def vmem(*shape):
    return pltpu.VMEM(shape, F32)


def shaped(*shape):
    return jax.ShapeDtypeStruct(shape, F32)


def cost(flops, transcendentals, nbytes):
    return pl.CostEstimate(flops=flops, transcendentals=transcendentals, bytes_accessed=nbytes)


PARAMS = pltpu.CompilerParams(vmem_limit_bytes=32 * 1024 * 1024)
WHOLE = pl.BlockSpec(memory_space=pltpu.VMEM)
HBM = pl.BlockSpec(memory_space=pltpu.HBM)


def carried_in(own, block_decay, reverse):
    devices, place = lax.axis_size("ctx"), lax.axis_index("ctx")
    everything = lax.all_gather(own, "ctx")

    def step(k, before):
        at = devices - 1 - k if reverse else k
        reached = at > place if reverse else at < place
        return jnp.where(reached, block_decay * before + everything[at], before)

    return lax.fori_loop(0, devices, step, jnp.zeros_like(own))


def body(signal, cotangent, residue, decay):
    tokens, channels = signal.shape
    modes = decay.shape[0]
    n = lax.axis_size("ctx")
    chunks = tokens // (SUB * SUB)
    direct = n <= SUB and modes % n == 0
    elements = tokens * channels
    tokens_scratch = [vmem(tokens, LANES), vmem(tokens, LANES)]
    spans = vmem(modes * SUB, LANES)
    staging = [
        pltpu.VMEM(signal.shape, signal.dtype),
        pltpu.VMEM(cotangent.shape, cotangent.dtype),
        vmem(modes, channels),
        pltpu.SemaphoreType.DMA((3,)),
    ]

    if direct:
        share = modes // n
        messages = pl.pallas_call(
            functools.partial(gather_kernel, True, n),
            out_shape=shaped(n, modes + 4 * share, channels),
            in_specs=[HBM] * 3,
            scratch_shapes=tokens_scratch + [vmem(2, modes, LANES), spans, spans, spans]
            + [vmem(modes, channels)] * 3 + [vmem(n, 4 * share, channels)] + staging,
            compiler_params=PARAMS,
            cost_estimate=cost(elements * modes * 5, modes * channels * 3, elements * 6),
            name="block_states",
        )(signal, cotangent, decay)
        arrived = lax.all_to_all(messages, "ctx", 0, 0)
    else:
        closing, opening, local_grad = pl.pallas_call(
            functools.partial(gather_kernel, False, n),
            out_shape=[shaped(modes, channels)] * 3,
            in_specs=[HBM] * 3,
            scratch_shapes=tokens_scratch + [vmem(2, modes, LANES), spans, spans, spans] + staging,
            compiler_params=PARAMS,
            cost_estimate=cost(elements * modes * 5, modes * channels * 3, elements * 6),
            name="block_states",
        )(signal, cotangent, decay)

    near_out, near_back = pl.pallas_call(
        local_kernel,
        out_shape=[shaped(chunks * SUB, SUB, channels)] * 2,
        scratch_shapes=tokens_scratch + [vmem(3, modes, LANES), spans, spans]
        + [vmem(modes, chunks - 1, SUB, LANES)] * 2 + [spans, spans],
        compiler_params=PARAMS,
        cost_estimate=cost(elements * modes * 10, modes * channels * 3, elements * 12),
        name="local_convolutions",
    )(signal, cotangent, residue, decay)

    if direct:
        part = pl.pallas_call(
            functools.partial(owner_kernel, float(tokens)),
            out_shape=shaped(share, channels),
            grid=(1,),
            in_specs=[pl.BlockSpec((n, 4 * share, channels), lambda i: (0, modes // (4 * share), 0))],
            out_specs=WHOLE,
            compiler_params=PARAMS,
            cost_estimate=cost(elements, modes * channels, modes * channels * 16),
            name="owned_modes",
        )(arrived)
        pieces = lax.all_gather(part, ("ctx", "ch"))
        residue_grad = pl.pallas_call(
            functools.partial(assemble_kernel, n),
            out_shape=shaped(modes, channels),
            compiler_params=PARAMS,
            cost_estimate=cost(modes * channels, 0, modes * channels * 8),
            name="assemble_gradient",
        )(pieces)
        sources = [arrived]
        source_specs = [pl.BlockSpec((n, modes, channels), lambda i: (0, 0, 0))]
    else:
        block_decay = jnp.exp(-decay * tokens)
        incoming = carried_in(closing, block_decay, False)
        outgoing = carried_in(opening, block_decay, True)
        summed = lax.psum(local_grad + jnp.exp(-decay) * opening * incoming, ("ctx", "ch"))
        residue_grad = summed / (tokens * n)
        sources = [incoming, outgoing]
        source_specs = [WHOLE] * 2

    conv_out, signal_grad = pl.pallas_call(
        functools.partial(finish_kernel, direct, n),
        out_shape=[jax.ShapeDtypeStruct((tokens, channels), signal.dtype)] * 2,
        grid=(1,),
        in_specs=[WHOLE] * 4 + source_specs,
        out_specs=[WHOLE] * 2,
        scratch_shapes=[vmem(tokens, LANES), vmem(5, modes, LANES)] + [vmem(modes, channels)] * 2,
        compiler_params=PARAMS,
        cost_estimate=cost(elements * modes * 4, modes * channels * 10, elements * 12),
        name="add_arrivals",
    )(residue, decay, near_out, near_back, *sources)
    return conv_out, signal_grad, residue_grad


def solution(mesh):
    return jax.shard_map(
        body,
        mesh=mesh,
        in_specs=(P("ctx", "ch"), P("ctx", "ch"), P(), P()),
        out_specs=(P("ctx", "ch"), P("ctx", "ch"), P()),
        check_vma=False,
    )
```

```python
import functools

import jax
import jax.numpy as jnp
from jax import lax
from jax.experimental import pallas as pl
from jax.experimental.pallas import tpu as pltpu
from jax.sharding import PartitionSpec as P

SUB = 8
LANES = 128
F32 = jnp.float32


def row(ref, *index):
    return jnp.broadcast_to(ref[index], (SUB, LANES))


def split_lanes(source, target, tile):
    lanes = pl.ds(pl.multiple_of(tile * LANES, LANES), LANES)
    target[...] = source[:, lanes].astype(F32)


def read_tokens(scratch, chunks):
    span = chunks * SUB
    return [[scratch[pl.ds(p * SUB + r, SUB, stride=span), :] for r in range(SUB)] for p in range(chunks)]


def powers(decay, pw):
    pw[0] = jnp.exp(-decay)
    pw[1] = jnp.exp(-decay * SUB)


def horner(terms, factor):
    total = terms[0]
    for term in terms[1:]:
        total = total * factor + term
    return total


def chunk_states(m, xs, gs, pw):
    a, a8 = row(pw, 0, pl.ds(m, 1)), row(pw, 1, pl.ds(m, 1))
    chunks = len(xs)
    held, back = [], [None] * chunks
    for p in range(chunks):
        own = horner(xs[p], a)
        held.append(own if p == 0 else held[-1] * a8 + own)
    opens = [horner(gs[p][::-1], a) for p in range(chunks)]
    for p in reversed(range(chunks)):
        back[p] = opens[p] if p == chunks - 1 else back[p + 1] * a8 + opens[p]
    return held, back, opens


def by_span(scratch, half, j):
    return scratch[pl.ds(half * SUB * SUB + j, SUB, stride=SUB), :]


def gather_kernel(x_hbm, g_hbm, decay_hbm, segment, *refs):
    xf, gf, pw, ends, starts, inner, x_ref, g_ref, decay_ref, sems = refs
    copies = [
        pltpu.make_async_copy(source, target, sems.at[i])
        for i, (source, target) in enumerate(((x_hbm, x_ref), (g_hbm, g_ref), (decay_hbm, decay_ref)))
    ]
    for copy in copies:
        copy.start()
    modes, channels = decay_ref.shape
    chunks = x_ref.shape[0] // (SUB * SUB)
    span = chunks * SUB
    closing, opening, grad = (segment.at[pl.ds(i * modes, modes)] for i in range(3))
    for copy in copies:
        copy.wait()

    def tile_step(tile, _):
        lanes = pl.ds(pl.multiple_of(tile * LANES, LANES), LANES)
        split_lanes(x_ref, xf, tile)
        split_lanes(g_ref, gf, tile)
        decay = decay_ref[:, lanes]
        powers(decay, pw)
        xs, gs = read_tokens(xf, chunks), read_tokens(gf, chunks)
        for m in range(modes):
            held, back, opens = chunk_states(m, xs, gs, pw)
            rows = pl.ds(m * SUB, SUB)
            ends[rows, :] = held[-1]
            starts[rows, :] = back[0]
            inner[rows, :] = sum(opens[p] * held[p - 1] for p in range(1, chunks))
        lagged = []
        for lag in range(SUB):
            pairs = [gs[p][r] * xs[p][r - lag] for p in range(chunks) for r in range(lag, SUB)]
            lagged.append(jnp.sum(sum(pairs), axis=0, keepdims=True))
        for half in range(modes // SUB):
            some = pl.ds(half * SUB, SUB)
            a = pw[0, some, :]
            across = jnp.exp(-decay[half * SUB:(half + 1) * SUB] * span)
            arriving = jnp.zeros((SUB, LANES), F32)
            cross = jnp.zeros((SUB, LANES), F32)
            for j in range(SUB):
                cross = cross + (by_span(inner, half, j) + by_span(starts, half, j) * arriving)
                arriving = arriving * across + by_span(ends, half, j)
            leaving = horner([by_span(starts, half, j) for j in reversed(range(SUB))], across)
            near = horner([jnp.broadcast_to(v, (SUB, LANES)) for v in reversed(lagged)], a)
            closing[some, lanes] = arriving
            opening[some, lanes] = leaving
            grad[some, lanes] = near + a * cross
        return 0

    lax.fori_loop(0, channels // LANES, tile_step, 0)


def local_kernel(tiles, x_ref, g_ref, residue_ref, decay_ref, _, out_ref, back_ref,
                 xf, gf, pw, ends, starts, before, after, arrive, leave):
    modes, channels = decay_ref.shape
    chunks = x_ref.shape[0] // (SUB * SUB)
    span = chunks * SUB

    def tile_step(tile, _):
        lanes = pl.ds(pl.multiple_of(tile * LANES, LANES), LANES)
        split_lanes(x_ref, xf, tile)
        split_lanes(g_ref, gf, tile)
        decay = decay_ref[:, lanes]
        residue = residue_ref[:, lanes]
        powers(decay, pw)
        pw[2] = residue * pw[0]
        xs, gs = read_tokens(xf, chunks), read_tokens(gf, chunks)
        for m in range(modes):
            held, back, _ = chunk_states(m, xs, gs, pw)
            rows = pl.ds(m * SUB, SUB)
            ends[rows, :] = held[-1]
            starts[rows, :] = back[0]
            for p in range(1, chunks):
                before[m, p - 1] = held[p - 1]
                after[m, p - 1] = back[p]
        for half in range(modes // SUB):
            across = jnp.exp(-decay[half * SUB:(half + 1) * SUB] * span)
            for target, source, order in ((arrive, ends, range(SUB)), (leave, starts, range(SUB - 1, -1, -1))):
                running = jnp.zeros((SUB, LANES), F32)
                for j in order:
                    target[pl.ds(half * SUB * SUB + j, SUB, stride=SUB), :] = running
                    running = running * across + by_span(source, half, j)
        taps = []
        weight = residue
        for lag in range(SUB):
            taps.append(jnp.broadcast_to(jnp.sum(weight, axis=0, keepdims=True), (SUB, LANES)))
            weight = weight * pw[0]
        for values, carried, inside, target, forward in (
            (xs, arrive, before, out_ref, True), (gs, leave, after, back_ref, False)
        ):
            order = range(SUB) if forward else range(SUB - 1, -1, -1)
            totals = []
            for p in range(chunks):
                seq = [values[p][r] for r in order]
                totals.append([sum(taps[lag] * seq[r - lag] for lag in range(r + 1)) for r in range(SUB)])
            for m in range(modes):
                a, a8, first = (row(pw, i, pl.ds(m, 1)) for i in range(3))
                edge = carried[pl.ds(m * SUB, SUB), :]
                for q in range(chunks):
                    p = q if forward else chunks - 1 - q
                    if q == 0:
                        state = edge
                    else:
                        edge = edge * a8
                        state = edge + inside[m, p - 1 if forward else p]
                    wave = state * first
                    for r in range(SUB):
                        totals[p][r] = totals[p][r] + wave
                        if r < SUB - 1:
                            wave = wave * a
            for p in range(chunks):
                for r, at in enumerate(order):
                    target[tile - tiles[0], p * SUB + at] = totals[p][r]
        return 0

    lax.fori_loop(tiles[0], tiles[1], tile_step, 0)


def join_kernel(tokens, bit, last, segment, other, decay_ref, carried, _, *outs):
    modes = decay_ref.shape[0]
    place = lax.axis_index("ctx")
    size = 1 << bit
    inside = lax.rem(place, size)
    late = lax.rem(lax.div(place, size), 2) == 1
    decay = decay_ref[...]
    parts = [slice(i * modes, (i + 1) * modes) for i in range(3)]
    mine = [segment[rows] for rows in parts]
    theirs = [other[rows] for rows in parts]
    behind = (inside * tokens).astype(F32)
    ahead = ((size - 1 - inside) * tokens).astype(F32)
    reach = jnp.exp(decay * -jnp.where(late, behind, ahead))
    first = reach * jnp.where(late, theirs[0], 0.0)
    second = reach * jnp.where(late, 0.0, theirs[1])
    if bit:
        first = first + carried[0:modes]
        second = second + carried[modes:]
    outs[0][0:modes] = first
    outs[0][modes:] = second
    early_close = jnp.where(late, theirs[0], mine[0])
    late_open = jnp.where(late, mine[1], theirs[1])
    grad = (mine[2] + theirs[2]) + jnp.exp(-decay) * late_open * early_close
    if last:
        outs[1][...] = grad
    else:
        block = jnp.exp(decay * (-1.0 * size * tokens))
        outs[1][parts[0]] = block * early_close + jnp.where(late, mine[0], theirs[0])
        outs[1][parts[1]] = jnp.where(late, theirs[1], mine[1]) + block * late_open
        outs[1][parts[2]] = grad


def finish_kernel(tiles, residue_ref, decay_ref, near_out, near_back, carried, _, *refs):
    out_ref, back_ref, result, pw, arrive, leave = refs[-6:]
    modes, channels = decay_ref.shape
    chunks = near_out.shape[1] // SUB
    span = chunks * SUB
    first = residue_ref[...] * jnp.exp(-decay_ref[...])
    arrive[...] = carried[0:modes] * first
    leave[...] = carried[modes:] * first

    def tile_step(tile, _):
        lanes = pl.ds(pl.multiple_of(tile * LANES, LANES), LANES)
        decay = decay_ref[:, lanes]
        powers(decay, pw)
        pw[2] = decay * (-1.0 * span)
        pw[3] = arrive[:, lanes]
        pw[4] = leave[:, lanes]
        level = lax.broadcasted_iota(jnp.int32, (SUB, LANES), 0).astype(F32)
        for near, target, forward in ((near_out, out_ref, True), (near_back, back_ref, False)):
            order = range(SUB) if forward else range(SUB - 1, -1, -1)
            spans = level if forward else SUB - 1.0 - level
            totals = [[near[tile - tiles[0], p * SUB + r] for r in range(SUB)] for p in range(chunks)]
            for m in range(modes):
                a, a8, rate = (row(pw, i, pl.ds(m, 1)) for i in range(3))
                state = row(pw, 3 if forward else 4, pl.ds(m, 1)) * jnp.exp(rate * spans)
                for q in range(chunks):
                    p = q if forward else chunks - 1 - q
                    wave = state
                    for r in order:
                        totals[p][r] = totals[p][r] + wave
                        wave = wave * a
                    if q < chunks - 1:
                        state = state * a8
            for p in range(chunks):
                for r in range(SUB):
                    result[pl.ds(p * SUB + r, SUB, stride=span), :] = totals[p][r]
            place = pl.ds(pl.multiple_of((tile - tiles[0]) * LANES, LANES), LANES)
            target[:, place] = result[...].astype(target.dtype)
        return 0

    lax.fori_loop(tiles[0], tiles[1], tile_step, 0)


def vmem(*shape):
    return pltpu.VMEM(shape, F32)


def shaped(*shape):
    return jax.ShapeDtypeStruct(shape, F32)


def cost(flops, transcendentals, nbytes):
    return pl.CostEstimate(flops=flops, transcendentals=transcendentals, bytes_accessed=nbytes)


PARAMS = pltpu.CompilerParams(vmem_limit_bytes=32 * 1024 * 1024)
WHOLE = pl.BlockSpec(memory_space=pltpu.VMEM)
HBM = pl.BlockSpec(memory_space=pltpu.HBM)


UNREAD = pl.BlockSpec(memory_space=pl.ANY)
PARTS = 2


def body(signal, cotangent, residue, decay):
    tokens, channels = signal.shape
    modes = decay.shape[0]
    n, groups = lax.axis_size("ctx"), lax.axis_size("ch")
    chunks = tokens // (SUB * SUB)
    elements = tokens * channels
    steps = n.bit_length() - 1
    tokens_scratch = [vmem(tokens, LANES), vmem(tokens, LANES)]
    spans = vmem(modes * SUB, LANES)
    width = channels // LANES // PARTS
    ranges = [(k * width, (k + 1) * width) for k in range(PARTS)]

    segment = pl.pallas_call(
        gather_kernel,
        out_shape=shaped(3 * modes, channels),
        in_specs=[HBM] * 3,
        scratch_shapes=tokens_scratch
        + [vmem(2, modes, LANES), spans, spans, spans]
        + [pltpu.VMEM(signal.shape, signal.dtype)] * 2
        + [vmem(modes, channels), pltpu.SemaphoreType.DMA((3,))],
        compiler_params=PARAMS,
        cost_estimate=cost(elements * modes * 5, modes * channels * 3, elements * 6),
        name="block_states",
    )(*(pltpu.with_memory_space_constraint(a, pltpu.HBM) for a in (signal, cotangent, decay)))

    def near_part(part, after):
        return pl.pallas_call(
            functools.partial(local_kernel, ranges[part]),
            out_shape=[shaped(width, chunks * SUB, SUB, LANES)] * 2,
            in_specs=[WHOLE] * 4 + [UNREAD],
            scratch_shapes=tokens_scratch
            + [vmem(3, modes, LANES), spans, spans]
            + [vmem(modes, chunks - 1, SUB, LANES)] * 2
            + [spans, spans],
            compiler_params=PARAMS,
            cost_estimate=cost(elements * modes * 400 // PARTS, 0, elements * 12 // PARTS),
            name="local_convolutions",
        )(signal, cotangent, residue, decay, after)

    near = [None] * PARTS
    carried = jnp.zeros((SUB, LANES), F32)
    pinned = segment
    for bit in range(steps):
        other = lax.ppermute(segment, "ctx", [(i, i ^ (1 << bit)) for i in range(n)])
        last = bit == steps - 1
        part = bit - (steps - PARTS)
        if part >= 0:
            near[part] = near_part(part, segment)
            pinned = near[part][0]
        carried, segment = pl.pallas_call(
            functools.partial(join_kernel, tokens, bit, last),
            out_shape=[shaped(2 * modes, channels), shaped(modes if last else 3 * modes, channels)],
            in_specs=[WHOLE] * 4 + [UNREAD],
            compiler_params=PARAMS,
            cost_estimate=cost(elements, modes * channels * 3, modes * channels * 48),
            name="join_segments",
        )(segment, other, decay, carried, pinned)

    def finish_part(part, after, done):
        spec = pl.BlockSpec((tokens, width * LANES), lambda i: (0, part))
        kept = [] if done is None else list(done)
        return pl.pallas_call(
            functools.partial(finish_kernel, ranges[part]),
            out_shape=[jax.ShapeDtypeStruct((tokens, channels), signal.dtype)] * 2,
            grid=(1,),
            in_specs=[WHOLE] * 5 + [UNREAD] + [UNREAD] * len(kept),
            out_specs=[spec] * 2,
            input_output_aliases={6 + i: i for i in range(len(kept))},
            scratch_shapes=[vmem(tokens, LANES), vmem(5, modes, LANES)] + [vmem(modes, channels)] * 2,
            compiler_params=PARAMS,
            cost_estimate=cost(elements * modes * 300 // PARTS, 0, elements * 12 // PARTS),
            name="add_arrivals",
        )(residue, decay, *near[part], carried, after, *kept)

    grad = segment
    results = None
    part = 0
    shift = 1
    while shift < groups:
        other = lax.ppermute(grad, "ch", [(i, i ^ shift) for i in range(groups)])
        if part < PARTS:
            results = finish_part(part, grad, results)
            part += 1
        grad = grad + other
        shift *= 2
    while part < PARTS:
        results = finish_part(part, grad, results)
        part += 1
    return results[0], results[1], grad / (tokens * n)


def solution(mesh):
    return jax.shard_map(
        body,
        mesh=mesh,
        in_specs=(P("ctx", "ch"), P("ctx", "ch"), P(), P()),
        out_specs=(P("ctx", "ch"), P("ctx", "ch"), P()),
        check_vma=False,
    )
```

```python
import functools

import jax
import jax.numpy as jnp
from jax import lax
from jax.experimental import pallas as pl
from jax.experimental.pallas import tpu as pltpu
from jax.sharding import PartitionSpec as P

SUB = 8
LANES = 128
F32 = jnp.float32


def row(ref, *index):
    return jnp.broadcast_to(ref[index], (SUB, LANES))


def split_lanes(source, target, tile):
    lanes = pl.ds(pl.multiple_of(tile * LANES, LANES), LANES)
    target[...] = source[:, lanes].astype(F32)


def read_tokens(scratch, chunks):
    span = chunks * SUB
    return [[scratch[pl.ds(p * SUB + r, SUB, stride=span), :] for r in range(SUB)] for p in range(chunks)]


def powers(decay, pw):
    pw[0] = jnp.exp(-decay)
    pw[1] = jnp.exp(-decay * SUB)


def horner(terms, factor):
    total = terms[0]
    for term in terms[1:]:
        total = total * factor + term
    return total


def chunk_states(m, xs, gs, pw):
    a, a8 = row(pw, 0, pl.ds(m, 1)), row(pw, 1, pl.ds(m, 1))
    chunks = len(xs)
    held, back = [], [None] * chunks
    for p in range(chunks):
        own = horner(xs[p], a)
        held.append(own if p == 0 else held[-1] * a8 + own)
    opens = [horner(gs[p][::-1], a) for p in range(chunks)]
    for p in reversed(range(chunks)):
        back[p] = opens[p] if p == chunks - 1 else back[p + 1] * a8 + opens[p]
    return held, back, opens


def by_span(scratch, half, j):
    return scratch[pl.ds(half * SUB * SUB + j, SUB, stride=SUB), :]


def gather_kernel(x_hbm, g_hbm, decay_hbm, segment, *refs):
    xf, gf, pw, ends, starts, inner, x_ref, g_ref, decay_ref, sems = refs
    copies = [
        pltpu.make_async_copy(source, target, sems.at[i])
        for i, (source, target) in enumerate(((x_hbm, x_ref), (g_hbm, g_ref), (decay_hbm, decay_ref)))
    ]
    for copy in copies:
        copy.start()
    modes, channels = decay_ref.shape
    chunks = x_ref.shape[0] // (SUB * SUB)
    span = chunks * SUB
    closing, opening, grad = (segment.at[pl.ds(i * modes, modes)] for i in range(3))
    for copy in copies:
        copy.wait()

    def tile_step(tile, _):
        lanes = pl.ds(pl.multiple_of(tile * LANES, LANES), LANES)
        split_lanes(x_ref, xf, tile)
        split_lanes(g_ref, gf, tile)
        decay = decay_ref[:, lanes]
        powers(decay, pw)
        xs, gs = read_tokens(xf, chunks), read_tokens(gf, chunks)
        for m in range(modes):
            held, back, opens = chunk_states(m, xs, gs, pw)
            rows = pl.ds(m * SUB, SUB)
            ends[rows, :] = held[-1]
            starts[rows, :] = back[0]
            inner[rows, :] = sum(opens[p] * held[p - 1] for p in range(1, chunks))
        lagged = []
        for lag in range(SUB):
            pairs = [gs[p][r] * xs[p][r - lag] for p in range(chunks) for r in range(lag, SUB)]
            lagged.append(jnp.sum(sum(pairs), axis=0, keepdims=True))
        for half in range(modes // SUB):
            some = pl.ds(half * SUB, SUB)
            a = pw[0, some, :]
            across = jnp.exp(-decay[half * SUB:(half + 1) * SUB] * span)
            arriving = jnp.zeros((SUB, LANES), F32)
            cross = jnp.zeros((SUB, LANES), F32)
            for j in range(SUB):
                cross = cross + (by_span(inner, half, j) + by_span(starts, half, j) * arriving)
                arriving = arriving * across + by_span(ends, half, j)
            leaving = horner([by_span(starts, half, j) for j in reversed(range(SUB))], across)
            near = horner([jnp.broadcast_to(v, (SUB, LANES)) for v in reversed(lagged)], a)
            closing[some, lanes] = arriving
            opening[some, lanes] = leaving
            grad[some, lanes] = near + a * cross
        return 0

    lax.fori_loop(0, channels // LANES, tile_step, 0)


def local_kernel(tiles, x_ref, g_ref, residue_ref, decay_ref, _, out_ref, back_ref,
                 xf, gf, pw, ends, starts, before, after, arrive, leave):
    modes, channels = decay_ref.shape
    chunks = x_ref.shape[0] // (SUB * SUB)
    span = chunks * SUB

    def tile_step(tile, _):
        lanes = pl.ds(pl.multiple_of(tile * LANES, LANES), LANES)
        split_lanes(x_ref, xf, tile)
        split_lanes(g_ref, gf, tile)
        decay = decay_ref[:, lanes]
        residue = residue_ref[:, lanes]
        powers(decay, pw)
        pw[2] = residue * pw[0]
        xs, gs = read_tokens(xf, chunks), read_tokens(gf, chunks)
        for m in range(modes):
            held, back, _ = chunk_states(m, xs, gs, pw)
            rows = pl.ds(m * SUB, SUB)
            ends[rows, :] = held[-1]
            starts[rows, :] = back[0]
            for p in range(1, chunks):
                before[m, p - 1] = held[p - 1]
                after[m, p - 1] = back[p]
        for half in range(modes // SUB):
            across = jnp.exp(-decay[half * SUB:(half + 1) * SUB] * span)
            for target, source, order in ((arrive, ends, range(SUB)), (leave, starts, range(SUB - 1, -1, -1))):
                running = jnp.zeros((SUB, LANES), F32)
                for j in order:
                    target[pl.ds(half * SUB * SUB + j, SUB, stride=SUB), :] = running
                    running = running * across + by_span(source, half, j)
        taps = []
        weight = residue
        for lag in range(SUB):
            taps.append(jnp.broadcast_to(jnp.sum(weight, axis=0, keepdims=True), (SUB, LANES)))
            weight = weight * pw[0]
        for values, carried, inside, target, forward in (
            (xs, arrive, before, out_ref, True), (gs, leave, after, back_ref, False)
        ):
            order = range(SUB) if forward else range(SUB - 1, -1, -1)
            totals = []
            for p in range(chunks):
                seq = [values[p][r] for r in order]
                totals.append([sum(taps[lag] * seq[r - lag] for lag in range(r + 1)) for r in range(SUB)])
            for m in range(modes):
                a, a8, first = (row(pw, i, pl.ds(m, 1)) for i in range(3))
                edge = carried[pl.ds(m * SUB, SUB), :]
                for q in range(chunks):
                    p = q if forward else chunks - 1 - q
                    if q == 0:
                        state = edge
                    else:
                        edge = edge * a8
                        state = edge + inside[m, p - 1 if forward else p]
                    wave = state * first
                    for r in range(SUB):
                        totals[p][r] = totals[p][r] + wave
                        if r < SUB - 1:
                            wave = wave * a
            for p in range(chunks):
                for r, at in enumerate(order):
                    target[tile - tiles[0], p * SUB + at] = totals[p][r]
        return 0

    lax.fori_loop(tiles[0], tiles[1], tile_step, 0)


def join_kernel(tokens, bit, last, segment, other, decay_ref, carried, _, arrivals, joined, *message):
    modes = decay_ref.shape[0]
    place = lax.axis_index("ctx")
    size = 1 << bit
    late = lax.rem(lax.div(place, size), 2) == 1
    decay = decay_ref[...]
    parts = [slice(i * modes, (i + 1) * modes) for i in range(3)]
    compact = other.shape[0] == 2 * modes
    close, begin, grad = (segment[rows] for rows in parts)
    their_close = other[parts[0]]
    their_begin = other[parts[0 if compact else 1]]
    their_grad = other[parts[1 if compact else 2]]
    first = jnp.where(late, their_close, 0.0)
    second = jnp.where(late, 0.0, their_begin)
    if bit:
        inside = lax.rem(place, size)
        inside = inside - lax.rem(inside, 2)
        between = (jnp.where(late, inside, size - 2 - inside) * tokens).astype(F32)
        reach = jnp.exp(decay * -between)
        first, second = reach * first, reach * second
    if bit > 1:
        first = first + carried[0:modes]
        second = second + carried[modes:]
    arrivals[0:modes] = first
    arrivals[modes:] = second
    early_close = jnp.where(late, their_close, close)
    late_begin = jnp.where(late, begin, their_begin)
    grad = (grad + their_grad) + jnp.exp(-decay) * late_begin * early_close
    if last:
        joined[...] = grad
        return
    block = jnp.exp(decay * (-1.0 * size * tokens))
    close = block * early_close + jnp.where(late, close, their_close)
    begin = jnp.where(late, their_begin, begin) + block * late_begin
    joined[parts[0]] = close
    joined[parts[1]] = begin
    joined[parts[2]] = grad
    if message:
        next_late = lax.rem(lax.div(place, 2 * size), 2) == 1
        message[0][0:modes] = jnp.where(next_late, begin, close)
        message[0][modes:] = grad


def finish_kernel(ranges, residue_ref, decay_ref, core, chip, received, *refs):
    near = refs[:2 * len(ranges)]
    out_hbm, back_hbm, out_ref, back_ref, result, pw, arrive, leave, sems = refs[2 * len(ranges):]
    modes, channels = decay_ref.shape
    chunks = near[0].shape[1] // SUB
    span = chunks * SUB
    late = lax.rem(lax.axis_index("ctx"), 2) == 1
    decay = decay_ref[...]
    first = residue_ref[...] * jnp.exp(-decay)
    block = jnp.exp(decay * (-1.0 * span * SUB))
    incoming = jnp.where(late, chip[0:modes], received[0:modes])
    outgoing = jnp.where(late, chip[modes:], received[modes:])
    arrive[...] = (core[0:modes] + jnp.where(late, block, 1.0) * incoming) * first
    leave[...] = (core[modes:] + jnp.where(late, 1.0, block) * outgoing) * first

    def copy_out(tile, which):
        lanes = pl.ds(pl.multiple_of(tile * LANES, LANES), LANES)
        source, target = ((out_ref, out_hbm), (back_ref, back_hbm))[which]
        return pltpu.make_async_copy(source.at[:, lanes], target.at[:, lanes], sems.at[which, tile])

    def run(tiles, near_out, near_back):
        def tile_step(tile, _):
            lanes = pl.ds(pl.multiple_of(tile * LANES, LANES), LANES)
            decay = decay_ref[:, lanes]
            powers(decay, pw)
            pw[2] = decay * (-1.0 * span)
            pw[3] = arrive[:, lanes]
            pw[4] = leave[:, lanes]
            level = lax.broadcasted_iota(jnp.int32, (SUB, LANES), 0).astype(F32)
            for near, target, forward in ((near_out, out_ref, True), (near_back, back_ref, False)):
                order = range(SUB) if forward else range(SUB - 1, -1, -1)
                spans = level if forward else SUB - 1.0 - level
                totals = [[near[tile - tiles[0], p * SUB + r] for r in range(SUB)] for p in range(chunks)]
                for m in range(modes):
                    a, a8, rate = (row(pw, i, pl.ds(m, 1)) for i in range(3))
                    state = row(pw, 3 if forward else 4, pl.ds(m, 1)) * jnp.exp(rate * spans)
                    for q in range(chunks):
                        p = q if forward else chunks - 1 - q
                        wave = state
                        for r in order:
                            totals[p][r] = totals[p][r] + wave
                            wave = wave * a
                        if q < chunks - 1:
                            state = state * a8
                for p in range(chunks):
                    for r in range(SUB):
                        result[pl.ds(p * SUB + r, SUB, stride=span), :] = totals[p][r]
                target[:, lanes] = result[...].astype(target.dtype)
                copy_out(tile, 0 if forward else 1).start()
            return 0

        lax.fori_loop(tiles[0], tiles[1], tile_step, 0)

    for part, tiles in enumerate(ranges):
        run(tiles, near[2 * part], near[2 * part + 1])
    for tile in range(channels // LANES):
        for which in range(2):
            copy_out(tile, which).wait()


def vmem(*shape):
    return pltpu.VMEM(shape, F32)


def shaped(*shape):
    return jax.ShapeDtypeStruct(shape, F32)


def cost(flops, transcendentals, nbytes):
    return pl.CostEstimate(flops=flops, transcendentals=transcendentals, bytes_accessed=nbytes)


PARAMS = pltpu.CompilerParams(vmem_limit_bytes=32 * 1024 * 1024)
WHOLE = pl.BlockSpec(memory_space=pltpu.VMEM)
HBM = pl.BlockSpec(memory_space=pltpu.HBM)


UNREAD = pl.BlockSpec(memory_space=pl.ANY)
PARTS = 2


def body(signal, cotangent, residue, decay):
    tokens, channels = signal.shape
    modes = decay.shape[0]
    n, groups = lax.axis_size("ctx"), lax.axis_size("ch")
    chunks = tokens // (SUB * SUB)
    elements = tokens * channels
    steps = n.bit_length() - 1
    tokens_scratch = [vmem(tokens, LANES), vmem(tokens, LANES)]
    spans = vmem(modes * SUB, LANES)
    width = channels // LANES // PARTS
    ranges = [(k * width, (k + 1) * width) for k in range(PARTS)]

    segment = pl.pallas_call(
        gather_kernel,
        out_shape=shaped(3 * modes, channels),
        in_specs=[HBM] * 3,
        scratch_shapes=tokens_scratch
        + [vmem(2, modes, LANES), spans, spans, spans]
        + [pltpu.VMEM(signal.shape, signal.dtype)] * 2
        + [vmem(modes, channels), pltpu.SemaphoreType.DMA((3,))],
        compiler_params=PARAMS,
        cost_estimate=cost(elements * modes * 5, modes * channels * 3, elements * 6),
        name="block_states",
    )(*(pltpu.with_memory_space_constraint(a, pltpu.HBM) for a in (signal, cotangent, decay)))

    def near_part(part, after):
        return pl.pallas_call(
            functools.partial(local_kernel, ranges[part]),
            out_shape=[shaped(width, chunks * SUB, SUB, LANES)] * 2,
            in_specs=[WHOLE] * 4 + [UNREAD],
            scratch_shapes=tokens_scratch
            + [vmem(3, modes, LANES), spans, spans]
            + [vmem(modes, chunks - 1, SUB, LANES)] * 2
            + [spans, spans],
            compiler_params=PARAMS,
            cost_estimate=cost(elements * modes * 400 // PARTS, 0, elements * 12 // PARTS),
            name="local_convolutions",
        )(signal, cotangent, residue, decay, after)

    def pairs(shift):
        return [(i, i ^ shift) for i in range(n) if shift == 1 or i % 2]

    to_first = [(i, i - 1) for i in range(n) if i % 2]

    near = []
    carried = jnp.zeros((SUB, LANES), F32)
    pinned = message = segment
    for bit in range(steps):
        other = lax.ppermute(message, "ctx", pairs(1 << bit))
        last = bit == steps - 1
        if bit >= steps - PARTS:
            near += near_part(len(near) // 2, segment)
            pinned = near[-1]
        rows = [2 * modes, modes if last else 3 * modes] + ([2 * modes] if bit == steps - 2 else [])
        arrivals, segment, *message = pl.pallas_call(
            functools.partial(join_kernel, tokens, bit, last),
            out_shape=[shaped(r, channels) for r in rows],
            in_specs=[WHOLE] * 4 + [UNREAD],
            compiler_params=PARAMS,
            cost_estimate=cost(elements, modes * channels * 3, modes * channels * 48),
            name="join_segments",
        )(segment, other, decay, carried, pinned)
        message = message[0] if message else segment
        if bit == 0:
            from_core = arrivals
        else:
            carried = arrivals

    grad = segment
    received = lax.ppermute(carried, "ctx", to_first)
    stride = 1
    while stride < groups:
        count = min(4, groups // stride)
        terms = [grad] + [
            lax.ppermute(
                grad,
                ("ctx", "ch"),
                [(i * groups + k, i * groups + (k ^ (stride * m))) for i in range(n) if i % 2 for k in range(groups)],
            )
            for m in range(1, count)
        ]
        while len(terms) > 1:
            terms = [a + b for a, b in zip(terms[::2], terms[1::2])]
        grad = terms[0]
        stride *= count
    other = lax.ppermute(grad, "ctx", to_first)
    second = lax.rem(lax.axis_index("ctx"), 2) == 1
    residue_grad = jnp.where(second, grad, other) / (tokens * n)

    conv_out, signal_grad = pl.pallas_call(
        functools.partial(finish_kernel, ranges),
        out_shape=[jax.ShapeDtypeStruct((tokens, channels), signal.dtype)] * 2,
        in_specs=[WHOLE] * (5 + 2 * PARTS),
        out_specs=[HBM] * 2,
        scratch_shapes=[pltpu.VMEM((tokens, channels), signal.dtype)] * 2
        + [vmem(tokens, LANES), vmem(5, modes, LANES)]
        + [vmem(modes, channels)] * 2
        + [pltpu.SemaphoreType.DMA((2, channels // LANES))],
        compiler_params=PARAMS,
        cost_estimate=cost(elements * modes * 600, 0, elements * 12),
        name="add_arrivals",
    )(residue, decay, from_core, carried, received, *near)
    return conv_out, signal_grad, residue_grad


def solution(mesh):
    return jax.shard_map(
        body,
        mesh=mesh,
        in_specs=(P("ctx", "ch"), P("ctx", "ch"), P(), P()),
        out_specs=(P("ctx", "ch"), P("ctx", "ch"), P()),
        check_vma=False,
    )
```

```python
import functools

import jax
import jax.numpy as jnp
from jax import lax
from jax.experimental import pallas as pl
from jax.experimental.pallas import tpu as pltpu
from jax.sharding import PartitionSpec as P

SUB = 8
LANES = 128
F32 = jnp.float32


def row(ref, *index):
    return jnp.broadcast_to(ref[index], (SUB, LANES))


def split_lanes(source, target, tile):
    lanes = pl.ds(pl.multiple_of(tile * LANES, LANES), LANES)
    target[...] = source[:, lanes].astype(F32)


def read_tokens(scratch, chunks):
    span = chunks * SUB
    return [[scratch[pl.ds(p * SUB + r, SUB, stride=span), :] for r in range(SUB)] for p in range(chunks)]


def powers(decay, pw):
    pw[0] = jnp.exp(-decay)
    pw[1] = jnp.exp(-decay * SUB)


def horner(terms, factor):
    total = terms[0]
    for term in terms[1:]:
        total = total * factor + term
    return total


def chunk_states(m, xs, gs, pw):
    a, a8 = row(pw, 0, pl.ds(m, 1)), row(pw, 1, pl.ds(m, 1))
    chunks = len(xs)
    held, back = [], [None] * chunks
    for p in range(chunks):
        own = horner(xs[p], a)
        held.append(own if p == 0 else held[-1] * a8 + own)
    opens = [horner(gs[p][::-1], a) for p in range(chunks)]
    for p in reversed(range(chunks)):
        back[p] = opens[p] if p == chunks - 1 else back[p + 1] * a8 + opens[p]
    return held, back, opens


def by_span(scratch, half, j):
    return scratch[pl.ds(half * SUB * SUB + j, SUB, stride=SUB), :]


def gather_kernel(x_hbm, g_hbm, decay_hbm, segment, *refs):
    xf, gf, pw, ends, starts, inner, x_ref, g_ref, decay_ref, sems = refs
    copies = [
        pltpu.make_async_copy(source, target, sems.at[i])
        for i, (source, target) in enumerate(((x_hbm, x_ref), (g_hbm, g_ref), (decay_hbm, decay_ref)))
    ]
    for copy in copies:
        copy.start()
    modes, channels = decay_ref.shape
    chunks = x_ref.shape[0] // (SUB * SUB)
    span = chunks * SUB
    closing, opening, grad = (segment.at[pl.ds(i * modes, modes)] for i in range(3))
    for copy in copies:
        copy.wait()

    def tile_step(tile, _):
        lanes = pl.ds(pl.multiple_of(tile * LANES, LANES), LANES)
        split_lanes(x_ref, xf, tile)
        split_lanes(g_ref, gf, tile)
        decay = decay_ref[:, lanes]
        powers(decay, pw)
        xs, gs = read_tokens(xf, chunks), read_tokens(gf, chunks)
        for m in range(modes):
            held, back, opens = chunk_states(m, xs, gs, pw)
            rows = pl.ds(m * SUB, SUB)
            ends[rows, :] = held[-1]
            starts[rows, :] = back[0]
            inner[rows, :] = sum(opens[p] * held[p - 1] for p in range(1, chunks))
        lagged = []
        for lag in range(SUB):
            pairs = [gs[p][r] * xs[p][r - lag] for p in range(chunks) for r in range(lag, SUB)]
            lagged.append(jnp.sum(sum(pairs), axis=0, keepdims=True))
        for half in range(modes // SUB):
            some = pl.ds(half * SUB, SUB)
            a = pw[0, some, :]
            across = jnp.exp(-decay[half * SUB:(half + 1) * SUB] * span)
            arriving = jnp.zeros((SUB, LANES), F32)
            cross = jnp.zeros((SUB, LANES), F32)
            for j in range(SUB):
                cross = cross + (by_span(inner, half, j) + by_span(starts, half, j) * arriving)
                arriving = arriving * across + by_span(ends, half, j)
            leaving = horner([by_span(starts, half, j) for j in reversed(range(SUB))], across)
            near = horner([jnp.broadcast_to(v, (SUB, LANES)) for v in reversed(lagged)], a)
            closing[some, lanes] = arriving
            opening[some, lanes] = leaving
            grad[some, lanes] = near + a * cross
        return 0

    lax.fori_loop(0, channels // LANES, tile_step, 0)


def local_kernel(tiles, x_ref, g_ref, residue_ref, decay_ref, _, out_ref, back_ref,
                 xf, gf, pw, ends, starts, before, after, arrive, leave):
    modes, channels = decay_ref.shape
    chunks = x_ref.shape[0] // (SUB * SUB)
    span = chunks * SUB

    def tile_step(tile, _):
        lanes = pl.ds(pl.multiple_of(tile * LANES, LANES), LANES)
        split_lanes(x_ref, xf, tile)
        split_lanes(g_ref, gf, tile)
        decay = decay_ref[:, lanes]
        residue = residue_ref[:, lanes]
        powers(decay, pw)
        pw[2] = residue * pw[0]
        xs, gs = read_tokens(xf, chunks), read_tokens(gf, chunks)
        for m in range(modes):
            held, back, _ = chunk_states(m, xs, gs, pw)
            rows = pl.ds(m * SUB, SUB)
            ends[rows, :] = held[-1]
            starts[rows, :] = back[0]
            for p in range(1, chunks):
                before[m, p - 1] = held[p - 1]
                after[m, p - 1] = back[p]
        for half in range(modes // SUB):
            across = jnp.exp(-decay[half * SUB:(half + 1) * SUB] * span)
            for target, source, order in ((arrive, ends, range(SUB)), (leave, starts, range(SUB - 1, -1, -1))):
                running = jnp.zeros((SUB, LANES), F32)
                for j in order:
                    target[pl.ds(half * SUB * SUB + j, SUB, stride=SUB), :] = running
                    running = running * across + by_span(source, half, j)
        taps = []
        weight = residue
        for lag in range(SUB):
            taps.append(jnp.broadcast_to(jnp.sum(weight, axis=0, keepdims=True), (SUB, LANES)))
            weight = weight * pw[0]
        for values, carried, inside, target, forward in (
            (xs, arrive, before, out_ref, True), (gs, leave, after, back_ref, False)
        ):
            order = range(SUB) if forward else range(SUB - 1, -1, -1)
            totals = []
            for p in range(chunks):
                seq = [values[p][r] for r in order]
                totals.append([sum(taps[lag] * seq[r - lag] for lag in range(r + 1)) for r in range(SUB)])
            for m in range(modes):
                a, a8, first = (row(pw, i, pl.ds(m, 1)) for i in range(3))
                edge = carried[pl.ds(m * SUB, SUB), :]
                for q in range(chunks):
                    p = q if forward else chunks - 1 - q
                    if q == 0:
                        state = edge
                    else:
                        edge = edge * a8
                        state = edge + inside[m, p - 1 if forward else p]
                    wave = state * first
                    for r in range(SUB):
                        totals[p][r] = totals[p][r] + wave
                        if r < SUB - 1:
                            wave = wave * a
            for p in range(chunks):
                for r, at in enumerate(order):
                    target[tile - tiles[0], p * SUB + at] = totals[p][r]
        return 0

    lax.fori_loop(tiles[0], tiles[1], tile_step, 0)


def join_kernel(tokens, bit, last, segment, other, decay_ref, carried, _, arrivals, joined, *message):
    modes = decay_ref.shape[0]
    place = lax.axis_index("ctx")
    size = 1 << bit
    late = lax.rem(lax.div(place, size), 2) == 1
    decay = decay_ref[...]
    parts = [slice(i * modes, (i + 1) * modes) for i in range(3)]
    compact = other.shape[0] == 2 * modes
    close, begin, grad = (segment[rows] for rows in parts)
    their_close = other[parts[0]]
    their_begin = other[parts[0 if compact else 1]]
    their_grad = other[parts[1 if compact else 2]]
    first = jnp.where(late, their_close, 0.0)
    second = jnp.where(late, 0.0, their_begin)
    if bit:
        inside = lax.rem(place, size)
        inside = inside - lax.rem(inside, 2)
        between = (jnp.where(late, inside, size - 2 - inside) * tokens).astype(F32)
        reach = jnp.exp(decay * -between)
        first, second = reach * first, reach * second
    if bit > 1:
        first = first + carried[0:modes]
        second = second + carried[modes:]
    arrivals[0:modes] = first
    arrivals[modes:] = second
    early_close = jnp.where(late, their_close, close)
    late_begin = jnp.where(late, begin, their_begin)
    grad = (grad + their_grad) + jnp.exp(-decay) * late_begin * early_close
    if last:
        joined[...] = grad
        return
    block = jnp.exp(decay * (-1.0 * size * tokens))
    close = block * early_close + jnp.where(late, close, their_close)
    begin = jnp.where(late, their_begin, begin) + block * late_begin
    joined[parts[0]] = close
    joined[parts[1]] = begin
    joined[parts[2]] = grad
    if message:
        next_late = lax.rem(lax.div(place, 2 * size), 2) == 1
        message[0][0:modes] = jnp.where(next_late, begin, close)
        message[0][modes:] = grad


def finish_kernel(ranges, residue_ref, decay_ref, core, chip, received, *refs):
    near = refs[:2 * len(ranges)]
    out_hbm, back_hbm, finished, out_ref, back_ref, result, pw, arrive, leave, sems = refs[2 * len(ranges):]
    modes, channels = decay_ref.shape
    chunks = near[0].shape[1] // SUB
    span = chunks * SUB
    late = lax.rem(lax.axis_index("ctx"), 2) == 1
    decay = decay_ref[...]
    first = residue_ref[...] * jnp.exp(-decay)
    block = jnp.exp(decay * (-1.0 * span * SUB))
    incoming = jnp.where(late, chip[0:modes], received[0:modes])
    outgoing = jnp.where(late, chip[modes:], received[modes:])
    arrive[...] = (core[0:modes] + jnp.where(late, block, 1.0) * incoming) * first
    leave[...] = (core[modes:] + jnp.where(late, 1.0, block) * outgoing) * first

    def copy_out(tile, which):
        lanes = pl.ds(pl.multiple_of(tile * LANES, LANES), LANES)
        source, target = ((out_ref, out_hbm), (back_ref, back_hbm))[which]
        return pltpu.make_async_copy(source.at[:, lanes], target.at[:, lanes], sems.at[which, tile])

    def run(tiles, near_out, near_back):
        def tile_step(tile, _):
            lanes = pl.ds(pl.multiple_of(tile * LANES, LANES), LANES)
            decay = decay_ref[:, lanes]
            powers(decay, pw)
            pw[2] = decay * (-1.0 * span)
            pw[3] = arrive[:, lanes]
            pw[4] = leave[:, lanes]
            level = lax.broadcasted_iota(jnp.int32, (SUB, LANES), 0).astype(F32)
            for near, target, forward in ((near_out, out_ref, True), (near_back, back_ref, False)):
                order = range(SUB) if forward else range(SUB - 1, -1, -1)
                spans = level if forward else SUB - 1.0 - level
                totals = [[near[tile - tiles[0], p * SUB + r] for r in range(SUB)] for p in range(chunks)]
                for m in range(modes):
                    a, a8, rate = (row(pw, i, pl.ds(m, 1)) for i in range(3))
                    state = row(pw, 3 if forward else 4, pl.ds(m, 1)) * jnp.exp(rate * spans)
                    for q in range(chunks):
                        p = q if forward else chunks - 1 - q
                        wave = state
                        for r in order:
                            totals[p][r] = totals[p][r] + wave
                            wave = wave * a
                        if q < chunks - 1:
                            state = state * a8
                for p in range(chunks):
                    for r in range(SUB):
                        result[pl.ds(p * SUB + r, SUB, stride=span), :] = totals[p][r]
                target[:, lanes] = result[...].astype(target.dtype)
                copy_out(tile, 0 if forward else 1).start()
            return 0

        lax.fori_loop(tiles[0], tiles[1], tile_step, 0)

    for part, tiles in enumerate(ranges):
        run(tiles, near[2 * part], near[2 * part + 1])
    for tile in range(channels // LANES):
        for which in range(2):
            copy_out(tile, which).wait()
    finished[...] = jnp.zeros(finished.shape, F32)


def vmem(*shape):
    return pltpu.VMEM(shape, F32)


def shaped(*shape):
    return jax.ShapeDtypeStruct(shape, F32)


def cost(flops, transcendentals, nbytes):
    return pl.CostEstimate(flops=flops, transcendentals=transcendentals, bytes_accessed=nbytes)


PARAMS = pltpu.CompilerParams(vmem_limit_bytes=32 * 1024 * 1024)
WHOLE = pl.BlockSpec(memory_space=pltpu.VMEM)
HBM = pl.BlockSpec(memory_space=pltpu.HBM)


UNREAD = pl.BlockSpec(memory_space=pl.ANY)
PARTS = 2


def body(signal, cotangent, residue, decay):
    tokens, channels = signal.shape
    modes = decay.shape[0]
    n, groups = lax.axis_size("ctx"), lax.axis_size("ch")
    chunks = tokens // (SUB * SUB)
    elements = tokens * channels
    steps = n.bit_length() - 1
    tokens_scratch = [vmem(tokens, LANES), vmem(tokens, LANES)]
    spans = vmem(modes * SUB, LANES)
    width = channels // LANES // PARTS
    ranges = [(k * width, (k + 1) * width) for k in range(PARTS)]

    segment = pl.pallas_call(
        gather_kernel,
        out_shape=shaped(3 * modes, channels),
        in_specs=[HBM] * 3,
        scratch_shapes=tokens_scratch
        + [vmem(2, modes, LANES), spans, spans, spans]
        + [pltpu.VMEM(signal.shape, signal.dtype)] * 2
        + [vmem(modes, channels), pltpu.SemaphoreType.DMA((3,))],
        compiler_params=PARAMS,
        cost_estimate=cost(elements * modes * 5, modes * channels * 3, elements * 6),
        name="block_states",
    )(*(pltpu.with_memory_space_constraint(a, pltpu.HBM) for a in (signal, cotangent, decay)))

    def near_part(part, after):
        return pl.pallas_call(
            functools.partial(local_kernel, ranges[part]),
            out_shape=[shaped(width, chunks * SUB, SUB, LANES)] * 2,
            in_specs=[WHOLE] * 4 + [UNREAD],
            scratch_shapes=tokens_scratch
            + [vmem(3, modes, LANES), spans, spans]
            + [vmem(modes, chunks - 1, SUB, LANES)] * 2
            + [spans, spans],
            compiler_params=PARAMS,
            cost_estimate=cost(elements * modes * 400 // PARTS, 0, elements * 12 // PARTS),
            name="local_convolutions",
        )(signal, cotangent, residue, decay, after)

    def pairs(shift):
        return [(i, i ^ shift if shift == 1 or i % 2 else i) for i in range(n)]

    near = []
    carried = jnp.zeros((SUB, LANES), F32)
    pinned = message = segment
    for bit in range(steps):
        other = lax.ppermute(message, "ctx", pairs(1 << bit))
        last = bit == steps - 1
        if bit >= steps - PARTS:
            near += near_part(len(near) // 2, segment)
            pinned = near[-1]
        rows = [2 * modes, modes if last else 3 * modes] + ([2 * modes] if bit == steps - 2 else [])
        arrivals, segment, *message = pl.pallas_call(
            functools.partial(join_kernel, tokens, bit, last),
            out_shape=[shaped(r, channels) for r in rows],
            in_specs=[WHOLE] * 4 + [UNREAD],
            compiler_params=PARAMS,
            cost_estimate=cost(elements, modes * channels * 3, modes * channels * 48),
            name="join_segments",
        )(segment, other, decay, carried, pinned)
        message = message[0] if message else segment
        if bit == 0:
            from_core = arrivals
        else:
            carried = arrivals

    received = lax.ppermute(carried, "ctx", pairs(1))

    def summed(*terms):
        while len(terms) > 1:
            terms = [a + b for a, b in zip(terms[::2], terms[1::2])]
        return terms[0]

    def sum_kernel(*refs):
        refs[-1][...] = summed(*(ref[...] for ref in refs[:-2]))

    conv_out, signal_grad, finished = pl.pallas_call(
        functools.partial(finish_kernel, ranges),
        out_shape=[jax.ShapeDtypeStruct((tokens, channels), signal.dtype)] * 2 + [shaped(SUB, LANES)],
        in_specs=[WHOLE] * (5 + 2 * PARTS),
        out_specs=[HBM] * 2 + [WHOLE],
        scratch_shapes=[pltpu.VMEM((tokens, channels), signal.dtype)] * 2
        + [vmem(tokens, LANES), vmem(5, modes, LANES)]
        + [vmem(modes, channels)] * 2
        + [pltpu.SemaphoreType.DMA((2, channels // LANES))],
        compiler_params=PARAMS,
        cost_estimate=cost(elements * modes * 600, 0, elements * 12),
        name="add_arrivals",
    )(residue, decay, from_core, carried, received, *near)

    grad = segment
    stride = 1
    while stride < groups:
        count = min(4, groups // stride)
        terms = [grad] + [
            lax.ppermute(
                grad,
                ("ctx", "ch"),
                [(i * groups + k, i * groups + (k ^ (stride * m if i % 2 else 0))) for i in range(n) for k in range(groups)],
            )
            for m in range(1, count)
        ]
        grad = pl.pallas_call(
            sum_kernel,
            out_shape=shaped(modes, channels),
            in_specs=[WHOLE] * count + [UNREAD],
            compiler_params=PARAMS,
            cost_estimate=cost(modes * channels * count, 0, modes * channels * 4 * count),
            name="sum_groups",
        )(*terms, finished)
        stride *= count
    other = lax.ppermute(grad, "ctx", pairs(1))
    second = lax.rem(lax.axis_index("ctx"), 2) == 1
    residue_grad = jnp.where(second, grad, other) / (tokens * n)
    return conv_out, signal_grad, residue_grad


def solution(mesh):
    return jax.shard_map(
        body,
        mesh=mesh,
        in_specs=(P("ctx", "ch"), P("ctx", "ch"), P(), P()),
        out_specs=(P("ctx", "ch"), P("ctx", "ch"), P()),
        check_vma=False,
    )
```

```python
import functools

import jax
import jax.numpy as jnp
from jax import lax
from jax.experimental import pallas as pl
from jax.experimental.pallas import tpu as pltpu
from jax.sharding import PartitionSpec as P

SUB = 8
LANES = 128
F32 = jnp.float32


def row(ref, *index):
    return jnp.broadcast_to(ref[index], (SUB, LANES))


def split_lanes(source, target, tile):
    lanes = pl.ds(pl.multiple_of(tile * LANES, LANES), LANES)
    target[...] = source[:, lanes].astype(F32)


def read_tokens(scratch, chunks):
    span = chunks * SUB
    return [[scratch[pl.ds(p * SUB + r, SUB, stride=span), :] for r in range(SUB)] for p in range(chunks)]


def powers(decay, pw):
    pw[0] = jnp.exp(-decay)
    pw[1] = jnp.exp(-decay * SUB)


def horner(terms, factor):
    total = terms[0]
    for term in terms[1:]:
        total = total * factor + term
    return total


def chunk_states(m, xs, gs, pw):
    a, a8 = row(pw, 0, pl.ds(m, 1)), row(pw, 1, pl.ds(m, 1))
    chunks = len(xs)
    held, back = [], [None] * chunks
    for p in range(chunks):
        own = horner(xs[p], a)
        held.append(own if p == 0 else held[-1] * a8 + own)
    opens = [horner(gs[p][::-1], a) for p in range(chunks)]
    for p in reversed(range(chunks)):
        back[p] = opens[p] if p == chunks - 1 else back[p + 1] * a8 + opens[p]
    return held, back, opens


def by_span(scratch, half, j):
    return scratch[pl.ds(half * SUB * SUB + j, SUB, stride=SUB), :]


def gather_kernel(x_hbm, g_hbm, decay_hbm, segment, message, *refs):
    xf, gf, pw, ends, starts, inner, x_ref, g_ref, decay_ref, sems = refs
    copies = [
        pltpu.make_async_copy(source, target, sems.at[i])
        for i, (source, target) in enumerate(((x_hbm, x_ref), (g_hbm, g_ref), (decay_hbm, decay_ref)))
    ]
    for copy in copies:
        copy.start()
    modes, channels = decay_ref.shape
    chunks = x_ref.shape[0] // (SUB * SUB)
    span = chunks * SUB
    closing, opening, grad = (segment.at[pl.ds(i * modes, modes)] for i in range(3))
    for copy in copies:
        copy.wait()

    def tile_step(tile, _):
        lanes = pl.ds(pl.multiple_of(tile * LANES, LANES), LANES)
        split_lanes(x_ref, xf, tile)
        split_lanes(g_ref, gf, tile)
        decay = decay_ref[:, lanes]
        powers(decay, pw)
        xs, gs = read_tokens(xf, chunks), read_tokens(gf, chunks)
        for m in range(modes):
            held, back, opens = chunk_states(m, xs, gs, pw)
            rows = pl.ds(m * SUB, SUB)
            ends[rows, :] = held[-1]
            starts[rows, :] = back[0]
            inner[rows, :] = sum(opens[p] * held[p - 1] for p in range(1, chunks))
        lagged = []
        for lag in range(SUB):
            pairs = [gs[p][r] * xs[p][r - lag] for p in range(chunks) for r in range(lag, SUB)]
            lagged.append(jnp.sum(sum(pairs), axis=0, keepdims=True))
        for half in range(modes // SUB):
            some = pl.ds(half * SUB, SUB)
            a = pw[0, some, :]
            across = jnp.exp(-decay[half * SUB:(half + 1) * SUB] * span)
            arriving = jnp.zeros((SUB, LANES), F32)
            cross = jnp.zeros((SUB, LANES), F32)
            for j in range(SUB):
                cross = cross + (by_span(inner, half, j) + by_span(starts, half, j) * arriving)
                arriving = arriving * across + by_span(ends, half, j)
            leaving = horner([by_span(starts, half, j) for j in reversed(range(SUB))], across)
            near = horner([jnp.broadcast_to(v, (SUB, LANES)) for v in reversed(lagged)], a)
            closing[some, lanes] = arriving
            opening[some, lanes] = leaving
            grad[some, lanes] = near + a * cross
        return 0

    lax.fori_loop(0, channels // LANES, tile_step, 0)


    second = on_second()
    half = modes // 2
    for i in range(3):
        low, high = segment[pl.ds(i * modes, half)], segment[pl.ds(i * modes + half, half)]
        message[pl.ds(i * half, half)] = jnp.where(second, low, high)


def on_second():
    return lax.rem(lax.axis_index("ctx"), 2) == 1


def own_half(second, values):
    half = values.shape[0] // 2
    return jnp.where(second, values[half:], values[:half])


def both_halves(second, own, other):
    return jnp.where(second, other, own), jnp.where(second, own, other)


def local_kernel(tiles, x_ref, g_ref, residue_ref, decay_ref, _, out_ref, back_ref,
                 xf, gf, pw, ends, starts, before, after, arrive, leave):
    modes, channels = decay_ref.shape
    chunks = x_ref.shape[0] // (SUB * SUB)
    span = chunks * SUB

    def tile_step(tile, _):
        lanes = pl.ds(pl.multiple_of(tile * LANES, LANES), LANES)
        split_lanes(x_ref, xf, tile)
        split_lanes(g_ref, gf, tile)
        decay = decay_ref[:, lanes]
        residue = residue_ref[:, lanes]
        powers(decay, pw)
        pw[2] = residue * pw[0]
        xs, gs = read_tokens(xf, chunks), read_tokens(gf, chunks)
        for m in range(modes):
            held, back, _ = chunk_states(m, xs, gs, pw)
            rows = pl.ds(m * SUB, SUB)
            ends[rows, :] = held[-1]
            starts[rows, :] = back[0]
            for p in range(1, chunks):
                before[m, p - 1] = held[p - 1]
                after[m, p - 1] = back[p]
        for half in range(modes // SUB):
            across = jnp.exp(-decay[half * SUB:(half + 1) * SUB] * span)
            for target, source, order in ((arrive, ends, range(SUB)), (leave, starts, range(SUB - 1, -1, -1))):
                running = jnp.zeros((SUB, LANES), F32)
                for j in order:
                    target[pl.ds(half * SUB * SUB + j, SUB, stride=SUB), :] = running
                    running = running * across + by_span(source, half, j)
        taps = []
        weight = residue
        for lag in range(SUB):
            taps.append(jnp.broadcast_to(jnp.sum(weight, axis=0, keepdims=True), (SUB, LANES)))
            weight = weight * pw[0]
        for values, carried, inside, target, forward in (
            (xs, arrive, before, out_ref, True), (gs, leave, after, back_ref, False)
        ):
            order = range(SUB) if forward else range(SUB - 1, -1, -1)
            totals = []
            for p in range(chunks):
                seq = [values[p][r] for r in order]
                totals.append([sum(taps[lag] * seq[r - lag] for lag in range(r + 1)) for r in range(SUB)])
            for m in range(modes):
                a, a8, first = (row(pw, i, pl.ds(m, 1)) for i in range(3))
                edge = carried[pl.ds(m * SUB, SUB), :]
                for q in range(chunks):
                    p = q if forward else chunks - 1 - q
                    if q == 0:
                        state = edge
                    else:
                        edge = edge * a8
                        state = edge + inside[m, p - 1 if forward else p]
                    wave = state * first
                    for r in range(SUB):
                        totals[p][r] = totals[p][r] + wave
                        if r < SUB - 1:
                            wave = wave * a
            for p in range(chunks):
                for r, at in enumerate(order):
                    target[tile - tiles[0], p * SUB + at] = totals[p][r]
        return 0

    lax.fori_loop(tiles[0], tiles[1], tile_step, 0)


def join_chip_kernel(tokens, segment, other, decay_ref, _, joined, core):
    modes = decay_ref.shape[0]
    half = modes // 2
    second = on_second()
    decay = own_half(second, decay_ref[...])
    mine = [own_half(second, segment[i * modes:(i + 1) * modes]) for i in range(3)]
    theirs = [other[i * half:(i + 1) * half] for i in range(3)]
    (close0, close1), (open0, open1), _ = (both_halves(second, a, b) for a, b in zip(mine, theirs))
    block = jnp.exp(decay * (-1.0 * tokens))
    joined[0:half] = block * close0 + close1
    joined[half:2 * half] = open0 + block * open1
    joined[2 * half:] = (mine[2] + theirs[2]) + jnp.exp(-decay) * open1 * close0
    core[0:half] = close0
    core[half:] = open1


def join_kernel(tokens, size, count, last, *refs):
    segments = refs[:count]
    core, decay_ref, carried, _ = refs[count:count + 4]
    *outs, ordered = refs[count + 4:]
    second = on_second()
    decay = own_half(second, decay_ref[...])
    half = decay.shape[0]
    chip = lax.div(lax.axis_index("ctx"), 2)
    place = lax.rem(lax.div(chip, size), count)
    for m in range(count):
        ordered[place ^ m] = segments[m][...]
    block = jnp.exp(decay * (-2.0 * size * tokens))
    zero = jnp.zeros_like(decay)
    close, cross, grad, incoming = zero, zero, zero, zero
    for k in range(count):
        grad = grad + ordered[k, 2 * half:]
        if k:
            cross = cross + ordered[k, half:2 * half] * close
            incoming = jnp.where(place == k, close, incoming)
        close = close * block + ordered[k, 0:half]
    begin, outgoing = zero, zero
    for k in reversed(range(count)):
        outgoing = jnp.where(place == k, begin, outgoing)
        begin = begin * block + ordered[k, half:2 * half]
    grad = grad + jnp.exp(-decay) * cross
    if size > 1:
        inside = lax.rem(chip, size)
        incoming = carried[0:half] + incoming * jnp.exp(decay * (inside * (-2 * tokens)).astype(F32))
        outgoing = carried[half:] + outgoing * jnp.exp(decay * ((size - 1 - inside) * (-2 * tokens)).astype(F32))
    if not last:
        joined, arrivals = outs
        joined[0:half] = close
        joined[half:2 * half] = begin
        joined[2 * half:] = grad
        arrivals[0:half] = incoming
        arrivals[half:] = outgoing
        return
    total, own, message = outs
    total[...] = grad
    block = jnp.exp(decay * (-1.0 * tokens))
    into = incoming, block * incoming + core[0:half]
    out = block * outgoing + core[half:], outgoing
    own[0:half] = jnp.where(second, into[1], into[0])
    own[half:] = jnp.where(second, out[1], out[0])
    message[0:half] = jnp.where(second, into[0], into[1])
    message[half:] = jnp.where(second, out[0], out[1])


def finish_kernel(ranges, residue_ref, decay_ref, own, other, *refs):
    near = refs[:2 * len(ranges)]
    out_hbm, back_hbm, finished, out_ref, back_ref, result, pw, arrive, leave, sems = refs[2 * len(ranges):]
    modes, channels = decay_ref.shape
    half = modes // 2
    chunks = near[0].shape[1] // SUB
    span = chunks * SUB
    second = on_second()
    first = residue_ref[...] * jnp.exp(-decay_ref[...])
    for target, rows in ((arrive, slice(0, half)), (leave, slice(half, modes))):
        low, high = both_halves(second, own[rows], other[rows])
        target[0:half] = low * first[0:half]
        target[half:] = high * first[half:]

    def copy_out(tile, which):
        lanes = pl.ds(pl.multiple_of(tile * LANES, LANES), LANES)
        source, target = ((out_ref, out_hbm), (back_ref, back_hbm))[which]
        return pltpu.make_async_copy(source.at[:, lanes], target.at[:, lanes], sems.at[which, tile])

    def run(tiles, near_out, near_back):
        def tile_step(tile, _):
            lanes = pl.ds(pl.multiple_of(tile * LANES, LANES), LANES)
            decay = decay_ref[:, lanes]
            powers(decay, pw)
            pw[2] = decay * (-1.0 * span)
            pw[3] = arrive[:, lanes]
            pw[4] = leave[:, lanes]
            level = lax.broadcasted_iota(jnp.int32, (SUB, LANES), 0).astype(F32)
            for near, target, forward in ((near_out, out_ref, True), (near_back, back_ref, False)):
                order = range(SUB) if forward else range(SUB - 1, -1, -1)
                spans = level if forward else SUB - 1.0 - level
                totals = [[near[tile - tiles[0], p * SUB + r] for r in range(SUB)] for p in range(chunks)]
                for m in range(modes):
                    a, a8, rate = (row(pw, i, pl.ds(m, 1)) for i in range(3))
                    state = row(pw, 3 if forward else 4, pl.ds(m, 1)) * jnp.exp(rate * spans)
                    for q in range(chunks):
                        p = q if forward else chunks - 1 - q
                        wave = state
                        for r in order:
                            totals[p][r] = totals[p][r] + wave
                            wave = wave * a
                        if q < chunks - 1:
                            state = state * a8
                for p in range(chunks):
                    for r in range(SUB):
                        result[pl.ds(p * SUB + r, SUB, stride=span), :] = totals[p][r]
                target[:, lanes] = result[...].astype(target.dtype)
                copy_out(tile, 0 if forward else 1).start()
            return 0

        lax.fori_loop(tiles[0], tiles[1], tile_step, 0)

    for part, tiles in enumerate(ranges):
        run(tiles, near[2 * part], near[2 * part + 1])
    for tile in range(channels // LANES):
        for which in range(2):
            copy_out(tile, which).wait()
    finished[...] = jnp.zeros(finished.shape, F32)


def balanced(terms):
    while len(terms) > 1:
        terms = [a + b for a, b in zip(terms[::2], terms[1::2])]
    return terms[0]


def sum_kernel(*refs):
    refs[-1][...] = balanced([ref[...] for ref in refs[:-2]])


def assemble_kernel(scale, own, other, out_ref):
    half = own.shape[0]
    low, high = both_halves(on_second(), own[...], other[...])
    out_ref[0:half] = low * scale
    out_ref[half:] = high * scale


def vmem(*shape):
    return pltpu.VMEM(shape, F32)


def shaped(*shape):
    return jax.ShapeDtypeStruct(shape, F32)


def cost(flops, transcendentals, nbytes):
    return pl.CostEstimate(flops=flops, transcendentals=transcendentals, bytes_accessed=nbytes)


PARAMS = pltpu.CompilerParams(vmem_limit_bytes=32 * 1024 * 1024)
WHOLE = pl.BlockSpec(memory_space=pltpu.VMEM)
HBM = pl.BlockSpec(memory_space=pltpu.HBM)


UNREAD = pl.BlockSpec(memory_space=pl.ANY)


def body(signal, cotangent, residue, decay):
    tokens, channels = signal.shape
    modes = decay.shape[0]
    half = modes // 2
    n, groups = lax.axis_size("ctx"), lax.axis_size("ch")
    chunks = tokens // (SUB * SUB)
    elements = tokens * channels
    tokens_scratch = [vmem(tokens, LANES), vmem(tokens, LANES)]
    spans = vmem(modes * SUB, LANES)
    tiles = channels // LANES
    ranges = [(0, tiles // 4), (tiles // 4, tiles)]
    small = dict(compiler_params=PARAMS, cost_estimate=cost(elements, modes * channels, modes * channels * 32))

    def swap(x, axis, size, mask):
        return lax.ppermute(x, axis, [(i, i ^ mask) for i in range(size)])

    def near_part(part, after):
        first, last = ranges[part]
        share = elements * modes * (last - first) // tiles
        return pl.pallas_call(
            functools.partial(local_kernel, ranges[part]),
            out_shape=[shaped(last - first, chunks * SUB, SUB, LANES)] * 2,
            in_specs=[WHOLE] * 4 + [UNREAD],
            scratch_shapes=tokens_scratch
            + [vmem(3, modes, LANES), spans, spans]
            + [vmem(modes, chunks - 1, SUB, LANES)] * 2
            + [spans, spans],
            compiler_params=PARAMS,
            cost_estimate=cost(share * 400, 0, share),
            name="local_convolutions",
        )(signal, cotangent, residue, decay, after)

    segment, message = pl.pallas_call(
        gather_kernel,
        out_shape=[shaped(3 * modes, channels), shaped(3 * half, channels)],
        in_specs=[HBM] * 3,
        scratch_shapes=tokens_scratch
        + [vmem(2, modes, LANES), spans, spans, spans]
        + [pltpu.VMEM(signal.shape, signal.dtype)] * 2
        + [vmem(modes, channels), pltpu.SemaphoreType.DMA((3,))],
        compiler_params=PARAMS,
        cost_estimate=cost(elements * modes * 5, modes * channels * 3, elements * 6),
        name="block_states",
    )(*(pltpu.with_memory_space_constraint(a, pltpu.HBM) for a in (signal, cotangent, decay)))

    other = swap(message, "ctx", n, 1)
    near = near_part(0, segment)
    joined, core = pl.pallas_call(
        functools.partial(join_chip_kernel, tokens),
        out_shape=[shaped(3 * half, channels), shaped(2 * half, channels)],
        in_specs=[WHOLE] * 3 + [UNREAD],
        name="join_chip",
        **small,
    )(segment, other, decay, near[0])

    chips = n // 2
    size = 1
    carried = core
    while size < chips:
        count = min(4, chips // size)
        last = size * count == chips
        others = [swap(joined, "ctx", n, 2 * size * m) for m in range(1, count)]
        if last:
            near = near + near_part(1, joined)
        rows = [half, 2 * half, 2 * half] if last else [3 * half, 2 * half]
        joined, carried, *message = pl.pallas_call(
            functools.partial(join_kernel, tokens, size, count, last),
            out_shape=[shaped(r, channels) for r in rows],
            in_specs=[WHOLE] * (count + 3) + [UNREAD],
            scratch_shapes=[vmem(count, 3 * half, channels)],
            name="join_chips",
            **small,
        )(joined, *others, core, decay, carried, near[-1])
        size *= count

    received = swap(message[0], "ctx", n, 1)
    conv_out, signal_grad, finished = pl.pallas_call(
        functools.partial(finish_kernel, ranges),
        out_shape=[jax.ShapeDtypeStruct((tokens, channels), signal.dtype)] * 2 + [shaped(SUB, LANES)],
        in_specs=[WHOLE] * (4 + 2 * len(ranges)),
        out_specs=[HBM] * 2 + [WHOLE],
        scratch_shapes=[pltpu.VMEM((tokens, channels), signal.dtype)] * 2
        + [vmem(tokens, LANES), vmem(5, modes, LANES)]
        + [vmem(modes, channels)] * 2
        + [pltpu.SemaphoreType.DMA((2, tiles))],
        compiler_params=PARAMS,
        cost_estimate=cost(elements * modes * 600, 0, elements * 12),
        name="add_arrivals",
    )(residue, decay, carried, received, *near)

    grad = joined
    stride = 1
    while stride < groups:
        count = min(4, groups // stride)
        others = [swap(grad, "ch", groups, stride * m) for m in range(1, count)]
        grad = pl.pallas_call(
            sum_kernel,
            out_shape=shaped(half, channels),
            in_specs=[WHOLE] * count + [UNREAD],
            name="sum_groups",
            **small,
        )(grad, *others, finished)
        stride *= count
    residue_grad = pl.pallas_call(
        functools.partial(assemble_kernel, 1.0 / (tokens * n)),
        out_shape=shaped(modes, channels),
        name="assemble_gradient",
        **small,
    )(grad, swap(grad, "ctx", n, 1))
    return conv_out, signal_grad, residue_grad


def solution(mesh):
    return jax.shard_map(
        body,
        mesh=mesh,
        in_specs=(P("ctx", "ch"), P("ctx", "ch"), P(), P()),
        out_specs=(P("ctx", "ch"), P("ctx", "ch"), P()),
        check_vma=False,
    )
```

```python
import functools

import jax
import jax.numpy as jnp
from jax import lax
from jax.experimental import pallas as pl
from jax.experimental.pallas import tpu as pltpu
from jax.sharding import PartitionSpec as P

SUB = 8
LANES = 128
F32 = jnp.float32


def row(ref, *index):
    return jnp.broadcast_to(ref[index], (SUB, LANES))


def split_lanes(source, target, tile):
    lanes = pl.ds(pl.multiple_of(tile * LANES, LANES), LANES)
    target[...] = source[:, lanes].astype(F32)


def read_tokens(scratch, chunks):
    span = chunks * SUB
    return [[scratch[pl.ds(p * SUB + r, SUB, stride=span), :] for r in range(SUB)] for p in range(chunks)]


def powers(decay, pw):
    pw[0] = jnp.exp(-decay)
    pw[1] = jnp.exp(-decay * SUB)


def horner(terms, factor):
    total = terms[0]
    for term in terms[1:]:
        total = total * factor + term
    return total


def chunk_states(m, xs, gs, pw):
    a, a8 = row(pw, 0, pl.ds(m, 1)), row(pw, 1, pl.ds(m, 1))
    chunks = len(xs)
    held, back = [], [None] * chunks
    for p in range(chunks):
        own = horner(xs[p], a)
        held.append(own if p == 0 else held[-1] * a8 + own)
    opens = [horner(gs[p][::-1], a) for p in range(chunks)]
    for p in reversed(range(chunks)):
        back[p] = opens[p] if p == chunks - 1 else back[p + 1] * a8 + opens[p]
    return held, back, opens


def by_span(scratch, half, j):
    return scratch[pl.ds(half * SUB * SUB + j, SUB, stride=SUB), :]


def gather_kernel(*refs):
    sources, staged = refs[:4], refs[4:8]
    segment, message, xf, gf, pw, ends, starts, inner, sems = refs[8:]
    x_ref, g_ref, _, decay_ref = staged
    copies = [pltpu.make_async_copy(*pair, sems.at[i]) for i, pair in enumerate(zip(sources, staged))]
    for copy in copies:
        copy.start()
    modes, channels = decay_ref.shape
    chunks = x_ref.shape[0] // (SUB * SUB)
    span = chunks * SUB
    closing, opening, grad = (segment.at[pl.ds(i * modes, modes)] for i in range(3))
    for copy in copies:
        copy.wait()

    def tile_step(tile, _):
        lanes = pl.ds(pl.multiple_of(tile * LANES, LANES), LANES)
        split_lanes(x_ref, xf, tile)
        split_lanes(g_ref, gf, tile)
        decay = decay_ref[:, lanes]
        powers(decay, pw)
        xs, gs = read_tokens(xf, chunks), read_tokens(gf, chunks)
        for m in range(modes):
            held, back, opens = chunk_states(m, xs, gs, pw)
            rows = pl.ds(m * SUB, SUB)
            ends[rows, :] = held[-1]
            starts[rows, :] = back[0]
            inner[rows, :] = sum(opens[p] * held[p - 1] for p in range(1, chunks))
        lagged = []
        for lag in range(SUB):
            pairs = [gs[p][r] * xs[p][r - lag] for p in range(chunks) for r in range(lag, SUB)]
            lagged.append(jnp.sum(sum(pairs), axis=0, keepdims=True))
        for half in range(modes // SUB):
            some = pl.ds(half * SUB, SUB)
            a = pw[0, some, :]
            across = jnp.exp(-decay[half * SUB:(half + 1) * SUB] * span)
            arriving = jnp.zeros((SUB, LANES), F32)
            cross = jnp.zeros((SUB, LANES), F32)
            for j in range(SUB):
                cross = cross + (by_span(inner, half, j) + by_span(starts, half, j) * arriving)
                arriving = arriving * across + by_span(ends, half, j)
            leaving = horner([by_span(starts, half, j) for j in reversed(range(SUB))], across)
            near = horner([jnp.broadcast_to(v, (SUB, LANES)) for v in reversed(lagged)], a)
            closing[some, lanes] = arriving
            opening[some, lanes] = leaving
            grad[some, lanes] = near + a * cross
        return 0

    lax.fori_loop(0, channels // LANES, tile_step, 0)


    second = on_second()
    half = modes // 2
    for i in range(3):
        low, high = segment[pl.ds(i * modes, half)], segment[pl.ds(i * modes + half, half)]
        message[pl.ds(i * half, half)] = jnp.where(second, low, high)


def on_second():
    return lax.rem(lax.axis_index("ctx"), 2) == 1


def own_half(second, values):
    half = values.shape[0] // 2
    return jnp.where(second, values[half:], values[:half])


def both_halves(second, own, other):
    return jnp.where(second, other, own), jnp.where(second, own, other)


def local_kernel(tiles, x_ref, g_ref, residue_ref, decay_ref, _, out_ref, back_ref,
                 xf, gf, pw, ends, starts, before, after, arrive, leave):
    modes, channels = decay_ref.shape
    chunks = x_ref.shape[0] // (SUB * SUB)
    span = chunks * SUB

    def tile_step(tile, _):
        lanes = pl.ds(pl.multiple_of(tile * LANES, LANES), LANES)
        split_lanes(x_ref, xf, tile)
        split_lanes(g_ref, gf, tile)
        decay = decay_ref[:, lanes]
        residue = residue_ref[:, lanes]
        powers(decay, pw)
        pw[2] = residue * pw[0]
        xs, gs = read_tokens(xf, chunks), read_tokens(gf, chunks)
        for m in range(modes):
            held, back, _ = chunk_states(m, xs, gs, pw)
            rows = pl.ds(m * SUB, SUB)
            ends[rows, :] = held[-1]
            starts[rows, :] = back[0]
            for p in range(1, chunks):
                before[m, p - 1] = held[p - 1]
                after[m, p - 1] = back[p]
        for half in range(modes // SUB):
            across = jnp.exp(-decay[half * SUB:(half + 1) * SUB] * span)
            for target, source, order in ((arrive, ends, range(SUB)), (leave, starts, range(SUB - 1, -1, -1))):
                running = jnp.zeros((SUB, LANES), F32)
                for j in order:
                    target[pl.ds(half * SUB * SUB + j, SUB, stride=SUB), :] = running
                    running = running * across + by_span(source, half, j)
        taps = []
        weight = residue
        for lag in range(SUB):
            taps.append(jnp.broadcast_to(jnp.sum(weight, axis=0, keepdims=True), (SUB, LANES)))
            weight = weight * pw[0]
        for values, carried, inside, target, forward in (
            (xs, arrive, before, out_ref, True), (gs, leave, after, back_ref, False)
        ):
            order = range(SUB) if forward else range(SUB - 1, -1, -1)
            totals = []
            for p in range(chunks):
                seq = [values[p][r] for r in order]
                totals.append([sum(taps[lag] * seq[r - lag] for lag in range(r + 1)) for r in range(SUB)])
            for m in range(modes):
                a, a8, first = (row(pw, i, pl.ds(m, 1)) for i in range(3))
                edge = carried[pl.ds(m * SUB, SUB), :]
                for q in range(chunks):
                    p = q if forward else chunks - 1 - q
                    if q == 0:
                        state = edge
                    else:
                        edge = edge * a8
                        state = edge + inside[m, p - 1 if forward else p]
                    wave = state * first
                    for r in range(SUB):
                        totals[p][r] = totals[p][r] + wave
                        if r < SUB - 1:
                            wave = wave * a
            for p in range(chunks):
                for r, at in enumerate(order):
                    target[tile - tiles[0], p * SUB + at] = totals[p][r]
        return 0

    lax.fori_loop(tiles[0], tiles[1], tile_step, 0)


def join_chip_kernel(tokens, segment, other, decay_ref, _, joined, core):
    modes = decay_ref.shape[0]
    half = modes // 2
    second = on_second()
    decay = own_half(second, decay_ref[...])
    mine = [own_half(second, segment[i * modes:(i + 1) * modes]) for i in range(3)]
    theirs = [other[i * half:(i + 1) * half] for i in range(3)]
    (close0, close1), (open0, open1), _ = (both_halves(second, a, b) for a, b in zip(mine, theirs))
    block = jnp.exp(decay * (-1.0 * tokens))
    joined[0:half] = block * close0 + close1
    joined[half:2 * half] = open0 + block * open1
    joined[2 * half:] = (mine[2] + theirs[2]) + jnp.exp(-decay) * open1 * close0
    core[0:half] = close0
    core[half:] = open1


def join_kernel(tokens, size, masks, last, *refs):
    count = len(masks)
    segments = refs[:count]
    core, decay_ref, carried, _ = refs[count:count + 4]
    *outs, ordered = refs[count + 4:]
    second = on_second()
    decay = own_half(second, decay_ref[...])
    half = decay.shape[0]
    chip = lax.div(lax.axis_index("ctx"), 2)
    place = lax.rem(lax.div(chip, size), count)
    for mask, segment in zip(masks, segments):
        ordered[place ^ mask] = segment[...]
    block = jnp.exp(decay * (-2.0 * size * tokens))
    zero = jnp.zeros_like(decay)
    close, cross, grad, incoming = zero, zero, zero, zero
    for k in range(count):
        grad = grad + ordered[k, 2 * half:]
        if k:
            cross = cross + ordered[k, half:2 * half] * close
            incoming = jnp.where(place == k, close, incoming)
        close = close * block + ordered[k, 0:half]
    begin, outgoing = zero, zero
    for k in reversed(range(count)):
        outgoing = jnp.where(place == k, begin, outgoing)
        begin = begin * block + ordered[k, half:2 * half]
    grad = grad + jnp.exp(-decay) * cross
    if size > 1:
        inside = lax.rem(chip, size)
        incoming = carried[0:half] + incoming * jnp.exp(decay * (inside * (-2 * tokens)).astype(F32))
        outgoing = carried[half:] + outgoing * jnp.exp(decay * ((size - 1 - inside) * (-2 * tokens)).astype(F32))
    if not last:
        joined, arrivals = outs
        joined[0:half] = close
        joined[half:2 * half] = begin
        joined[2 * half:] = grad
        arrivals[0:half] = incoming
        arrivals[half:] = outgoing
        return
    total, own, message = outs
    total[...] = grad
    block = jnp.exp(decay * (-1.0 * tokens))
    into = incoming, block * incoming + core[0:half]
    out = block * outgoing + core[half:], outgoing
    own[0:half] = jnp.where(second, into[1], into[0])
    own[half:] = jnp.where(second, out[1], out[0])
    message[0:half] = jnp.where(second, into[0], into[1])
    message[half:] = jnp.where(second, out[0], out[1])


def finish_kernel(ranges, residue_ref, decay_ref, own, other, *refs):
    near = refs[:2 * len(ranges)]
    _, out_hbm, back_hbm, finished, out_ref, back_ref, result, pw, arrive, leave, sems = refs[2 * len(ranges):]
    modes, channels = decay_ref.shape
    half = modes // 2
    chunks = near[0].shape[1] // SUB
    span = chunks * SUB
    second = on_second()
    first = residue_ref[...] * jnp.exp(-decay_ref[...])
    for target, rows in ((arrive, slice(0, half)), (leave, slice(half, modes))):
        low, high = both_halves(second, own[rows], other[rows])
        target[0:half] = low * first[0:half]
        target[half:] = high * first[half:]

    def copy_out(tile, which):
        lanes = pl.ds(pl.multiple_of(tile * LANES, LANES), LANES)
        source, target = ((out_ref, out_hbm), (back_ref, back_hbm))[which]
        return pltpu.make_async_copy(source.at[:, lanes], target.at[:, lanes], sems.at[which, tile])

    def run(tiles, near_out, near_back):
        def tile_step(tile, _):
            lanes = pl.ds(pl.multiple_of(tile * LANES, LANES), LANES)
            decay = decay_ref[:, lanes]
            powers(decay, pw)
            pw[2] = decay * (-1.0 * span)
            pw[3] = arrive[:, lanes]
            pw[4] = leave[:, lanes]
            level = lax.broadcasted_iota(jnp.int32, (SUB, LANES), 0).astype(F32)
            for near, target, forward in ((near_out, out_ref, True), (near_back, back_ref, False)):
                order = range(SUB) if forward else range(SUB - 1, -1, -1)
                spans = level if forward else SUB - 1.0 - level
                totals = [[near[tile - tiles[0], p * SUB + r] for r in range(SUB)] for p in range(chunks)]
                for m in range(modes):
                    a, a8, rate = (row(pw, i, pl.ds(m, 1)) for i in range(3))
                    state = row(pw, 3 if forward else 4, pl.ds(m, 1)) * jnp.exp(rate * spans)
                    for q in range(chunks):
                        p = q if forward else chunks - 1 - q
                        wave = state
                        for r in order:
                            totals[p][r] = totals[p][r] + wave
                            wave = wave * a
                        if q < chunks - 1:
                            state = state * a8
                for p in range(chunks):
                    for r in range(SUB):
                        result[pl.ds(p * SUB + r, SUB, stride=span), :] = totals[p][r]
                target[:, lanes] = result[...].astype(target.dtype)
                copy_out(tile, 0 if forward else 1).start()
            return 0

        lax.fori_loop(tiles[0], tiles[1], tile_step, 0)

    for part, tiles in enumerate(ranges):
        run(tiles, near[2 * part], near[2 * part + 1])
    for tile in range(channels // LANES):
        for which in range(2):
            copy_out(tile, which).wait()
    finished[...] = jnp.zeros(finished.shape, F32)


def sum_kernel(own, other, _, out_ref):
    out_ref[...] = own[...] + other[...]


def assemble_kernel(scale, own, other, out_ref):
    half = own.shape[0]
    low, high = both_halves(on_second(), own[...], other[...])
    out_ref[0:half] = low * scale
    out_ref[half:] = high * scale


def vmem(*shape):
    return pltpu.VMEM(shape, F32)


def shaped(*shape):
    return jax.ShapeDtypeStruct(shape, F32)


def cost(flops, transcendentals, nbytes):
    return pl.CostEstimate(flops=flops, transcendentals=transcendentals, bytes_accessed=nbytes)


PARAMS = pltpu.CompilerParams(vmem_limit_bytes=32 * 1024 * 1024)
WHOLE = pl.BlockSpec(memory_space=pltpu.VMEM)
HBM = pl.BlockSpec(memory_space=pltpu.HBM)


UNREAD = pl.BlockSpec(memory_space=pl.ANY)


def body(signal, cotangent, residue, decay):
    tokens, channels = signal.shape
    modes = decay.shape[0]
    half = modes // 2
    n, groups = lax.axis_size("ctx"), lax.axis_size("ch")
    chunks = tokens // (SUB * SUB)
    elements = tokens * channels
    tokens_scratch = [vmem(tokens, LANES), vmem(tokens, LANES)]
    spans = vmem(modes * SUB, LANES)
    tiles = channels // LANES
    quarter = tiles // 4
    ranges = [(0, quarter), (quarter, 3 * quarter), (3 * quarter, tiles)]
    small = dict(compiler_params=PARAMS, cost_estimate=cost(elements, modes * channels, modes * channels * 32))

    def swap(x, axis, size, mask):
        return lax.ppermute(x, axis, [(i, i ^ mask) for i in range(size)])

    def near_part(part, after):
        first, last = ranges[part]
        share = elements * modes * (last - first) // tiles
        return pl.pallas_call(
            functools.partial(local_kernel, ranges[part]),
            out_shape=[shaped(last - first, chunks * SUB, SUB, LANES)] * 2,
            in_specs=[WHOLE] * 4 + [UNREAD],
            scratch_shapes=tokens_scratch
            + [vmem(3, modes, LANES), spans, spans]
            + [vmem(modes, chunks - 1, SUB, LANES)] * 2
            + [spans, spans],
            compiler_params=PARAMS,
            cost_estimate=cost(share * 400, 0, share),
            name="local_convolutions",
        )(signal, cotangent, residue, decay, after)

    inputs = signal, cotangent, residue, decay
    signal, cotangent, residue, decay, segment, message = pl.pallas_call(
        gather_kernel,
        out_shape=[jax.ShapeDtypeStruct(a.shape, a.dtype) for a in inputs]
        + [shaped(3 * modes, channels), shaped(3 * half, channels)],
        in_specs=[HBM] * 4,
        scratch_shapes=tokens_scratch
        + [vmem(2, modes, LANES), spans, spans, spans, pltpu.SemaphoreType.DMA((4,))],
        compiler_params=PARAMS,
        cost_estimate=cost(elements * modes * 5, modes * channels * 3, elements * 6),
        name="block_states",
    )(*(pltpu.with_memory_space_constraint(a, pltpu.HBM) for a in inputs))

    other = swap(message, "ctx", n, 1)
    near = near_part(0, segment)
    joined, core = pl.pallas_call(
        functools.partial(join_chip_kernel, tokens),
        out_shape=[shaped(3 * half, channels), shaped(2 * half, channels)],
        in_specs=[WHOLE] * 3 + [UNREAD],
        name="join_chip",
        **small,
    )(segment, other, decay, near[0])

    chips = n // 2
    size = 1
    carried = core
    while size < chips:
        count = min(4, chips // size)
        last = size * count == chips
        masks = [3, 1, 2] if count == 4 else [1]
        others = [swap(joined, "ctx", n, 2 * size * m) for m in masks]
        if last:
            near = near + near_part(1, joined)
        rows = [half, 2 * half, 2 * half] if last else [3 * half, 2 * half]
        joined, carried, *message = pl.pallas_call(
            functools.partial(join_kernel, tokens, size, [0] + masks, last),
            out_shape=[shaped(r, channels) for r in rows],
            in_specs=[WHOLE] * (count + 3) + [UNREAD],
            scratch_shapes=[vmem(count, 3 * half, channels)],
            name="join_chips",
            **small,
        )(joined, *others, core, decay, carried, near[-1])
        size *= count

    grad = joined
    stride = 1
    while stride < groups:
        other = swap(grad, "ch", groups, stride)
        if stride == 1:
            received = swap(message[0], "ctx", n, 1)
            near = near + near_part(2, grad)
            pinned = near[-1]
        stride *= 2
        if stride == groups:
            conv_out, signal_grad, pinned = pl.pallas_call(
                functools.partial(finish_kernel, ranges),
                out_shape=[jax.ShapeDtypeStruct((tokens, channels), signal.dtype)] * 2 + [shaped(SUB, LANES)],
                in_specs=[WHOLE] * (4 + 2 * len(ranges)) + [UNREAD],
                out_specs=[HBM] * 2 + [WHOLE],
                scratch_shapes=[pltpu.VMEM((tokens, channels), signal.dtype)] * 2
                + [vmem(tokens, LANES), vmem(5, modes, LANES)]
                + [vmem(modes, channels)] * 2
                + [pltpu.SemaphoreType.DMA((2, tiles))],
                compiler_params=PARAMS,
                cost_estimate=cost(elements * modes * 600, 0, elements * 12),
                name="add_arrivals",
            )(residue, decay, carried, received, *near, grad)
        grad = pl.pallas_call(
            sum_kernel,
            out_shape=shaped(half, channels),
            in_specs=[WHOLE] * 2 + [UNREAD],
            name="sum_groups",
            **small,
        )(grad, other, pinned)
    residue_grad = pl.pallas_call(
        functools.partial(assemble_kernel, 1.0 / (tokens * n)),
        out_shape=shaped(modes, channels),
        name="assemble_gradient",
        **small,
    )(grad, swap(grad, "ctx", n, 1))
    return conv_out, signal_grad, residue_grad


def solution(mesh):
    return jax.shard_map(
        body,
        mesh=mesh,
        in_specs=(P("ctx", "ch"), P("ctx", "ch"), P(), P()),
        out_specs=(P("ctx", "ch"), P("ctx", "ch"), P()),
        check_vma=False,
    )
```

```python
import functools

import jax
import jax.numpy as jnp
from jax import lax
from jax.experimental import pallas as pl
from jax.experimental.pallas import tpu as pltpu
from jax.sharding import PartitionSpec as P

SUB = 8
LANES = 128
F32 = jnp.float32


def row(ref, *index):
    return jnp.broadcast_to(ref[index], (SUB, LANES))


def split_lanes(source, target, tile):
    lanes = pl.ds(pl.multiple_of(tile * LANES, LANES), LANES)
    target[...] = source[:, lanes].astype(F32)


def read_tokens(scratch, chunks):
    span = chunks * SUB
    return [[scratch[pl.ds(p * SUB + r, SUB, stride=span), :] for r in range(SUB)] for p in range(chunks)]


def powers(decay, pw):
    pw[0] = jnp.exp(-decay)
    pw[1] = jnp.exp(-decay * SUB)


def horner(terms, factor):
    total = terms[0]
    for term in terms[1:]:
        total = total * factor + term
    return total


def chunk_states(m, xs, gs, pw):
    a, a8 = row(pw, 0, pl.ds(m, 1)), row(pw, 1, pl.ds(m, 1))
    chunks = len(xs)
    held, back = [], [None] * chunks
    for p in range(chunks):
        own = horner(xs[p], a)
        held.append(own if p == 0 else held[-1] * a8 + own)
    opens = [horner(gs[p][::-1], a) for p in range(chunks)]
    for p in reversed(range(chunks)):
        back[p] = opens[p] if p == chunks - 1 else back[p + 1] * a8 + opens[p]
    return held, back, opens


def by_span(scratch, half, j):
    return scratch[pl.ds(half * SUB * SUB + j, SUB, stride=SUB), :]


def gather_kernel(*refs):
    sources, staged = refs[:4], refs[4:8]
    segment, message, xf, gf, pw, ends, starts, inner, sems = refs[8:]
    x_ref, g_ref, _, decay_ref = staged
    copies = [pltpu.make_async_copy(*pair, sems.at[i]) for i, pair in enumerate(zip(sources, staged))]
    for copy in copies:
        copy.start()
    modes, channels = decay_ref.shape
    chunks = x_ref.shape[0] // (SUB * SUB)
    span = chunks * SUB
    closing, opening, grad = (segment.at[pl.ds(i * modes, modes)] for i in range(3))
    for copy in copies:
        copy.wait()

    def tile_step(tile, _):
        lanes = pl.ds(pl.multiple_of(tile * LANES, LANES), LANES)
        split_lanes(x_ref, xf, tile)
        split_lanes(g_ref, gf, tile)
        decay = decay_ref[:, lanes]
        powers(decay, pw)
        xs, gs = read_tokens(xf, chunks), read_tokens(gf, chunks)
        for m in range(modes):
            held, back, opens = chunk_states(m, xs, gs, pw)
            rows = pl.ds(m * SUB, SUB)
            ends[rows, :] = held[-1]
            starts[rows, :] = back[0]
            inner[rows, :] = sum(opens[p] * held[p - 1] for p in range(1, chunks))
        lagged = []
        for lag in range(SUB):
            pairs = [gs[p][r] * xs[p][r - lag] for p in range(chunks) for r in range(lag, SUB)]
            lagged.append(jnp.sum(sum(pairs), axis=0, keepdims=True))
        for half in range(modes // SUB):
            some = pl.ds(half * SUB, SUB)
            a = pw[0, some, :]
            across = jnp.exp(-decay[half * SUB:(half + 1) * SUB] * span)
            arriving = jnp.zeros((SUB, LANES), F32)
            cross = jnp.zeros((SUB, LANES), F32)
            for j in range(SUB):
                cross = cross + (by_span(inner, half, j) + by_span(starts, half, j) * arriving)
                arriving = arriving * across + by_span(ends, half, j)
            leaving = horner([by_span(starts, half, j) for j in reversed(range(SUB))], across)
            near = horner([jnp.broadcast_to(v, (SUB, LANES)) for v in reversed(lagged)], a)
            closing[some, lanes] = arriving
            opening[some, lanes] = leaving
            grad[some, lanes] = near + a * cross
        return 0

    lax.fori_loop(0, channels // LANES, tile_step, 0)


    own_high = owns_high()
    half = modes // 2
    for i in range(3):
        low, high = segment[pl.ds(i * modes, half)], segment[pl.ds(i * modes + half, half)]
        message[pl.ds(i * half, half)] = jnp.where(own_high, low, high)


def on_second():
    return lax.rem(lax.axis_index("ctx"), 2) == 1


def owns_high():
    place, group = lax.axis_index("ctx"), lax.axis_index("ch")
    bits = place ^ group
    for shift in (16, 8, 4, 2, 1):
        bits = bits ^ lax.shift_right_logical(bits, jnp.int32(shift))
    return lax.rem(bits, 2) == 1


def own_half(high, values):
    half = values.shape[0] // 2
    return jnp.where(high, values[half:], values[:half])


def in_order(second, own, other):
    return jnp.where(second, other, own), jnp.where(second, own, other)


def local_kernel(tiles, x_ref, g_ref, residue_ref, decay_ref, _, out_ref, back_ref,
                 xf, gf, pw, ends, starts, before, after, arrive, leave):
    modes, channels = decay_ref.shape
    chunks = x_ref.shape[0] // (SUB * SUB)
    span = chunks * SUB

    def tile_step(tile, _):
        lanes = pl.ds(pl.multiple_of(tile * LANES, LANES), LANES)
        split_lanes(x_ref, xf, tile)
        split_lanes(g_ref, gf, tile)
        decay = decay_ref[:, lanes]
        residue = residue_ref[:, lanes]
        powers(decay, pw)
        pw[2] = residue * pw[0]
        xs, gs = read_tokens(xf, chunks), read_tokens(gf, chunks)
        for m in range(modes):
            held, back, _ = chunk_states(m, xs, gs, pw)
            rows = pl.ds(m * SUB, SUB)
            ends[rows, :] = held[-1]
            starts[rows, :] = back[0]
            for p in range(1, chunks):
                before[m, p - 1] = held[p - 1]
                after[m, p - 1] = back[p]
        for half in range(modes // SUB):
            across = jnp.exp(-decay[half * SUB:(half + 1) * SUB] * span)
            for target, source, order in ((arrive, ends, range(SUB)), (leave, starts, range(SUB - 1, -1, -1))):
                running = jnp.zeros((SUB, LANES), F32)
                for j in order:
                    target[pl.ds(half * SUB * SUB + j, SUB, stride=SUB), :] = running
                    running = running * across + by_span(source, half, j)
        taps = []
        weight = residue
        for lag in range(SUB):
            taps.append(jnp.broadcast_to(jnp.sum(weight, axis=0, keepdims=True), (SUB, LANES)))
            weight = weight * pw[0]
        for values, carried, inside, target, forward in (
            (xs, arrive, before, out_ref, True), (gs, leave, after, back_ref, False)
        ):
            order = range(SUB) if forward else range(SUB - 1, -1, -1)
            totals = []
            for p in range(chunks):
                seq = [values[p][r] for r in order]
                totals.append([sum(taps[lag] * seq[r - lag] for lag in range(r + 1)) for r in range(SUB)])
            for m in range(modes):
                a, a8, first = (row(pw, i, pl.ds(m, 1)) for i in range(3))
                edge = carried[pl.ds(m * SUB, SUB), :]
                for q in range(chunks):
                    p = q if forward else chunks - 1 - q
                    if q == 0:
                        state = edge
                    else:
                        edge = edge * a8
                        state = edge + inside[m, p - 1 if forward else p]
                    wave = state * first
                    for r in range(SUB):
                        totals[p][r] = totals[p][r] + wave
                        if r < SUB - 1:
                            wave = wave * a
            for p in range(chunks):
                for r, at in enumerate(order):
                    target[tile - tiles[0], p * SUB + at] = totals[p][r]
        return 0

    lax.fori_loop(tiles[0], tiles[1], tile_step, 0)


def join_chip_kernel(tokens, segment, other, decay_ref, _, joined, core):
    modes = decay_ref.shape[0]
    half = modes // 2
    high = owns_high()
    decay = own_half(high, decay_ref[...])
    mine = [own_half(high, segment[i * modes:(i + 1) * modes]) for i in range(3)]
    theirs = [other[i * half:(i + 1) * half] for i in range(3)]
    (close0, close1), (open0, open1), _ = (in_order(on_second(), a, b) for a, b in zip(mine, theirs))
    block = jnp.exp(decay * (-1.0 * tokens))
    joined[0:half] = block * close0 + close1
    joined[half:2 * half] = open0 + block * open1
    joined[2 * half:] = (mine[2] + theirs[2]) + jnp.exp(-decay) * open1 * close0
    core[0:half] = close0
    core[half:] = open1


def join_kernel(tokens, size, masks, last, *refs):
    count = len(masks)
    segments = refs[:count]
    core, decay_ref, carried, _ = refs[count:count + 4]
    *outs, ordered = refs[count + 4:]
    second = on_second()
    decay = own_half(owns_high(), decay_ref[...])
    half = decay.shape[0]
    chip = lax.div(lax.axis_index("ctx"), 2)
    place = lax.rem(lax.div(chip, size), count)
    for mask, segment in zip(masks, segments):
        ordered[place ^ mask] = segment[...]
    block = jnp.exp(decay * (-2.0 * size * tokens))
    zero = jnp.zeros_like(decay)
    close, cross, grad, incoming = zero, zero, zero, zero
    for k in range(count):
        grad = grad + ordered[k, 2 * half:]
        if k:
            cross = cross + ordered[k, half:2 * half] * close
            incoming = jnp.where(place == k, close, incoming)
        close = close * block + ordered[k, 0:half]
    begin, outgoing = zero, zero
    for k in reversed(range(count)):
        outgoing = jnp.where(place == k, begin, outgoing)
        begin = begin * block + ordered[k, half:2 * half]
    grad = grad + jnp.exp(-decay) * cross
    if size > 1:
        inside = lax.rem(chip, size)
        incoming = carried[0:half] + incoming * jnp.exp(decay * (inside * (-2 * tokens)).astype(F32))
        outgoing = carried[half:] + outgoing * jnp.exp(decay * ((size - 1 - inside) * (-2 * tokens)).astype(F32))
    if not last:
        joined, arrivals = outs
        joined[0:half] = close
        joined[half:2 * half] = begin
        joined[2 * half:] = grad
        arrivals[0:half] = incoming
        arrivals[half:] = outgoing
        return
    total, own, message = outs
    total[...] = grad
    block = jnp.exp(decay * (-1.0 * tokens))
    into = incoming, block * incoming + core[0:half]
    out = block * outgoing + core[half:], outgoing
    own[0:half] = jnp.where(second, into[1], into[0])
    own[half:] = jnp.where(second, out[1], out[0])
    message[0:half] = jnp.where(second, into[0], into[1])
    message[half:] = jnp.where(second, out[0], out[1])


def finish_kernel(ranges, residue_ref, decay_ref, own, other, *refs):
    near = refs[:2 * len(ranges)]
    _, out_hbm, back_hbm, finished, out_ref, back_ref, result, pw, arrive, leave, sems = refs[2 * len(ranges):]
    modes, channels = decay_ref.shape
    half = modes // 2
    chunks = near[0].shape[1] // SUB
    span = chunks * SUB
    own_high = owns_high()
    first = residue_ref[...] * jnp.exp(-decay_ref[...])
    for target, rows in ((arrive, slice(0, half)), (leave, slice(half, modes))):
        low, high = in_order(own_high, own[rows], other[rows])
        target[0:half] = low * first[0:half]
        target[half:] = high * first[half:]

    def copy_out(tile, which):
        lanes = pl.ds(pl.multiple_of(tile * LANES, LANES), LANES)
        source, target = ((out_ref, out_hbm), (back_ref, back_hbm))[which]
        return pltpu.make_async_copy(source.at[:, lanes], target.at[:, lanes], sems.at[which, tile])

    def run(tiles, near_out, near_back):
        def tile_step(tile, _):
            lanes = pl.ds(pl.multiple_of(tile * LANES, LANES), LANES)
            decay = decay_ref[:, lanes]
            powers(decay, pw)
            pw[2] = decay * (-1.0 * span)
            pw[3] = arrive[:, lanes]
            pw[4] = leave[:, lanes]
            level = lax.broadcasted_iota(jnp.int32, (SUB, LANES), 0).astype(F32)
            for near, target, forward in ((near_out, out_ref, True), (near_back, back_ref, False)):
                order = range(SUB) if forward else range(SUB - 1, -1, -1)
                spans = level if forward else SUB - 1.0 - level
                totals = [[near[tile - tiles[0], p * SUB + r] for r in range(SUB)] for p in range(chunks)]
                for m in range(modes):
                    a, a8, rate = (row(pw, i, pl.ds(m, 1)) for i in range(3))
                    state = row(pw, 3 if forward else 4, pl.ds(m, 1)) * jnp.exp(rate * spans)
                    for q in range(chunks):
                        p = q if forward else chunks - 1 - q
                        wave = state
                        for r in order:
                            totals[p][r] = totals[p][r] + wave
                            wave = wave * a
                        if q < chunks - 1:
                            state = state * a8
                for p in range(chunks):
                    for r in range(SUB):
                        result[pl.ds(p * SUB + r, SUB, stride=span), :] = totals[p][r]
                target[:, lanes] = result[...].astype(target.dtype)
                copy_out(tile, 0 if forward else 1).start()
            return 0

        lax.fori_loop(tiles[0], tiles[1], tile_step, 0)

    for part, tiles in enumerate(ranges):
        run(tiles, near[2 * part], near[2 * part + 1])
    for tile in range(channels // LANES):
        for which in range(2):
            copy_out(tile, which).wait()
    finished[...] = jnp.zeros(finished.shape, F32)


def sum_kernel(own, other, _, out_ref):
    out_ref[...] = own[...] + other[...]


def assemble_kernel(scale, own, other, out_ref):
    half = own.shape[0]
    low, high = in_order(owns_high(), own[...], other[...])
    out_ref[0:half] = low * scale
    out_ref[half:] = high * scale


def vmem(*shape):
    return pltpu.VMEM(shape, F32)


def shaped(*shape):
    return jax.ShapeDtypeStruct(shape, F32)


def cost(flops, transcendentals, nbytes):
    return pl.CostEstimate(flops=flops, transcendentals=transcendentals, bytes_accessed=nbytes)


PARAMS = pltpu.CompilerParams(vmem_limit_bytes=32 * 1024 * 1024)
WHOLE = pl.BlockSpec(memory_space=pltpu.VMEM)
HBM = pl.BlockSpec(memory_space=pltpu.HBM)


UNREAD = pl.BlockSpec(memory_space=pl.ANY)


def body(signal, cotangent, residue, decay):
    tokens, channels = signal.shape
    modes = decay.shape[0]
    half = modes // 2
    n, groups = lax.axis_size("ctx"), lax.axis_size("ch")
    chunks = tokens // (SUB * SUB)
    elements = tokens * channels
    tokens_scratch = [vmem(tokens, LANES), vmem(tokens, LANES)]
    spans = vmem(modes * SUB, LANES)
    tiles = channels // LANES
    quarter = tiles // 4
    ranges = [(0, quarter), (quarter, 3 * quarter), (3 * quarter, tiles)]
    small = dict(compiler_params=PARAMS, cost_estimate=cost(elements, modes * channels, modes * channels * 32))

    def swap(x, ctx_mask, ch_mask=0):
        if ctx_mask != 1:
            ctx_mask |= (ctx_mask.bit_count() + ch_mask.bit_count()) % 2
        mask = ctx_mask * groups + ch_mask
        return lax.ppermute(x, ("ctx", "ch"), [(i, i ^ mask) for i in range(n * groups)])

    def near_part(part, after):
        first, last = ranges[part]
        share = elements * modes * (last - first) // tiles
        return pl.pallas_call(
            functools.partial(local_kernel, ranges[part]),
            out_shape=[shaped(last - first, chunks * SUB, SUB, LANES)] * 2,
            in_specs=[WHOLE] * 4 + [UNREAD],
            scratch_shapes=tokens_scratch
            + [vmem(3, modes, LANES), spans, spans]
            + [vmem(modes, chunks - 1, SUB, LANES)] * 2
            + [spans, spans],
            compiler_params=PARAMS,
            cost_estimate=cost(share * 400, 0, share),
            name="local_convolutions",
        )(signal, cotangent, residue, decay, after)

    inputs = signal, cotangent, residue, decay
    signal, cotangent, residue, decay, segment, message = pl.pallas_call(
        gather_kernel,
        out_shape=[jax.ShapeDtypeStruct(a.shape, a.dtype) for a in inputs]
        + [shaped(3 * modes, channels), shaped(3 * half, channels)],
        in_specs=[HBM] * 4,
        scratch_shapes=tokens_scratch
        + [vmem(2, modes, LANES), spans, spans, spans, pltpu.SemaphoreType.DMA((4,))],
        compiler_params=PARAMS,
        cost_estimate=cost(elements * modes * 5, modes * channels * 3, elements * 6),
        name="block_states",
    )(*(pltpu.with_memory_space_constraint(a, pltpu.HBM) for a in inputs))

    other = swap(message, 1)
    near = near_part(0, segment)
    joined, core = pl.pallas_call(
        functools.partial(join_chip_kernel, tokens),
        out_shape=[shaped(3 * half, channels), shaped(2 * half, channels)],
        in_specs=[WHOLE] * 3 + [UNREAD],
        name="join_chip",
        **small,
    )(segment, other, decay, near[0])

    chips = n // 2
    size = 1
    carried = core
    while size < chips:
        count = min(4, chips // size)
        last = size * count == chips
        masks = [3, 1, 2] if count == 4 else [1]
        others = [swap(joined, 2 * size * m) for m in masks]
        if last:
            near = near + near_part(1, joined)
        rows = [half, 2 * half, 2 * half] if last else [3 * half, 2 * half]
        joined, carried, *message = pl.pallas_call(
            functools.partial(join_kernel, tokens, size, [0] + masks, last),
            out_shape=[shaped(r, channels) for r in rows],
            in_specs=[WHOLE] * (count + 3) + [UNREAD],
            scratch_shapes=[vmem(count, 3 * half, channels)],
            name="join_chips",
            **small,
        )(joined, *others, core, decay, carried, near[-1])
        size *= count

    grad = joined
    stride = 1
    while stride < groups:
        other = swap(grad, 0, stride)
        if stride == 1:
            received = swap(message[0], 1)
            near = near + near_part(2, grad)
            pinned = near[-1]
        stride *= 2
        if stride == groups:
            conv_out, signal_grad, pinned = pl.pallas_call(
                functools.partial(finish_kernel, ranges),
                out_shape=[jax.ShapeDtypeStruct((tokens, channels), signal.dtype)] * 2 + [shaped(SUB, LANES)],
                in_specs=[WHOLE] * (4 + 2 * len(ranges)) + [UNREAD],
                out_specs=[HBM] * 2 + [WHOLE],
                scratch_shapes=[pltpu.VMEM((tokens, channels), signal.dtype)] * 2
                + [vmem(tokens, LANES), vmem(5, modes, LANES)]
                + [vmem(modes, channels)] * 2
                + [pltpu.SemaphoreType.DMA((2, tiles))],
                compiler_params=PARAMS,
                cost_estimate=cost(elements * modes * 600, 0, elements * 12),
                name="add_arrivals",
            )(residue, decay, carried, received, *near, grad)
        grad = pl.pallas_call(
            sum_kernel,
            out_shape=shaped(half, channels),
            in_specs=[WHOLE] * 2 + [UNREAD],
            name="sum_groups",
            **small,
        )(grad, other, pinned)
    residue_grad = pl.pallas_call(
        functools.partial(assemble_kernel, 1.0 / (tokens * n)),
        out_shape=shaped(modes, channels),
        name="assemble_gradient",
        **small,
    )(grad, swap(grad, 1))
    return conv_out, signal_grad, residue_grad


def solution(mesh):
    return jax.shard_map(
        body,
        mesh=mesh,
        in_specs=(P("ctx", "ch"), P("ctx", "ch"), P(), P()),
        out_specs=(P("ctx", "ch"), P("ctx", "ch"), P()),
        check_vma=False,
    )
```

```python
import functools

import jax
import jax.numpy as jnp
from jax import lax
from jax.experimental import pallas as pl
from jax.experimental.pallas import tpu as pltpu
from jax.sharding import PartitionSpec as P

SUB = 8
LANES = 128
F32 = jnp.float32


def row(ref, *index):
    return jnp.broadcast_to(ref[index], (SUB, LANES))


def token_order(tokens):
    rows = lax.broadcasted_iota(jnp.int32, (tokens, tokens), 0)
    columns = lax.broadcasted_iota(jnp.int32, (tokens, tokens), 1)
    wanted = lax.rem(rows, SUB) * (tokens // SUB) + lax.div(rows, SUB)
    return jnp.where(columns == wanted, 1.0, 0.0).astype(jnp.bfloat16)


def read_tokens(ref, chunks, lanes):
    return [[ref[pl.ds((p * SUB + r) * SUB, SUB), lanes] for r in range(SUB)] for p in range(chunks)]


def powers(decay, pw):
    pw[0] = jnp.exp(-decay)
    pw[1] = jnp.exp(-decay * SUB)


def horner(terms, factor):
    total = terms[0]
    for term in terms[1:]:
        total = total * factor + term
    return total


def chunk_states(m, xs, gs, pw):
    a, a8 = row(pw, 0, pl.ds(m, 1)), row(pw, 1, pl.ds(m, 1))
    chunks = len(xs)
    held, back = [], [None] * chunks
    for p in range(chunks):
        own = horner(xs[p], a)
        held.append(own if p == 0 else held[-1] * a8 + own)
    opens = [horner(gs[p][::-1], a) for p in range(chunks)]
    for p in reversed(range(chunks)):
        back[p] = opens[p] if p == chunks - 1 else back[p + 1] * a8 + opens[p]
    return held, back, opens


def by_span(scratch, half, j):
    return scratch[pl.ds(half * SUB * SUB + j, SUB, stride=SUB), :]


def gather_kernel(*refs):
    sources = refs[:4]
    xf, gf, residue_ref, decay_ref, segment, message, pw, ends, starts, inner, x_ref, g_ref, sems = refs[4:]
    staged = x_ref, g_ref, residue_ref, decay_ref
    copies = [pltpu.make_async_copy(*pair, sems.at[i]) for i, pair in enumerate(zip(sources, staged))]
    for copy in copies:
        copy.start()
    modes, channels = decay_ref.shape
    tokens = x_ref.shape[0]
    chunks = tokens // (SUB * SUB)
    span = chunks * SUB
    closing, opening, grad = (segment.at[pl.ds(i * modes, modes)] for i in range(3))
    order = token_order(tokens)
    for copy in copies:
        copy.wait()
    xf[...] = jnp.dot(order, x_ref[...], preferred_element_type=F32)
    gf[...] = jnp.dot(order, g_ref[...], preferred_element_type=F32)

    def tile_step(tile, _):
        lanes = pl.ds(pl.multiple_of(tile * LANES, LANES), LANES)
        decay = decay_ref[:, lanes]
        powers(decay, pw)
        xs, gs = read_tokens(xf, chunks, lanes), read_tokens(gf, chunks, lanes)
        for m in range(modes):
            held, back, opens = chunk_states(m, xs, gs, pw)
            rows = pl.ds(m * SUB, SUB)
            ends[rows, :] = held[-1]
            starts[rows, :] = back[0]
            inner[rows, :] = sum(opens[p] * held[p - 1] for p in range(1, chunks))
        lagged = []
        for lag in range(SUB):
            pairs = [gs[p][r] * xs[p][r - lag] for p in range(chunks) for r in range(lag, SUB)]
            lagged.append(jnp.sum(sum(pairs), axis=0, keepdims=True))
        for half in range(modes // SUB):
            some = pl.ds(half * SUB, SUB)
            a = pw[0, some, :]
            across = jnp.exp(-decay[half * SUB:(half + 1) * SUB] * span)
            arriving = jnp.zeros((SUB, LANES), F32)
            cross = jnp.zeros((SUB, LANES), F32)
            for j in range(SUB):
                cross = cross + (by_span(inner, half, j) + by_span(starts, half, j) * arriving)
                arriving = arriving * across + by_span(ends, half, j)
            leaving = horner([by_span(starts, half, j) for j in reversed(range(SUB))], across)
            near = horner([jnp.broadcast_to(v, (SUB, LANES)) for v in reversed(lagged)], a)
            closing[some, lanes] = arriving
            opening[some, lanes] = leaving
            grad[some, lanes] = near + a * cross
        return 0

    lax.fori_loop(0, channels // LANES, tile_step, 0)


    own_high = owns_high()
    half = modes // 2
    for i in range(3):
        low, high = segment[pl.ds(i * modes, half)], segment[pl.ds(i * modes + half, half)]
        message[pl.ds(i * half, half)] = jnp.where(own_high, low, high)


def on_second():
    return lax.rem(lax.axis_index("ctx"), 2) == 1


def owns_high():
    place, group = lax.axis_index("ctx"), lax.axis_index("ch")
    bits = place ^ group
    for shift in (16, 8, 4, 2, 1):
        bits = bits ^ lax.shift_right_logical(bits, jnp.int32(shift))
    return lax.rem(bits, 2) == 1


def own_half(high, values):
    half = values.shape[0] // 2
    return jnp.where(high, values[half:], values[:half])


def in_order(second, own, other):
    return jnp.where(second, other, own), jnp.where(second, own, other)


def local_kernel(tiles, xf, gf, residue_ref, decay_ref, _, out_ref, back_ref,
                 pw, ends, starts, before, after, arrive, leave):
    modes, channels = decay_ref.shape
    chunks = xf.shape[0] // (SUB * SUB)
    span = chunks * SUB

    def tile_step(tile, _):
        lanes = pl.ds(pl.multiple_of(tile * LANES, LANES), LANES)
        decay = decay_ref[:, lanes]
        residue = residue_ref[:, lanes]
        powers(decay, pw)
        pw[2] = residue * pw[0]
        xs, gs = read_tokens(xf, chunks, lanes), read_tokens(gf, chunks, lanes)
        for m in range(modes):
            held, back, _ = chunk_states(m, xs, gs, pw)
            rows = pl.ds(m * SUB, SUB)
            ends[rows, :] = held[-1]
            starts[rows, :] = back[0]
            for p in range(1, chunks):
                before[m, p - 1] = held[p - 1]
                after[m, p - 1] = back[p]
        for half in range(modes // SUB):
            across = jnp.exp(-decay[half * SUB:(half + 1) * SUB] * span)
            for target, source, order in ((arrive, ends, range(SUB)), (leave, starts, range(SUB - 1, -1, -1))):
                running = jnp.zeros((SUB, LANES), F32)
                for j in order:
                    target[pl.ds(half * SUB * SUB + j, SUB, stride=SUB), :] = running
                    running = running * across + by_span(source, half, j)
        taps = []
        weight = residue
        for lag in range(SUB):
            taps.append(jnp.broadcast_to(jnp.sum(weight, axis=0, keepdims=True), (SUB, LANES)))
            weight = weight * pw[0]
        for values, carried, inside, target, forward in (
            (xs, arrive, before, out_ref, True), (gs, leave, after, back_ref, False)
        ):
            order = range(SUB) if forward else range(SUB - 1, -1, -1)
            totals = []
            for p in range(chunks):
                seq = [values[p][r] for r in order]
                totals.append([sum(taps[lag] * seq[r - lag] for lag in range(r + 1)) for r in range(SUB)])
            for m in range(modes):
                a, a8, first = (row(pw, i, pl.ds(m, 1)) for i in range(3))
                edge = carried[pl.ds(m * SUB, SUB), :]
                for q in range(chunks):
                    p = q if forward else chunks - 1 - q
                    if q == 0:
                        state = edge
                    else:
                        edge = edge * a8
                        state = edge + inside[m, p - 1 if forward else p]
                    wave = state * first
                    for r in range(SUB):
                        totals[p][r] = totals[p][r] + wave
                        if r < SUB - 1:
                            wave = wave * a
            for p in range(chunks):
                for r, at in enumerate(order):
                    target[tile - tiles[0], p * SUB + at] = totals[p][r]
        return 0

    lax.fori_loop(tiles[0], tiles[1], tile_step, 0)


def join_chip_kernel(tokens, segment, other, decay_ref, _, joined, core):
    modes = decay_ref.shape[0]
    half = modes // 2
    high = owns_high()
    decay = own_half(high, decay_ref[...])
    mine = [own_half(high, segment[i * modes:(i + 1) * modes]) for i in range(3)]
    theirs = [other[i * half:(i + 1) * half] for i in range(3)]
    (close0, close1), (open0, open1), _ = (in_order(on_second(), a, b) for a, b in zip(mine, theirs))
    block = jnp.exp(decay * (-1.0 * tokens))
    joined[0:half] = block * close0 + close1
    joined[half:2 * half] = open0 + block * open1
    joined[2 * half:] = (mine[2] + theirs[2]) + jnp.exp(-decay) * open1 * close0
    core[0:half] = close0
    core[half:] = open1


def join_kernel(tokens, size, masks, last, *refs):
    count = len(masks)
    segments = refs[:count]
    core, decay_ref, carried, _ = refs[count:count + 4]
    *outs, ordered = refs[count + 4:]
    second = on_second()
    decay = own_half(owns_high(), decay_ref[...])
    half = decay.shape[0]
    chip = lax.div(lax.axis_index("ctx"), 2)
    place = lax.rem(lax.div(chip, size), count)
    for mask, segment in zip(masks, segments):
        ordered[place ^ mask] = segment[...]
    block = jnp.exp(decay * (-2.0 * size * tokens))
    zero = jnp.zeros_like(decay)
    close, cross, grad, incoming = zero, zero, zero, zero
    for k in range(count):
        grad = grad + ordered[k, 2 * half:]
        if k:
            cross = cross + ordered[k, half:2 * half] * close
            incoming = jnp.where(place == k, close, incoming)
        close = close * block + ordered[k, 0:half]
    begin, outgoing = zero, zero
    for k in reversed(range(count)):
        outgoing = jnp.where(place == k, begin, outgoing)
        begin = begin * block + ordered[k, half:2 * half]
    grad = grad + jnp.exp(-decay) * cross
    if size > 1:
        inside = lax.rem(chip, size)
        incoming = carried[0:half] + incoming * jnp.exp(decay * (inside * (-2 * tokens)).astype(F32))
        outgoing = carried[half:] + outgoing * jnp.exp(decay * ((size - 1 - inside) * (-2 * tokens)).astype(F32))
    if not last:
        joined, arrivals = outs
        joined[0:half] = close
        joined[half:2 * half] = begin
        joined[2 * half:] = grad
        arrivals[0:half] = incoming
        arrivals[half:] = outgoing
        return
    total, own, message = outs
    total[...] = grad
    block = jnp.exp(decay * (-1.0 * tokens))
    into = incoming, block * incoming + core[0:half]
    out = block * outgoing + core[half:], outgoing
    own[0:half] = jnp.where(second, into[1], into[0])
    own[half:] = jnp.where(second, out[1], out[0])
    message[0:half] = jnp.where(second, into[0], into[1])
    message[half:] = jnp.where(second, out[0], out[1])


def finish_kernel(ranges, residue_ref, decay_ref, own, other, *refs):
    near = refs[:2 * len(ranges)]
    _, out_hbm, back_hbm, finished, out_ref, back_ref, result, pw, arrive, leave, sems = refs[2 * len(ranges):]
    modes, channels = decay_ref.shape
    half = modes // 2
    chunks = near[0].shape[1] // SUB
    span = chunks * SUB
    own_high = owns_high()
    first = residue_ref[...] * jnp.exp(-decay_ref[...])
    for target, rows in ((arrive, slice(0, half)), (leave, slice(half, modes))):
        low, high = in_order(own_high, own[rows], other[rows])
        target[0:half] = low * first[0:half]
        target[half:] = high * first[half:]

    def copy_out(tile, which):
        lanes = pl.ds(pl.multiple_of(tile * LANES, LANES), LANES)
        source, target = ((out_ref, out_hbm), (back_ref, back_hbm))[which]
        return pltpu.make_async_copy(source.at[:, lanes], target.at[:, lanes], sems.at[which, tile])

    def run(tiles, near_out, near_back):
        def tile_step(tile, _):
            lanes = pl.ds(pl.multiple_of(tile * LANES, LANES), LANES)
            decay = decay_ref[:, lanes]
            powers(decay, pw)
            pw[2] = decay * (-1.0 * span)
            pw[3] = arrive[:, lanes]
            pw[4] = leave[:, lanes]
            level = lax.broadcasted_iota(jnp.int32, (SUB, LANES), 0).astype(F32)
            for near, target, forward in ((near_out, out_ref, True), (near_back, back_ref, False)):
                order = range(SUB) if forward else range(SUB - 1, -1, -1)
                spans = level if forward else SUB - 1.0 - level
                totals = [[near[tile - tiles[0], p * SUB + r] for r in range(SUB)] for p in range(chunks)]
                for m in range(modes):
                    a, a8, rate = (row(pw, i, pl.ds(m, 1)) for i in range(3))
                    state = row(pw, 3 if forward else 4, pl.ds(m, 1)) * jnp.exp(rate * spans)
                    for q in range(chunks):
                        p = q if forward else chunks - 1 - q
                        wave = state
                        for r in order:
                            totals[p][r] = totals[p][r] + wave
                            wave = wave * a
                        if q < chunks - 1:
                            state = state * a8
                for p in range(chunks):
                    for r in range(SUB):
                        result[pl.ds(p * SUB + r, SUB, stride=span), :] = totals[p][r]
                target[:, lanes] = result[...].astype(target.dtype)
                copy_out(tile, 0 if forward else 1).start()
            return 0

        lax.fori_loop(tiles[0], tiles[1], tile_step, 0)

    for part, tiles in enumerate(ranges):
        run(tiles, near[2 * part], near[2 * part + 1])
    for tile in range(channels // LANES):
        for which in range(2):
            copy_out(tile, which).wait()
    finished[...] = jnp.zeros(finished.shape, F32)


def sum_kernel(own, other, _, out_ref):
    out_ref[...] = own[...] + other[...]


def assemble_kernel(scale, own, other, out_ref):
    half = own.shape[0]
    low, high = in_order(owns_high(), own[...], other[...])
    out_ref[0:half] = low * scale
    out_ref[half:] = high * scale


def vmem(*shape):
    return pltpu.VMEM(shape, F32)


def shaped(*shape):
    return jax.ShapeDtypeStruct(shape, F32)


def cost(flops, transcendentals, nbytes):
    return pl.CostEstimate(flops=flops, transcendentals=transcendentals, bytes_accessed=nbytes)


PARAMS = pltpu.CompilerParams(vmem_limit_bytes=32 * 1024 * 1024)
WHOLE = pl.BlockSpec(memory_space=pltpu.VMEM)
HBM = pl.BlockSpec(memory_space=pltpu.HBM)


UNREAD = pl.BlockSpec(memory_space=pl.ANY)


def body(signal, cotangent, residue, decay):
    tokens, channels = signal.shape
    modes = decay.shape[0]
    half = modes // 2
    n, groups = lax.axis_size("ctx"), lax.axis_size("ch")
    chunks = tokens // (SUB * SUB)
    elements = tokens * channels
    spans = vmem(modes * SUB, LANES)
    tiles = channels // LANES
    quarter = tiles // 4
    ranges = [(0, quarter), (quarter, 3 * quarter), (3 * quarter, tiles)]
    small = dict(compiler_params=PARAMS, cost_estimate=cost(elements, modes * channels, modes * channels * 32))

    def swap(x, ctx_mask, ch_mask=0):
        if ctx_mask != 1:
            ctx_mask |= (ctx_mask.bit_count() + ch_mask.bit_count()) % 2
        mask = ctx_mask * groups + ch_mask
        return lax.ppermute(x, ("ctx", "ch"), [(i, i ^ mask) for i in range(n * groups)])

    def near_part(part, after):
        first, last = ranges[part]
        share = elements * modes * (last - first) // tiles
        return pl.pallas_call(
            functools.partial(local_kernel, ranges[part]),
            out_shape=[shaped(last - first, chunks * SUB, SUB, LANES)] * 2,
            in_specs=[WHOLE] * 4 + [UNREAD],
            scratch_shapes=[vmem(3, modes, LANES), spans, spans]
            + [vmem(modes, chunks - 1, SUB, LANES)] * 2
            + [spans, spans],
            compiler_params=PARAMS,
            cost_estimate=cost(share * 400, 0, share),
            name="local_convolutions",
        )(*inputs, after)

    values = shaped(tokens, channels)
    *inputs, segment, message = pl.pallas_call(
        gather_kernel,
        out_shape=[values, values]
        + [shaped(modes, channels)] * 2
        + [shaped(3 * modes, channels), shaped(3 * half, channels)],
        in_specs=[HBM] * 4,
        scratch_shapes=[vmem(2, modes, LANES), spans, spans, spans]
        + [pltpu.VMEM(signal.shape, signal.dtype)] * 2
        + [pltpu.SemaphoreType.DMA((4,))],
        compiler_params=PARAMS,
        cost_estimate=cost(elements * modes * 5, modes * channels * 3, elements * 6),
        name="block_states",
    )(*(pltpu.with_memory_space_constraint(a, pltpu.HBM) for a in (signal, cotangent, residue, decay)))
    residue, decay = inputs[2:]

    other = swap(message, 1)
    near = near_part(0, segment)
    joined, core = pl.pallas_call(
        functools.partial(join_chip_kernel, tokens),
        out_shape=[shaped(3 * half, channels), shaped(2 * half, channels)],
        in_specs=[WHOLE] * 3 + [UNREAD],
        name="join_chip",
        **small,
    )(segment, other, decay, near[0])

    chips = n // 2
    size = 1
    carried = core
    while size < chips:
        count = min(4, chips // size)
        last = size * count == chips
        masks = [3, 1, 2] if count == 4 else [1]
        others = [swap(joined, 2 * size * m) for m in masks]
        if last:
            near = near + near_part(1, joined)
        rows = [half, 2 * half, 2 * half] if last else [3 * half, 2 * half]
        joined, carried, *message = pl.pallas_call(
            functools.partial(join_kernel, tokens, size, [0] + masks, last),
            out_shape=[shaped(r, channels) for r in rows],
            in_specs=[WHOLE] * (count + 3) + [UNREAD],
            scratch_shapes=[vmem(count, 3 * half, channels)],
            name="join_chips",
            **small,
        )(joined, *others, core, decay, carried, near[-1])
        size *= count

    grad = joined
    stride = 1
    while stride < groups:
        other = swap(grad, 0, stride)
        if stride == 1:
            received = swap(message[0], 1)
            near = near + near_part(2, grad)
            pinned = near[-1]
        stride *= 2
        if stride == groups:
            conv_out, signal_grad, pinned = pl.pallas_call(
                functools.partial(finish_kernel, ranges),
                out_shape=[jax.ShapeDtypeStruct((tokens, channels), signal.dtype)] * 2 + [shaped(SUB, LANES)],
                in_specs=[WHOLE] * (4 + 2 * len(ranges)) + [UNREAD],
                out_specs=[HBM] * 2 + [WHOLE],
                scratch_shapes=[pltpu.VMEM((tokens, channels), signal.dtype)] * 2
                + [vmem(tokens, LANES), vmem(5, modes, LANES)]
                + [vmem(modes, channels)] * 2
                + [pltpu.SemaphoreType.DMA((2, tiles))],
                compiler_params=PARAMS,
                cost_estimate=cost(elements * modes * 600, 0, elements * 12),
                name="add_arrivals",
            )(residue, decay, carried, received, *near, grad)
        grad = pl.pallas_call(
            sum_kernel,
            out_shape=shaped(half, channels),
            in_specs=[WHOLE] * 2 + [UNREAD],
            name="sum_groups",
            **small,
        )(grad, other, pinned)
    residue_grad = pl.pallas_call(
        functools.partial(assemble_kernel, 1.0 / (tokens * n)),
        out_shape=shaped(modes, channels),
        name="assemble_gradient",
        **small,
    )(grad, swap(grad, 1))
    return conv_out, signal_grad, residue_grad


def solution(mesh):
    return jax.shard_map(
        body,
        mesh=mesh,
        in_specs=(P("ctx", "ch"), P("ctx", "ch"), P(), P()),
        out_specs=(P("ctx", "ch"), P("ctx", "ch"), P()),
        check_vma=False,
    )
```

```python
import functools

import jax
import jax.numpy as jnp
from jax import lax
from jax.experimental import pallas as pl
from jax.experimental.pallas import tpu as pltpu
from jax.sharding import PartitionSpec as P

SUB = 8
LANES = 128
F32 = jnp.float32


def row(ref, *index):
    return jnp.broadcast_to(ref[index], (SUB, LANES))


def token_order(tokens):
    rows = lax.broadcasted_iota(jnp.int32, (tokens, tokens), 0)
    columns = lax.broadcasted_iota(jnp.int32, (tokens, tokens), 1)
    wanted = lax.rem(rows, SUB) * (tokens // SUB) + lax.div(rows, SUB)
    return jnp.where(columns == wanted, 1.0, 0.0).astype(jnp.bfloat16)


def read_chunk(ref, p, lanes):
    return [ref[pl.ds((p * SUB + r) * SUB, SUB), lanes] for r in range(SUB)]


def read_tokens(ref, chunks, lanes):
    return [read_chunk(ref, p, lanes) for p in range(chunks)]


def powers(decay, pw):
    pw[0] = jnp.exp(-decay)
    pw[1] = jnp.exp(-decay * SUB)


def horner(terms, factor):
    total = terms[0]
    for term in terms[1:]:
        total = total * factor + term
    return total


def held_states(m, xs, pw):
    a, a8 = row(pw, 0, pl.ds(m, 1)), row(pw, 1, pl.ds(m, 1))
    held = []
    for chunk in xs:
        own = horner(chunk, a)
        held.append(held[-1] * a8 + own if held else own)
    return held


def back_states(m, gs, pw):
    a, a8 = row(pw, 0, pl.ds(m, 1)), row(pw, 1, pl.ds(m, 1))
    opens = [horner(chunk[::-1], a) for chunk in gs]
    back = opens[-1:]
    for own in reversed(opens[:-1]):
        back.insert(0, back[0] * a8 + own)
    return back, opens


def by_span(scratch, half, j):
    return scratch[pl.ds(half * SUB * SUB + j, SUB, stride=SUB), :]


def gather_kernel(*refs):
    sources = refs[:4]
    xf, gf, residue_ref, decay_ref, segment, message, *scratch, x_ref, g_ref, sems = refs[4:]
    staged = x_ref, g_ref, residue_ref, decay_ref
    copies = [pltpu.make_async_copy(*pair, sems.at[i]) for i, pair in enumerate(zip(sources, staged))]
    for copy in copies:
        copy.start()
    modes, channels = decay_ref.shape
    tokens = x_ref.shape[0]
    chunks = tokens // (SUB * SUB)
    span = chunks * SUB
    closing, opening, grad = (segment.at[pl.ds(i * modes, modes)] for i in range(3))
    order = token_order(tokens)
    for copy in copies:
        copy.wait()
    xf[...] = jnp.dot(order, x_ref[...], preferred_element_type=F32)
    gf[...] = jnp.dot(order, g_ref[...], preferred_element_type=F32)

    def tile_step(tile):
        lanes = pl.ds(tile * LANES, LANES)
        pw, ends, starts, inner, before = (ref.at[tile % 2] for ref in scratch)
        decay = decay_ref[:, lanes]
        powers(decay, pw)
        xs = read_tokens(xf, chunks, lanes)
        for m in range(modes):
            held = held_states(m, xs, pw)
            ends[pl.ds(m * SUB, SUB), :] = held[-1]
            for p in range(chunks - 1):
                before[m, p] = held[p]
        gs = read_tokens(gf, chunks, lanes)
        for m in range(modes):
            back, opens = back_states(m, gs, pw)
            rows = pl.ds(m * SUB, SUB)
            starts[rows, :] = back[0]
            inner[rows, :] = sum(opens[p] * before[m, p - 1] for p in range(1, chunks))
        lagged = [0.0] * SUB
        for p in range(chunks):
            xs, gs = read_chunk(xf, p, lanes), read_chunk(gf, p, lanes)
            for lag in range(SUB):
                lagged[lag] = lagged[lag] + sum(gs[r] * xs[r - lag] for r in range(lag, SUB))
        lagged = [jnp.sum(total, axis=0, keepdims=True) for total in lagged]
        for half in range(modes // SUB):
            some = pl.ds(half * SUB, SUB)
            a = pw[0, some, :]
            across = jnp.exp(-decay[half * SUB:(half + 1) * SUB] * span)
            arriving = jnp.zeros((SUB, LANES), F32)
            cross = jnp.zeros((SUB, LANES), F32)
            for j in range(SUB):
                cross = cross + (by_span(inner, half, j) + by_span(starts, half, j) * arriving)
                arriving = arriving * across + by_span(ends, half, j)
            leaving = horner([by_span(starts, half, j) for j in reversed(range(SUB))], across)
            near = horner([jnp.broadcast_to(v, (SUB, LANES)) for v in reversed(lagged)], a)
            closing[some, lanes] = arriving
            opening[some, lanes] = leaving
            grad[some, lanes] = near + a * cross

    for tile in range(channels // LANES):
        tile_step(tile)

    own_high = owns_high()
    half = modes // 2
    for i in range(3):
        low, high = segment[pl.ds(i * modes, half)], segment[pl.ds(i * modes + half, half)]
        message[pl.ds(i * half, half)] = jnp.where(own_high, low, high)


def on_second():
    return lax.rem(lax.axis_index("ctx"), 2) == 1


def owns_high():
    place, group = lax.axis_index("ctx"), lax.axis_index("ch")
    bits = place ^ group
    for shift in (16, 8, 4, 2, 1):
        bits = bits ^ lax.shift_right_logical(bits, jnp.int32(shift))
    return lax.rem(bits, 2) == 1


def own_half(high, values):
    half = values.shape[0] // 2
    return jnp.where(high, values[half:], values[:half])


def in_order(second, own, other):
    return jnp.where(second, other, own), jnp.where(second, own, other)


def local_kernel(tiles, xf, gf, residue_ref, decay_ref, _, out_ref, back_ref,
                 pw, ends, starts, before, after, arrive, leave):
    modes, channels = decay_ref.shape
    chunks = xf.shape[0] // (SUB * SUB)
    span = chunks * SUB

    def tile_step(tile, _):
        lanes = pl.ds(pl.multiple_of(tile * LANES, LANES), LANES)
        decay = decay_ref[:, lanes]
        residue = residue_ref[:, lanes]
        powers(decay, pw)
        pw[2] = residue * pw[0]
        xs, gs = read_tokens(xf, chunks, lanes), read_tokens(gf, chunks, lanes)
        for m in range(modes):
            held, (back, _) = held_states(m, xs, pw), back_states(m, gs, pw)
            rows = pl.ds(m * SUB, SUB)
            ends[rows, :] = held[-1]
            starts[rows, :] = back[0]
            for p in range(1, chunks):
                before[m, p - 1] = held[p - 1]
                after[m, p - 1] = back[p]
        for half in range(modes // SUB):
            across = jnp.exp(-decay[half * SUB:(half + 1) * SUB] * span)
            for target, source, order in ((arrive, ends, range(SUB)), (leave, starts, range(SUB - 1, -1, -1))):
                running = jnp.zeros((SUB, LANES), F32)
                for j in order:
                    target[pl.ds(half * SUB * SUB + j, SUB, stride=SUB), :] = running
                    running = running * across + by_span(source, half, j)
        taps = []
        weight = residue
        for lag in range(SUB):
            taps.append(jnp.broadcast_to(jnp.sum(weight, axis=0, keepdims=True), (SUB, LANES)))
            weight = weight * pw[0]
        for values, carried, inside, target, forward in (
            (xs, arrive, before, out_ref, True), (gs, leave, after, back_ref, False)
        ):
            order = range(SUB) if forward else range(SUB - 1, -1, -1)
            totals = []
            for p in range(chunks):
                seq = [values[p][r] for r in order]
                totals.append([sum(taps[lag] * seq[r - lag] for lag in range(r + 1)) for r in range(SUB)])
            for m in range(modes):
                a, a8, first = (row(pw, i, pl.ds(m, 1)) for i in range(3))
                edge = carried[pl.ds(m * SUB, SUB), :]
                for q in range(chunks):
                    p = q if forward else chunks - 1 - q
                    if q == 0:
                        state = edge
                    else:
                        edge = edge * a8
                        state = edge + inside[m, p - 1 if forward else p]
                    wave = state * first
                    for r in range(SUB):
                        totals[p][r] = totals[p][r] + wave
                        if r < SUB - 1:
                            wave = wave * a
            for p in range(chunks):
                for r, at in enumerate(order):
                    target[tile - tiles[0], p * SUB + at] = totals[p][r]
        return 0

    lax.fori_loop(tiles[0], tiles[1], tile_step, 0)


def join_chip_kernel(tokens, segment, other, decay_ref, _, joined, core):
    modes = decay_ref.shape[0]
    half = modes // 2
    high = owns_high()
    decay = own_half(high, decay_ref[...])
    mine = [own_half(high, segment[i * modes:(i + 1) * modes]) for i in range(3)]
    theirs = [other[i * half:(i + 1) * half] for i in range(3)]
    (close0, close1), (open0, open1), _ = (in_order(on_second(), a, b) for a, b in zip(mine, theirs))
    block = jnp.exp(decay * (-1.0 * tokens))
    joined[0:half] = block * close0 + close1
    joined[half:2 * half] = open0 + block * open1
    joined[2 * half:] = (mine[2] + theirs[2]) + jnp.exp(-decay) * open1 * close0
    core[0:half] = close0
    core[half:] = open1


def join_kernel(tokens, size, masks, last, *refs):
    count = len(masks)
    segments = refs[:count]
    core, decay_ref, carried, _ = refs[count:count + 4]
    *outs, ordered = refs[count + 4:]
    second = on_second()
    decay = own_half(owns_high(), decay_ref[...])
    half = decay.shape[0]
    chip = lax.div(lax.axis_index("ctx"), 2)
    place = lax.rem(lax.div(chip, size), count)
    for mask, segment in zip(masks, segments):
        ordered[place ^ mask] = segment[...]
    block = jnp.exp(decay * (-2.0 * size * tokens))
    zero = jnp.zeros_like(decay)
    close, cross, grad, incoming = zero, zero, zero, zero
    for k in range(count):
        grad = grad + ordered[k, 2 * half:]
        if k:
            cross = cross + ordered[k, half:2 * half] * close
            incoming = jnp.where(place == k, close, incoming)
        close = close * block + ordered[k, 0:half]
    begin, outgoing = zero, zero
    for k in reversed(range(count)):
        outgoing = jnp.where(place == k, begin, outgoing)
        begin = begin * block + ordered[k, half:2 * half]
    grad = grad + jnp.exp(-decay) * cross
    if size > 1:
        inside = lax.rem(chip, size)
        incoming = carried[0:half] + incoming * jnp.exp(decay * (inside * (-2 * tokens)).astype(F32))
        outgoing = carried[half:] + outgoing * jnp.exp(decay * ((size - 1 - inside) * (-2 * tokens)).astype(F32))
    if not last:
        joined, arrivals = outs
        joined[0:half] = close
        joined[half:2 * half] = begin
        joined[2 * half:] = grad
        arrivals[0:half] = incoming
        arrivals[half:] = outgoing
        return
    total, own, message = outs
    total[...] = grad
    block = jnp.exp(decay * (-1.0 * tokens))
    into = incoming, block * incoming + core[0:half]
    out = block * outgoing + core[half:], outgoing
    own[0:half] = jnp.where(second, into[1], into[0])
    own[half:] = jnp.where(second, out[1], out[0])
    message[0:half] = jnp.where(second, into[0], into[1])
    message[half:] = jnp.where(second, out[0], out[1])


def finish_kernel(ranges, residue_ref, decay_ref, own, other, *refs):
    near = refs[:2 * len(ranges)]
    _, out_hbm, back_hbm, finished, out_ref, back_ref, result, pw, arrive, leave, sems = refs[2 * len(ranges):]
    modes, channels = decay_ref.shape
    half = modes // 2
    chunks = near[0].shape[1] // SUB
    span = chunks * SUB
    own_high = owns_high()
    first = residue_ref[...] * jnp.exp(-decay_ref[...])
    for target, rows in ((arrive, slice(0, half)), (leave, slice(half, modes))):
        low, high = in_order(own_high, own[rows], other[rows])
        target[0:half] = low * first[0:half]
        target[half:] = high * first[half:]

    def copy_out(tile, which):
        lanes = pl.ds(pl.multiple_of(tile * LANES, LANES), LANES)
        source, target = ((out_ref, out_hbm), (back_ref, back_hbm))[which]
        return pltpu.make_async_copy(source.at[:, lanes], target.at[:, lanes], sems.at[which, tile])

    def run(tiles, near_out, near_back):
        def tile_step(tile, _):
            lanes = pl.ds(pl.multiple_of(tile * LANES, LANES), LANES)
            decay = decay_ref[:, lanes]
            powers(decay, pw)
            pw[2] = decay * (-1.0 * span)
            pw[3] = arrive[:, lanes]
            pw[4] = leave[:, lanes]
            level = lax.broadcasted_iota(jnp.int32, (SUB, LANES), 0).astype(F32)
            for near, target, forward in ((near_out, out_ref, True), (near_back, back_ref, False)):
                order = range(SUB) if forward else range(SUB - 1, -1, -1)
                spans = level if forward else SUB - 1.0 - level
                totals = [[near[tile - tiles[0], p * SUB + r] for r in range(SUB)] for p in range(chunks)]
                for m in range(modes):
                    a, a8, rate = (row(pw, i, pl.ds(m, 1)) for i in range(3))
                    state = row(pw, 3 if forward else 4, pl.ds(m, 1)) * jnp.exp(rate * spans)
                    for q in range(chunks):
                        p = q if forward else chunks - 1 - q
                        wave = state
                        for r in order:
                            totals[p][r] = totals[p][r] + wave
                            wave = wave * a
                        if q < chunks - 1:
                            state = state * a8
                for p in range(chunks):
                    for r in range(SUB):
                        result[pl.ds(p * SUB + r, SUB, stride=span), :] = totals[p][r]
                target[:, lanes] = result[...].astype(target.dtype)
                copy_out(tile, 0 if forward else 1).start()
            return 0

        lax.fori_loop(tiles[0], tiles[1], tile_step, 0)

    for part, tiles in enumerate(ranges):
        run(tiles, near[2 * part], near[2 * part + 1])
    for tile in range(channels // LANES):
        for which in range(2):
            copy_out(tile, which).wait()
    finished[...] = jnp.zeros(finished.shape, F32)


def sum_kernel(own, other, _, out_ref):
    out_ref[...] = own[...] + other[...]


def assemble_kernel(scale, own, other, out_ref):
    half = own.shape[0]
    low, high = in_order(owns_high(), own[...], other[...])
    out_ref[0:half] = low * scale
    out_ref[half:] = high * scale


def vmem(*shape):
    return pltpu.VMEM(shape, F32)


def shaped(*shape):
    return jax.ShapeDtypeStruct(shape, F32)


def cost(flops, transcendentals, nbytes):
    return pl.CostEstimate(flops=flops, transcendentals=transcendentals, bytes_accessed=nbytes)


PARAMS = pltpu.CompilerParams(vmem_limit_bytes=32 * 1024 * 1024)
WHOLE = pl.BlockSpec(memory_space=pltpu.VMEM)
HBM = pl.BlockSpec(memory_space=pltpu.HBM)


UNREAD = pl.BlockSpec(memory_space=pl.ANY)


def body(signal, cotangent, residue, decay):
    tokens, channels = signal.shape
    modes = decay.shape[0]
    half = modes // 2
    n, groups = lax.axis_size("ctx"), lax.axis_size("ch")
    chunks = tokens // (SUB * SUB)
    elements = tokens * channels
    spans = vmem(modes * SUB, LANES)
    tiles = channels // LANES
    quarter = tiles // 4
    ranges = [(0, quarter), (quarter, 3 * quarter), (3 * quarter, tiles)]
    small = dict(compiler_params=PARAMS, cost_estimate=cost(elements, modes * channels, modes * channels * 32))

    def swap(x, ctx_mask, ch_mask=0):
        if ctx_mask != 1:
            ctx_mask |= (ctx_mask.bit_count() + ch_mask.bit_count()) % 2
        mask = ctx_mask * groups + ch_mask
        return lax.ppermute(x, ("ctx", "ch"), [(i, i ^ mask) for i in range(n * groups)])

    def near_part(part, after):
        first, last = ranges[part]
        share = elements * modes * (last - first) // tiles
        return pl.pallas_call(
            functools.partial(local_kernel, ranges[part]),
            out_shape=[shaped(last - first, chunks * SUB, SUB, LANES)] * 2,
            in_specs=[WHOLE] * 4 + [UNREAD],
            scratch_shapes=[vmem(3, modes, LANES), spans, spans]
            + [vmem(modes, chunks - 1, SUB, LANES)] * 2
            + [spans, spans],
            compiler_params=PARAMS,
            cost_estimate=cost(share * 400, 0, share),
            name="local_convolutions",
        )(*inputs, after)

    values = shaped(tokens, channels)
    *inputs, segment, message = pl.pallas_call(
        gather_kernel,
        out_shape=[values, values]
        + [shaped(modes, channels)] * 2
        + [shaped(3 * modes, channels), shaped(3 * half, channels)],
        in_specs=[HBM] * 4,
        scratch_shapes=[vmem(2, 2, modes, LANES)]
        + [vmem(2, modes * SUB, LANES)] * 3
        + [vmem(2, modes, chunks - 1, SUB, LANES)]
        + [pltpu.VMEM(signal.shape, signal.dtype)] * 2
        + [pltpu.SemaphoreType.DMA((4,))],
        compiler_params=PARAMS,
        cost_estimate=cost(elements * modes * 5, modes * channels * 3, elements * 6),
        name="block_states",
    )(*(pltpu.with_memory_space_constraint(a, pltpu.HBM) for a in (signal, cotangent, residue, decay)))
    residue, decay = inputs[2:]

    other = swap(message, 1)
    near = near_part(0, segment)
    joined, core = pl.pallas_call(
        functools.partial(join_chip_kernel, tokens),
        out_shape=[shaped(3 * half, channels), shaped(2 * half, channels)],
        in_specs=[WHOLE] * 3 + [UNREAD],
        name="join_chip",
        **small,
    )(segment, other, decay, near[0])

    chips = n // 2
    size = 1
    carried = core
    while size < chips:
        count = min(4, chips // size)
        last = size * count == chips
        masks = [3, 1, 2] if count == 4 else [1]
        others = [swap(joined, 2 * size * m) for m in masks]
        if last:
            near = near + near_part(1, joined)
        rows = [half, 2 * half, 2 * half] if last else [3 * half, 2 * half]
        joined, carried, *message = pl.pallas_call(
            functools.partial(join_kernel, tokens, size, [0] + masks, last),
            out_shape=[shaped(r, channels) for r in rows],
            in_specs=[WHOLE] * (count + 3) + [UNREAD],
            scratch_shapes=[vmem(count, 3 * half, channels)],
            name="join_chips",
            **small,
        )(joined, *others, core, decay, carried, near[-1])
        size *= count

    grad = joined
    stride = 1
    while stride < groups:
        other = swap(grad, 0, stride)
        if stride == 1:
            received = swap(message[0], 1)
            near = near + near_part(2, grad)
            pinned = near[-1]
        stride *= 2
        if stride == groups:
            conv_out, signal_grad, pinned = pl.pallas_call(
                functools.partial(finish_kernel, ranges),
                out_shape=[jax.ShapeDtypeStruct((tokens, channels), signal.dtype)] * 2 + [shaped(SUB, LANES)],
                in_specs=[WHOLE] * (4 + 2 * len(ranges)) + [UNREAD],
                out_specs=[HBM] * 2 + [WHOLE],
                scratch_shapes=[pltpu.VMEM((tokens, channels), signal.dtype)] * 2
                + [vmem(tokens, LANES), vmem(5, modes, LANES)]
                + [vmem(modes, channels)] * 2
                + [pltpu.SemaphoreType.DMA((2, tiles))],
                compiler_params=PARAMS,
                cost_estimate=cost(elements * modes * 600, 0, elements * 12),
                name="add_arrivals",
            )(residue, decay, carried, received, *near, grad)
        grad = pl.pallas_call(
            sum_kernel,
            out_shape=shaped(half, channels),
            in_specs=[WHOLE] * 2 + [UNREAD],
            name="sum_groups",
            **small,
        )(grad, other, pinned)
    residue_grad = pl.pallas_call(
        functools.partial(assemble_kernel, 1.0 / (tokens * n)),
        out_shape=shaped(modes, channels),
        name="assemble_gradient",
        **small,
    )(grad, swap(grad, 1))
    return conv_out, signal_grad, residue_grad


def solution(mesh):
    return jax.shard_map(
        body,
        mesh=mesh,
        in_specs=(P("ctx", "ch"), P("ctx", "ch"), P(), P()),
        out_specs=(P("ctx", "ch"), P("ctx", "ch"), P()),
        check_vma=False,
    )
```

```python
import functools

import jax
import jax.numpy as jnp
from jax import lax
from jax.experimental import pallas as pl
from jax.experimental.pallas import tpu as pltpu
from jax.sharding import PartitionSpec as P

SUB = 8
LANES = 128
F32 = jnp.float32


def row(ref, *index):
    return jnp.broadcast_to(ref[index], (SUB, LANES))


def token_order(tokens):
    rows = lax.broadcasted_iota(jnp.int32, (tokens, tokens), 0)
    columns = lax.broadcasted_iota(jnp.int32, (tokens, tokens), 1)
    wanted = lax.rem(rows, SUB) * (tokens // SUB) + lax.div(rows, SUB)
    return jnp.where(columns == wanted, 1.0, 0.0).astype(jnp.bfloat16)


def read_chunk(ref, p, lanes):
    return [ref[pl.ds((p * SUB + r) * SUB, SUB), lanes] for r in range(SUB)]


def read_tokens(ref, chunks, lanes):
    return [read_chunk(ref, p, lanes) for p in range(chunks)]


def powers(decay, pw):
    pw[0] = jnp.exp(-decay)
    pw[1] = jnp.exp(-decay * SUB)


def horner(terms, factor):
    total = terms[0]
    for term in terms[1:]:
        total = total * factor + term
    return total


def held_states(m, xs, pw):
    a, a8 = row(pw, 0, pl.ds(m, 1)), row(pw, 1, pl.ds(m, 1))
    held = []
    for chunk in xs:
        own = horner(chunk, a)
        held.append(held[-1] * a8 + own if held else own)
    return held


def back_states(m, gs, pw):
    a, a8 = row(pw, 0, pl.ds(m, 1)), row(pw, 1, pl.ds(m, 1))
    opens = [horner(chunk[::-1], a) for chunk in gs]
    back = opens[-1:]
    for own in reversed(opens[:-1]):
        back.insert(0, back[0] * a8 + own)
    return back, opens


def by_span(scratch, half, j):
    return scratch[pl.ds(half * SUB * SUB + j, SUB, stride=SUB), :]


def gather_kernel(x_hbm, g_hbm, residue_hbm, decay_hbm, *refs):
    xf, gf, residue_ref, decay_ref, segment, message, *scratch, x_ref, g_ref, sems = refs
    modes, channels = decay_ref.shape
    tokens = x_ref.shape[0]
    chunks = tokens // (SUB * SUB)
    span = chunks * SUB
    tiles = channels // LANES
    groups = [slice(0, channels // 2), slice(channels // 2, channels)]
    pairs = [(decay_hbm, decay_ref)]
    for lanes in groups:
        pairs += [(x_hbm.at[:, lanes], x_ref.at[:, lanes]), (g_hbm.at[:, lanes], g_ref.at[:, lanes])]
    pairs.append((residue_hbm, residue_ref))
    copies = [pltpu.make_async_copy(*pair, sems.at[i]) for i, pair in enumerate(pairs)]
    for copy in copies:
        copy.start()
    closing, opening, grad = (segment.at[pl.ds(i * modes, modes)] for i in range(3))
    order = token_order(tokens)
    copies[0].wait()

    def tile_step(tile):
        lanes = pl.ds(tile * LANES, LANES)
        pw, ends, starts, inner, before = (ref.at[tile % 2] for ref in scratch)
        decay = decay_ref[:, lanes]
        powers(decay, pw)
        xs = read_tokens(xf, chunks, lanes)
        for m in range(modes):
            held = held_states(m, xs, pw)
            ends[pl.ds(m * SUB, SUB), :] = held[-1]
            for p in range(chunks - 1):
                before[m, p] = held[p]
        gs = read_tokens(gf, chunks, lanes)
        for m in range(modes):
            back, opens = back_states(m, gs, pw)
            rows = pl.ds(m * SUB, SUB)
            starts[rows, :] = back[0]
            inner[rows, :] = sum(opens[p] * before[m, p - 1] for p in range(1, chunks))
        lagged = [0.0] * SUB
        for p in range(chunks):
            xs, gs = read_chunk(xf, p, lanes), read_chunk(gf, p, lanes)
            for lag in range(SUB):
                lagged[lag] = lagged[lag] + sum(gs[r] * xs[r - lag] for r in range(lag, SUB))
        lagged = [jnp.sum(total, axis=0, keepdims=True) for total in lagged]
        for half in range(modes // SUB):
            some = pl.ds(half * SUB, SUB)
            a = pw[0, some, :]
            across = jnp.exp(-decay[half * SUB:(half + 1) * SUB] * span)
            arriving = jnp.zeros((SUB, LANES), F32)
            cross = jnp.zeros((SUB, LANES), F32)
            for j in range(SUB):
                cross = cross + (by_span(inner, half, j) + by_span(starts, half, j) * arriving)
                arriving = arriving * across + by_span(ends, half, j)
            leaving = horner([by_span(starts, half, j) for j in reversed(range(SUB))], across)
            near = horner([jnp.broadcast_to(v, (SUB, LANES)) for v in reversed(lagged)], a)
            closing[some, lanes] = arriving
            opening[some, lanes] = leaving
            grad[some, lanes] = near + a * cross

    for which, lanes in enumerate(groups):
        for copy, source, target in zip(copies[1 + 2 * which:], (x_ref, g_ref), (xf, gf)):
            copy.wait()
            target[:, lanes] = jnp.dot(order, source[:, lanes], preferred_element_type=F32)
        for tile in range(which * tiles // 2, (which + 1) * tiles // 2):
            tile_step(tile)
    copies[-1].wait()

    own_high = owns_high()
    half = modes // 2
    for i in range(3):
        low, high = segment[pl.ds(i * modes, half)], segment[pl.ds(i * modes + half, half)]
        message[pl.ds(i * half, half)] = jnp.where(own_high, low, high)


def on_second():
    return lax.rem(lax.axis_index("ctx"), 2) == 1


def owns_high():
    place, group = lax.axis_index("ctx"), lax.axis_index("ch")
    bits = place ^ group
    for shift in (16, 8, 4, 2, 1):
        bits = bits ^ lax.shift_right_logical(bits, jnp.int32(shift))
    return lax.rem(bits, 2) == 1


def own_half(high, values):
    half = values.shape[0] // 2
    return jnp.where(high, values[half:], values[:half])


def in_order(second, own, other):
    return jnp.where(second, other, own), jnp.where(second, own, other)


def local_kernel(tiles, xf, gf, residue_ref, decay_ref, _, out_ref, back_ref,
                 pw, ends, starts, before, after, arrive, leave):
    modes, channels = decay_ref.shape
    chunks = xf.shape[0] // (SUB * SUB)
    span = chunks * SUB

    def tile_step(tile, _):
        lanes = pl.ds(pl.multiple_of(tile * LANES, LANES), LANES)
        decay = decay_ref[:, lanes]
        residue = residue_ref[:, lanes]
        powers(decay, pw)
        pw[2] = residue * pw[0]
        xs, gs = read_tokens(xf, chunks, lanes), read_tokens(gf, chunks, lanes)
        for m in range(modes):
            held, (back, _) = held_states(m, xs, pw), back_states(m, gs, pw)
            rows = pl.ds(m * SUB, SUB)
            ends[rows, :] = held[-1]
            starts[rows, :] = back[0]
            for p in range(1, chunks):
                before[m, p - 1] = held[p - 1]
                after[m, p - 1] = back[p]
        for half in range(modes // SUB):
            across = jnp.exp(-decay[half * SUB:(half + 1) * SUB] * span)
            for target, source, order in ((arrive, ends, range(SUB)), (leave, starts, range(SUB - 1, -1, -1))):
                running = jnp.zeros((SUB, LANES), F32)
                for j in order:
                    target[pl.ds(half * SUB * SUB + j, SUB, stride=SUB), :] = running
                    running = running * across + by_span(source, half, j)
        taps = []
        weight = residue
        for lag in range(SUB):
            taps.append(jnp.broadcast_to(jnp.sum(weight, axis=0, keepdims=True), (SUB, LANES)))
            weight = weight * pw[0]
        for values, carried, inside, target, forward in (
            (xs, arrive, before, out_ref, True), (gs, leave, after, back_ref, False)
        ):
            order = range(SUB) if forward else range(SUB - 1, -1, -1)
            totals = []
            for p in range(chunks):
                seq = [values[p][r] for r in order]
                totals.append([sum(taps[lag] * seq[r - lag] for lag in range(r + 1)) for r in range(SUB)])
            for m in range(modes):
                a, a8, first = (row(pw, i, pl.ds(m, 1)) for i in range(3))
                edge = carried[pl.ds(m * SUB, SUB), :]
                for q in range(chunks):
                    p = q if forward else chunks - 1 - q
                    if q == 0:
                        state = edge
                    else:
                        edge = edge * a8
                        state = edge + inside[m, p - 1 if forward else p]
                    wave = state * first
                    for r in range(SUB):
                        totals[p][r] = totals[p][r] + wave
                        if r < SUB - 1:
                            wave = wave * a
            for p in range(chunks):
                for r, at in enumerate(order):
                    target[tile - tiles[0], p * SUB + at] = totals[p][r]
        return 0

    lax.fori_loop(tiles[0], tiles[1], tile_step, 0)


def join_chip_kernel(tokens, segment, other, decay_ref, _, joined, core):
    modes = decay_ref.shape[0]
    half = modes // 2
    high = owns_high()
    decay = own_half(high, decay_ref[...])
    mine = [own_half(high, segment[i * modes:(i + 1) * modes]) for i in range(3)]
    theirs = [other[i * half:(i + 1) * half] for i in range(3)]
    (close0, close1), (open0, open1), _ = (in_order(on_second(), a, b) for a, b in zip(mine, theirs))
    block = jnp.exp(decay * (-1.0 * tokens))
    joined[0:half] = block * close0 + close1
    joined[half:2 * half] = open0 + block * open1
    joined[2 * half:] = (mine[2] + theirs[2]) + jnp.exp(-decay) * open1 * close0
    core[0:half] = close0
    core[half:] = open1


def join_kernel(tokens, size, masks, last, *refs):
    count = len(masks)
    segments = refs[:count]
    core, decay_ref, carried, _ = refs[count:count + 4]
    *outs, ordered = refs[count + 4:]
    second = on_second()
    decay = own_half(owns_high(), decay_ref[...])
    half = decay.shape[0]
    chip = lax.div(lax.axis_index("ctx"), 2)
    place = lax.rem(lax.div(chip, size), count)
    for mask, segment in zip(masks, segments):
        ordered[place ^ mask] = segment[...]
    block = jnp.exp(decay * (-2.0 * size * tokens))
    zero = jnp.zeros_like(decay)
    close, cross, grad, incoming = zero, zero, zero, zero
    for k in range(count):
        grad = grad + ordered[k, 2 * half:]
        if k:
            cross = cross + ordered[k, half:2 * half] * close
            incoming = jnp.where(place == k, close, incoming)
        close = close * block + ordered[k, 0:half]
    begin, outgoing = zero, zero
    for k in reversed(range(count)):
        outgoing = jnp.where(place == k, begin, outgoing)
        begin = begin * block + ordered[k, half:2 * half]
    grad = grad + jnp.exp(-decay) * cross
    if size > 1:
        inside = lax.rem(chip, size)
        incoming = carried[0:half] + incoming * jnp.exp(decay * (inside * (-2 * tokens)).astype(F32))
        outgoing = carried[half:] + outgoing * jnp.exp(decay * ((size - 1 - inside) * (-2 * tokens)).astype(F32))
    if not last:
        joined, arrivals = outs
        joined[0:half] = close
        joined[half:2 * half] = begin
        joined[2 * half:] = grad
        arrivals[0:half] = incoming
        arrivals[half:] = outgoing
        return
    total, own, message = outs
    total[...] = grad
    block = jnp.exp(decay * (-1.0 * tokens))
    into = incoming, block * incoming + core[0:half]
    out = block * outgoing + core[half:], outgoing
    own[0:half] = jnp.where(second, into[1], into[0])
    own[half:] = jnp.where(second, out[1], out[0])
    message[0:half] = jnp.where(second, into[0], into[1])
    message[half:] = jnp.where(second, out[0], out[1])


def finish_kernel(ranges, residue_ref, decay_ref, own, other, *refs):
    near = refs[:2 * len(ranges)]
    _, out_hbm, back_hbm, finished, out_ref, back_ref, result, pw, arrive, leave, sems = refs[2 * len(ranges):]
    modes, channels = decay_ref.shape
    half = modes // 2
    chunks = near[0].shape[1] // SUB
    span = chunks * SUB
    own_high = owns_high()
    first = residue_ref[...] * jnp.exp(-decay_ref[...])
    for target, rows in ((arrive, slice(0, half)), (leave, slice(half, modes))):
        low, high = in_order(own_high, own[rows], other[rows])
        target[0:half] = low * first[0:half]
        target[half:] = high * first[half:]

    def copy_out(tile, which):
        lanes = pl.ds(pl.multiple_of(tile * LANES, LANES), LANES)
        source, target = ((out_ref, out_hbm), (back_ref, back_hbm))[which]
        return pltpu.make_async_copy(source.at[:, lanes], target.at[:, lanes], sems.at[which, tile])

    def run(tiles, near_out, near_back):
        def tile_step(tile, _):
            lanes = pl.ds(pl.multiple_of(tile * LANES, LANES), LANES)
            decay = decay_ref[:, lanes]
            powers(decay, pw)
            pw[2] = decay * (-1.0 * span)
            pw[3] = arrive[:, lanes]
            pw[4] = leave[:, lanes]
            level = lax.broadcasted_iota(jnp.int32, (SUB, LANES), 0).astype(F32)
            for near, target, forward in ((near_out, out_ref, True), (near_back, back_ref, False)):
                order = range(SUB) if forward else range(SUB - 1, -1, -1)
                spans = level if forward else SUB - 1.0 - level
                totals = [[near[tile - tiles[0], p * SUB + r] for r in range(SUB)] for p in range(chunks)]
                for m in range(modes):
                    a, a8, rate = (row(pw, i, pl.ds(m, 1)) for i in range(3))
                    state = row(pw, 3 if forward else 4, pl.ds(m, 1)) * jnp.exp(rate * spans)
                    for q in range(chunks):
                        p = q if forward else chunks - 1 - q
                        wave = state
                        for r in order:
                            totals[p][r] = totals[p][r] + wave
                            wave = wave * a
                        if q < chunks - 1:
                            state = state * a8
                for p in range(chunks):
                    for r in range(SUB):
                        result[pl.ds(p * SUB + r, SUB, stride=span), :] = totals[p][r]
                target[:, lanes] = result[...].astype(target.dtype)
                copy_out(tile, 0 if forward else 1).start()
            return 0

        lax.fori_loop(tiles[0], tiles[1], tile_step, 0)

    for part, tiles in enumerate(ranges):
        run(tiles, near[2 * part], near[2 * part + 1])
    for tile in range(channels // LANES):
        for which in range(2):
            copy_out(tile, which).wait()
    finished[...] = jnp.zeros(finished.shape, F32)


def sum_kernel(own, other, *refs):
    refs[-1][...] = own[...] + other[...]


def assemble_kernel(scale, own, other, out_ref):
    half = own.shape[0]
    low, high = in_order(owns_high(), own[...], other[...])
    out_ref[0:half] = low * scale
    out_ref[half:] = high * scale


def vmem(*shape):
    return pltpu.VMEM(shape, F32)


def shaped(*shape):
    return jax.ShapeDtypeStruct(shape, F32)


def cost(flops, transcendentals, nbytes):
    return pl.CostEstimate(flops=flops, transcendentals=transcendentals, bytes_accessed=nbytes)


PARAMS = pltpu.CompilerParams(vmem_limit_bytes=32 * 1024 * 1024)
WHOLE = pl.BlockSpec(memory_space=pltpu.VMEM)
HBM = pl.BlockSpec(memory_space=pltpu.HBM)


UNREAD = pl.BlockSpec(memory_space=pl.ANY)


def body(signal, cotangent, residue, decay):
    tokens, channels = signal.shape
    modes = decay.shape[0]
    half = modes // 2
    n, groups = lax.axis_size("ctx"), lax.axis_size("ch")
    chunks = tokens // (SUB * SUB)
    elements = tokens * channels
    spans = vmem(modes * SUB, LANES)
    tiles = channels // LANES
    quarter = tiles // 4
    ranges = [(0, quarter), (quarter, 3 * quarter), (3 * quarter, tiles)]
    small = dict(compiler_params=PARAMS, cost_estimate=cost(elements, modes * channels, modes * channels * 32))

    def swap(x, ctx_mask, ch_mask=0):
        if ctx_mask != 1:
            ctx_mask |= (ctx_mask.bit_count() + ch_mask.bit_count()) % 2
        mask = ctx_mask * groups + ch_mask
        return lax.ppermute(x, ("ctx", "ch"), [(i, i ^ mask) for i in range(n * groups)])

    def near_part(part, after):
        first, last = ranges[part]
        share = elements * modes * (last - first) // tiles
        return pl.pallas_call(
            functools.partial(local_kernel, ranges[part]),
            out_shape=[shaped(last - first, chunks * SUB, SUB, LANES)] * 2,
            in_specs=[WHOLE] * 4 + [UNREAD],
            scratch_shapes=[vmem(3, modes, LANES), spans, spans]
            + [vmem(modes, chunks - 1, SUB, LANES)] * 2
            + [spans, spans],
            compiler_params=PARAMS,
            cost_estimate=cost(share * 400, 0, share),
            name="local_convolutions",
        )(*inputs, after)

    values = shaped(tokens, channels)
    *inputs, segment, message = pl.pallas_call(
        gather_kernel,
        out_shape=[values, values]
        + [shaped(modes, channels)] * 2
        + [shaped(3 * modes, channels), shaped(3 * half, channels)],
        in_specs=[HBM] * 4,
        scratch_shapes=[vmem(2, 2, modes, LANES)]
        + [vmem(2, modes * SUB, LANES)] * 3
        + [vmem(2, modes, chunks - 1, SUB, LANES)]
        + [pltpu.VMEM(signal.shape, signal.dtype)] * 2
        + [pltpu.SemaphoreType.DMA((6,))],
        compiler_params=PARAMS,
        cost_estimate=cost(elements * modes * 5, modes * channels * 3, elements * 6),
        name="block_states",
    )(*(pltpu.with_memory_space_constraint(a, pltpu.HBM) for a in (signal, cotangent, residue, decay)))
    residue, decay = inputs[2:]

    other = swap(message, 1)
    near = near_part(0, segment)
    joined, core = pl.pallas_call(
        functools.partial(join_chip_kernel, tokens),
        out_shape=[shaped(3 * half, channels), shaped(2 * half, channels)],
        in_specs=[WHOLE] * 3 + [UNREAD],
        name="join_chip",
        **small,
    )(segment, other, decay, near[0])

    chips = n // 2
    size = 1
    carried = core
    while size < chips:
        count = min(4, chips // size)
        last = size * count == chips
        masks = [3, 1, 2] if count == 4 else [1]
        others = [swap(joined, 2 * size * m) for m in masks]
        if last:
            near = near + near_part(1, joined)
        rows = [half, 2 * half, 2 * half] if last else [3 * half, 2 * half]
        joined, carried, *message = pl.pallas_call(
            functools.partial(join_kernel, tokens, size, [0] + masks, last),
            out_shape=[shaped(r, channels) for r in rows],
            in_specs=[WHOLE] * (count + 3) + [UNREAD],
            scratch_shapes=[vmem(count, 3 * half, channels)],
            name="join_chips",
            **small,
        )(joined, *others, core, decay, carried, near[-1])
        size *= count

    grad = joined
    stride = 1
    while stride < groups:
        other = swap(grad, 0, stride)
        if stride == 1:
            received = swap(message[0], 1)
            near = near + near_part(2, grad)
            pinned = near[-1:]
        stride *= 2
        if stride == groups:
            conv_out, signal_grad, *pinned = pl.pallas_call(
                functools.partial(finish_kernel, ranges),
                out_shape=[jax.ShapeDtypeStruct((tokens, channels), signal.dtype)] * 2 + [shaped(SUB, LANES)],
                in_specs=[WHOLE] * (4 + 2 * len(ranges)) + [UNREAD],
                out_specs=[HBM] * 2 + [WHOLE],
                scratch_shapes=[pltpu.VMEM((tokens, channels), signal.dtype)] * 2
                + [vmem(tokens, LANES), vmem(5, modes, LANES)]
                + [vmem(modes, channels)] * 2
                + [pltpu.SemaphoreType.DMA((2, tiles))],
                compiler_params=PARAMS,
                cost_estimate=cost(elements * modes * 600, 0, elements * 12),
                name="add_arrivals",
            )(residue, decay, carried, received, *near, grad)
        grad = pl.pallas_call(
            sum_kernel,
            out_shape=shaped(half, channels),
            in_specs=[WHOLE] * 2 + [UNREAD] * len(pinned),
            name="sum_groups",
            **small,
        )(grad, other, *pinned)
    residue_grad = pl.pallas_call(
        functools.partial(assemble_kernel, 1.0 / (tokens * n)),
        out_shape=shaped(modes, channels),
        name="assemble_gradient",
        **small,
    )(grad, swap(grad, 1))
    return conv_out, signal_grad, residue_grad


def solution(mesh):
    return jax.shard_map(
        body,
        mesh=mesh,
        in_specs=(P("ctx", "ch"), P("ctx", "ch"), P(), P()),
        out_specs=(P("ctx", "ch"), P("ctx", "ch"), P()),
        check_vma=False,
    )
```

```python
import functools

import jax
import jax.numpy as jnp
from jax import lax
from jax.experimental import pallas as pl
from jax.experimental.pallas import tpu as pltpu
from jax.sharding import PartitionSpec as P

SUB = 8
LANES = 128
F32 = jnp.float32


def row(ref, *index):
    return jnp.broadcast_to(ref[index], (SUB, LANES))


def token_order(tokens):
    rows = lax.broadcasted_iota(jnp.int32, (tokens, tokens), 0)
    columns = lax.broadcasted_iota(jnp.int32, (tokens, tokens), 1)
    wanted = lax.rem(rows, SUB) * (tokens // SUB) + lax.div(rows, SUB)
    return jnp.where(columns == wanted, 1.0, 0.0).astype(jnp.bfloat16)


def read_chunk(ref, p, lanes):
    return [ref[pl.ds((p * SUB + r) * SUB, SUB), lanes] for r in range(SUB)]


def read_tokens(ref, chunks, lanes):
    return [read_chunk(ref, p, lanes) for p in range(chunks)]


def powers(decay, pw):
    pw[0] = jnp.exp(-decay)
    pw[1] = jnp.exp(-decay * SUB)


def horner(terms, factor):
    total = terms[0]
    for term in terms[1:]:
        total = total * factor + term
    return total


def held_states(m, xs, pw):
    a, a8 = row(pw, 0, pl.ds(m, 1)), row(pw, 1, pl.ds(m, 1))
    held = []
    for chunk in xs:
        own = horner(chunk, a)
        held.append(held[-1] * a8 + own if held else own)
    return held


def back_states(m, gs, pw):
    a, a8 = row(pw, 0, pl.ds(m, 1)), row(pw, 1, pl.ds(m, 1))
    opens = [horner(chunk[::-1], a) for chunk in gs]
    back = opens[-1:]
    for own in reversed(opens[:-1]):
        back.insert(0, back[0] * a8 + own)
    return back, opens


def by_span(scratch, half, j):
    return scratch[pl.ds(half * SUB * SUB + j, SUB, stride=SUB), :]


def gather_kernel(*refs):
    sources = refs[:4]
    xf, gf, residue_ref, decay_ref, segment, message, *scratch, x_ref, g_ref, sems = refs[4:]
    staged = x_ref, g_ref, residue_ref, decay_ref
    copies = [pltpu.make_async_copy(*pair, sems.at[i]) for i, pair in enumerate(zip(sources, staged))]
    for copy in copies:
        copy.start()
    modes, channels = decay_ref.shape
    tokens = x_ref.shape[0]
    chunks = tokens // (SUB * SUB)
    span = chunks * SUB
    closing, opening, grad = (segment.at[pl.ds(i * modes, modes)] for i in range(3))
    order = token_order(tokens)
    for copy in copies:
        copy.wait()
    xf[...] = jnp.dot(order, x_ref[...], preferred_element_type=F32)
    gf[...] = jnp.dot(order, g_ref[...], preferred_element_type=F32)

    def tile_step(tile):
        lanes = pl.ds(tile * LANES, LANES)
        pw, ends, starts, inner, before = (ref.at[tile % 2] for ref in scratch)
        decay = decay_ref[:, lanes]
        powers(decay, pw)
        xs = read_tokens(xf, chunks, lanes)
        for m in range(modes):
            held = held_states(m, xs, pw)
            ends[pl.ds(m * SUB, SUB), :] = held[-1]
            for p in range(chunks - 1):
                before[m, p] = held[p]
        gs = read_tokens(gf, chunks, lanes)
        for m in range(modes):
            back, opens = back_states(m, gs, pw)
            rows = pl.ds(m * SUB, SUB)
            starts[rows, :] = back[0]
            inner[rows, :] = sum(opens[p] * before[m, p - 1] for p in range(1, chunks))
        lagged = [0.0] * SUB
        for p in range(chunks):
            xs, gs = read_chunk(xf, p, lanes), read_chunk(gf, p, lanes)
            for lag in range(SUB):
                lagged[lag] = lagged[lag] + sum(gs[r] * xs[r - lag] for r in range(lag, SUB))
        lagged = [jnp.sum(total, axis=0, keepdims=True) for total in lagged]
        for half in range(modes // SUB):
            some = pl.ds(half * SUB, SUB)
            a = pw[0, some, :]
            across = jnp.exp(-decay[half * SUB:(half + 1) * SUB] * span)
            arriving = jnp.zeros((SUB, LANES), F32)
            cross = jnp.zeros((SUB, LANES), F32)
            for j in range(SUB):
                cross = cross + (by_span(inner, half, j) + by_span(starts, half, j) * arriving)
                arriving = arriving * across + by_span(ends, half, j)
            leaving = horner([by_span(starts, half, j) for j in reversed(range(SUB))], across)
            near = horner([jnp.broadcast_to(v, (SUB, LANES)) for v in reversed(lagged)], a)
            closing[some, lanes] = arriving
            opening[some, lanes] = leaving
            grad[some, lanes] = near + a * cross

    for tile in range(channels // LANES):
        tile_step(tile)

    own_high = owns_high()
    half = modes // 2
    for i in range(3):
        low, high = segment[pl.ds(i * modes, half)], segment[pl.ds(i * modes + half, half)]
        message[pl.ds(i * half, half)] = jnp.where(own_high, low, high)


def on_second():
    return lax.rem(lax.axis_index("ctx"), 2) == 1


def owns_high():
    place, group = lax.axis_index("ctx"), lax.axis_index("ch")
    bits = place ^ group
    for shift in (16, 8, 4, 2, 1):
        bits = bits ^ lax.shift_right_logical(bits, jnp.int32(shift))
    return lax.rem(bits, 2) == 1


def own_half(high, values):
    half = values.shape[0] // 2
    return jnp.where(high, values[half:], values[:half])


def in_order(second, own, other):
    return jnp.where(second, other, own), jnp.where(second, own, other)


def local_kernel(tiles, xf, gf, residue_ref, decay_ref, _, out_ref, back_ref,
                 pw, ends, starts, before, after, arrive, leave):
    modes, channels = decay_ref.shape
    chunks = xf.shape[0] // (SUB * SUB)
    span = chunks * SUB

    def tile_step(tile, _):
        lanes = pl.ds(pl.multiple_of(tile * LANES, LANES), LANES)
        decay = decay_ref[:, lanes]
        residue = residue_ref[:, lanes]
        powers(decay, pw)
        pw[2] = residue * pw[0]
        xs, gs = read_tokens(xf, chunks, lanes), read_tokens(gf, chunks, lanes)
        for m in range(modes):
            held, (back, _) = held_states(m, xs, pw), back_states(m, gs, pw)
            rows = pl.ds(m * SUB, SUB)
            ends[rows, :] = held[-1]
            starts[rows, :] = back[0]
            for p in range(1, chunks):
                before[m, p - 1] = held[p - 1]
                after[m, p - 1] = back[p]
        for half in range(modes // SUB):
            across = jnp.exp(-decay[half * SUB:(half + 1) * SUB] * span)
            for target, source, order in ((arrive, ends, range(SUB)), (leave, starts, range(SUB - 1, -1, -1))):
                running = jnp.zeros((SUB, LANES), F32)
                for j in order:
                    target[pl.ds(half * SUB * SUB + j, SUB, stride=SUB), :] = running
                    running = running * across + by_span(source, half, j)
        taps = []
        weight = residue
        for lag in range(SUB):
            taps.append(jnp.broadcast_to(jnp.sum(weight, axis=0, keepdims=True), (SUB, LANES)))
            weight = weight * pw[0]
        for values, carried, inside, target, forward in (
            (xs, arrive, before, out_ref, True), (gs, leave, after, back_ref, False)
        ):
            order = range(SUB) if forward else range(SUB - 1, -1, -1)
            totals = []
            for p in range(chunks):
                seq = [values[p][r] for r in order]
                totals.append([sum(taps[lag] * seq[r - lag] for lag in range(r + 1)) for r in range(SUB)])
            for m in range(modes):
                a, a8, first = (row(pw, i, pl.ds(m, 1)) for i in range(3))
                edge = carried[pl.ds(m * SUB, SUB), :]
                for q in range(chunks):
                    p = q if forward else chunks - 1 - q
                    if q == 0:
                        state = edge
                    else:
                        edge = edge * a8
                        state = edge + inside[m, p - 1 if forward else p]
                    wave = state * first
                    for r in range(SUB):
                        totals[p][r] = totals[p][r] + wave
                        if r < SUB - 1:
                            wave = wave * a
            for p in range(chunks):
                for r, at in enumerate(order):
                    target[tile - tiles[0], p * SUB + at] = totals[p][r]
        return 0

    lax.fori_loop(tiles[0], tiles[1], tile_step, 0)


def join_chip_kernel(tokens, segment, other, decay_ref, _, joined, core):
    modes = decay_ref.shape[0]
    half = modes // 2
    high = owns_high()
    decay = own_half(high, decay_ref[...])
    mine = [own_half(high, segment[i * modes:(i + 1) * modes]) for i in range(3)]
    theirs = [other[i * half:(i + 1) * half] for i in range(3)]
    (close0, close1), (open0, open1), _ = (in_order(on_second(), a, b) for a, b in zip(mine, theirs))
    block = jnp.exp(decay * (-1.0 * tokens))
    joined[0:half] = block * close0 + close1
    joined[half:2 * half] = open0 + block * open1
    joined[2 * half:] = (mine[2] + theirs[2]) + jnp.exp(-decay) * open1 * close0
    core[0:half] = close0
    core[half:] = open1


def join_kernel(tokens, size, masks, last, *refs):
    count = len(masks)
    segments = refs[:count]
    core, decay_ref, carried, _ = refs[count:count + 4]
    *outs, ordered = refs[count + 4:]
    second = on_second()
    decay = own_half(owns_high(), decay_ref[...])
    half = decay.shape[0]
    chip = lax.div(lax.axis_index("ctx"), 2)
    place = lax.rem(lax.div(chip, size), count)
    for mask, segment in zip(masks, segments):
        ordered[place ^ mask] = segment[...]
    block = jnp.exp(decay * (-2.0 * size * tokens))
    zero = jnp.zeros_like(decay)
    close, cross, grad, incoming = zero, zero, zero, zero
    for k in range(count):
        grad = grad + ordered[k, 2 * half:]
        if k:
            cross = cross + ordered[k, half:2 * half] * close
            incoming = jnp.where(place == k, close, incoming)
        close = close * block + ordered[k, 0:half]
    begin, outgoing = zero, zero
    for k in reversed(range(count)):
        outgoing = jnp.where(place == k, begin, outgoing)
        begin = begin * block + ordered[k, half:2 * half]
    grad = grad + jnp.exp(-decay) * cross
    if size > 1:
        inside = lax.rem(chip, size)
        incoming = carried[0:half] + incoming * jnp.exp(decay * (inside * (-2 * tokens)).astype(F32))
        outgoing = carried[half:] + outgoing * jnp.exp(decay * ((size - 1 - inside) * (-2 * tokens)).astype(F32))
    if not last:
        joined, arrivals = outs
        joined[0:half] = close
        joined[half:2 * half] = begin
        joined[2 * half:] = grad
        arrivals[0:half] = incoming
        arrivals[half:] = outgoing
        return
    total, own, message = outs
    total[...] = grad
    block = jnp.exp(decay * (-1.0 * tokens))
    into = incoming, block * incoming + core[0:half]
    out = block * outgoing + core[half:], outgoing
    own[0:half] = jnp.where(second, into[1], into[0])
    own[half:] = jnp.where(second, out[1], out[0])
    message[0:half] = jnp.where(second, into[0], into[1])
    message[half:] = jnp.where(second, out[0], out[1])


def finish_kernel(ranges, residue_ref, decay_ref, own, other, *refs):
    near = refs[:2 * len(ranges)]
    _, out_hbm, back_hbm, finished, out_ref, back_ref, result, pw, arrive, leave, sems = refs[2 * len(ranges):]
    modes, channels = decay_ref.shape
    half = modes // 2
    chunks = near[0].shape[1] // SUB
    span = chunks * SUB
    own_high = owns_high()
    first = residue_ref[...] * jnp.exp(-decay_ref[...])
    for target, rows in ((arrive, slice(0, half)), (leave, slice(half, modes))):
        low, high = in_order(own_high, own[rows], other[rows])
        target[0:half] = low * first[0:half]
        target[half:] = high * first[half:]

    def copy_out(tile, which):
        lanes = pl.ds(pl.multiple_of(tile * LANES, LANES), LANES)
        source, target = ((out_ref, out_hbm), (back_ref, back_hbm))[which]
        return pltpu.make_async_copy(source.at[:, lanes], target.at[:, lanes], sems.at[which, tile])

    def run(tiles, near_out, near_back):
        def tile_step(tile, _):
            lanes = pl.ds(pl.multiple_of(tile * LANES, LANES), LANES)
            decay = decay_ref[:, lanes]
            powers(decay, pw)
            pw[2] = decay * (-1.0 * span)
            pw[3] = arrive[:, lanes]
            pw[4] = leave[:, lanes]
            level = lax.broadcasted_iota(jnp.int32, (SUB, LANES), 0).astype(F32)
            for near, target, forward in ((near_out, out_ref, True), (near_back, back_ref, False)):
                order = range(SUB) if forward else range(SUB - 1, -1, -1)
                spans = level if forward else SUB - 1.0 - level
                totals = [[near[tile - tiles[0], p * SUB + r] for r in range(SUB)] for p in range(chunks)]
                for m in range(modes):
                    a, a8, rate = (row(pw, i, pl.ds(m, 1)) for i in range(3))
                    state = row(pw, 3 if forward else 4, pl.ds(m, 1)) * jnp.exp(rate * spans)
                    for q in range(chunks):
                        p = q if forward else chunks - 1 - q
                        wave = state
                        for r in order:
                            totals[p][r] = totals[p][r] + wave
                            wave = wave * a
                        if q < chunks - 1:
                            state = state * a8
                for p in range(chunks):
                    for r in range(SUB):
                        result[pl.ds(p * SUB + r, SUB, stride=span), :] = totals[p][r]
                target[:, lanes] = result[...].astype(target.dtype)
                copy_out(tile, 0 if forward else 1).start()
            return 0

        lax.fori_loop(tiles[0], tiles[1], tile_step, 0)

    for part, tiles in enumerate(ranges):
        run(tiles, near[2 * part], near[2 * part + 1])
    for tile in range(channels // LANES):
        for which in range(2):
            copy_out(tile, which).wait()
    finished[...] = jnp.zeros(finished.shape, F32)


def sum_kernel(own, other, _, out_ref):
    out_ref[...] = own[...] + other[...]


def assemble_kernel(scale, own, other, out_ref):
    half = own.shape[0]
    low, high = in_order(owns_high(), own[...], other[...])
    out_ref[0:half] = low * scale
    out_ref[half:] = high * scale


def vmem(*shape):
    return pltpu.VMEM(shape, F32)


def shaped(*shape):
    return jax.ShapeDtypeStruct(shape, F32)


def cost(flops, transcendentals, nbytes):
    return pl.CostEstimate(flops=flops, transcendentals=transcendentals, bytes_accessed=nbytes)


PARAMS = pltpu.CompilerParams(vmem_limit_bytes=32 * 1024 * 1024)
WHOLE = pl.BlockSpec(memory_space=pltpu.VMEM)
HBM = pl.BlockSpec(memory_space=pltpu.HBM)


UNREAD = pl.BlockSpec(memory_space=pl.ANY)


def body(signal, cotangent, residue, decay):
    tokens, channels = signal.shape
    modes = decay.shape[0]
    half = modes // 2
    n, groups = lax.axis_size("ctx"), lax.axis_size("ch")
    chunks = tokens // (SUB * SUB)
    elements = tokens * channels
    spans = vmem(modes * SUB, LANES)
    tiles = channels // LANES
    quarter = tiles // 4
    ranges = [(0, quarter), (quarter, 3 * quarter), (3 * quarter, tiles)]
    small = dict(compiler_params=PARAMS, cost_estimate=cost(elements, modes * channels, modes * channels * 32))

    def swap(x, ctx_mask, ch_mask=0):
        if ctx_mask != 1:
            ctx_mask |= (ctx_mask.bit_count() + ch_mask.bit_count()) % 2
        mask = ctx_mask * groups + ch_mask
        return lax.ppermute(x, ("ctx", "ch"), [(i, i ^ mask) for i in range(n * groups)])

    def near_part(part, after):
        first, last = ranges[part]
        share = elements * modes * (last - first) // tiles
        return pl.pallas_call(
            functools.partial(local_kernel, ranges[part]),
            out_shape=[shaped(last - first, chunks * SUB, SUB, LANES)] * 2,
            in_specs=[WHOLE] * 4 + [UNREAD],
            scratch_shapes=[vmem(3, modes, LANES), spans, spans]
            + [vmem(modes, chunks - 1, SUB, LANES)] * 2
            + [spans, spans],
            compiler_params=PARAMS,
            cost_estimate=cost(share * 400, 0, share),
            name="local_convolutions",
        )(*inputs, after)

    values = shaped(tokens, channels)
    *inputs, segment, message = pl.pallas_call(
        gather_kernel,
        out_shape=[values, values]
        + [shaped(modes, channels)] * 2
        + [shaped(3 * modes, channels), shaped(3 * half, channels)],
        in_specs=[HBM] * 4,
        scratch_shapes=[vmem(2, 2, modes, LANES)]
        + [vmem(2, modes * SUB, LANES)] * 3
        + [vmem(2, modes, chunks - 1, SUB, LANES)]
        + [pltpu.VMEM(signal.shape, signal.dtype)] * 2
        + [pltpu.SemaphoreType.DMA((4,))],
        compiler_params=PARAMS,
        cost_estimate=cost(elements * modes * 5, modes * channels * 3, elements * 6),
        name="block_states",
    )(*(pltpu.with_memory_space_constraint(a, pltpu.HBM) for a in (signal, cotangent, residue, decay)))
    residue, decay = inputs[2:]

    other = swap(message, 1)
    near = near_part(0, segment)
    joined, core = pl.pallas_call(
        functools.partial(join_chip_kernel, tokens),
        out_shape=[shaped(3 * half, channels), shaped(2 * half, channels)],
        in_specs=[WHOLE] * 3 + [UNREAD],
        name="join_chip",
        **small,
    )(segment, other, decay, near[0])

    chips = n // 2
    size = 1
    carried = core
    while size < chips:
        count = min(4, chips // size)
        last = size * count == chips
        masks = [3, 1, 2] if count == 4 else [1]
        others = [swap(joined, 2 * size * m) for m in masks]
        if last:
            near = near + near_part(1, joined)
        rows = [half, 2 * half, 2 * half] if last else [3 * half, 2 * half]
        joined, carried, *message = pl.pallas_call(
            functools.partial(join_kernel, tokens, size, [0] + masks, last),
            out_shape=[shaped(r, channels) for r in rows],
            in_specs=[WHOLE] * (count + 3) + [UNREAD],
            scratch_shapes=[vmem(count, 3 * half, channels)],
            name="join_chips",
            **small,
        )(joined, *others, core, decay, carried, near[-1])
        size *= count

    grad = joined
    stride = groups // 2
    while stride:
        other = swap(grad, 0, stride)
        if stride == groups // 2:
            received = swap(message[0], 1)
            near = near + near_part(2, grad)
            pinned = near[-1]
        stride //= 2
        if not stride:
            conv_out, signal_grad, pinned = pl.pallas_call(
                functools.partial(finish_kernel, ranges),
                out_shape=[jax.ShapeDtypeStruct((tokens, channels), signal.dtype)] * 2 + [shaped(SUB, LANES)],
                in_specs=[WHOLE] * (4 + 2 * len(ranges)) + [UNREAD],
                out_specs=[HBM] * 2 + [WHOLE],
                scratch_shapes=[pltpu.VMEM((tokens, channels), signal.dtype)] * 2
                + [vmem(tokens, LANES), vmem(5, modes, LANES)]
                + [vmem(modes, channels)] * 2
                + [pltpu.SemaphoreType.DMA((2, tiles))],
                compiler_params=PARAMS,
                cost_estimate=cost(elements * modes * 600, 0, elements * 12),
                name="add_arrivals",
            )(residue, decay, carried, received, *near, grad)
        grad = pl.pallas_call(
            sum_kernel,
            out_shape=shaped(half, channels),
            in_specs=[WHOLE] * 2 + [UNREAD],
            name="sum_groups",
            **small,
        )(grad, other, pinned)
    residue_grad = pl.pallas_call(
        functools.partial(assemble_kernel, 1.0 / (tokens * n)),
        out_shape=shaped(modes, channels),
        name="assemble_gradient",
        **small,
    )(grad, swap(grad, 1))
    return conv_out, signal_grad, residue_grad


def solution(mesh):
    return jax.shard_map(
        body,
        mesh=mesh,
        in_specs=(P("ctx", "ch"), P("ctx", "ch"), P(), P()),
        out_specs=(P("ctx", "ch"), P("ctx", "ch"), P()),
        check_vma=False,
    )
```

```python
import functools

import jax
import jax.numpy as jnp
from jax import lax
from jax.experimental import pallas as pl
from jax.experimental.pallas import tpu as pltpu
from jax.sharding import PartitionSpec as P

SUB = 8
LANES = 128
F32 = jnp.float32


def row(ref, *index):
    return jnp.broadcast_to(ref[index], (SUB, LANES))


def token_order(tokens):
    rows = lax.broadcasted_iota(jnp.int32, (tokens, tokens), 0)
    columns = lax.broadcasted_iota(jnp.int32, (tokens, tokens), 1)
    wanted = lax.rem(rows, SUB) * (tokens // SUB) + lax.div(rows, SUB)
    return jnp.where(columns == wanted, 1.0, 0.0).astype(jnp.bfloat16)


def read_chunk(ref, p, lanes):
    return [ref[pl.ds((p * SUB + r) * SUB, SUB), lanes] for r in range(SUB)]


def read_tokens(ref, chunks, lanes):
    return [read_chunk(ref, p, lanes) for p in range(chunks)]


def powers(decay, pw):
    pw[0] = jnp.exp(-decay)
    pw[1] = jnp.exp(-decay * SUB)


def horner(terms, factor):
    total = terms[0]
    for term in terms[1:]:
        total = total * factor + term
    return total


def held_states(m, xs, pw):
    a, a8 = row(pw, 0, pl.ds(m, 1)), row(pw, 1, pl.ds(m, 1))
    held = []
    for chunk in xs:
        own = horner(chunk, a)
        held.append(held[-1] * a8 + own if held else own)
    return held


def back_states(m, gs, pw):
    a, a8 = row(pw, 0, pl.ds(m, 1)), row(pw, 1, pl.ds(m, 1))
    opens = [horner(chunk[::-1], a) for chunk in gs]
    back = opens[-1:]
    for own in reversed(opens[:-1]):
        back.insert(0, back[0] * a8 + own)
    return back, opens


def by_span(scratch, half, j):
    return scratch[pl.ds(half * SUB * SUB + j, SUB, stride=SUB), :]


def gather_kernel(*refs):
    sources = refs[:4]
    xf, gf, residue_ref, decay_ref, segment, message, *scratch, x_ref, g_ref, sems = refs[4:]
    staged = x_ref, g_ref, residue_ref, decay_ref
    copies = [pltpu.make_async_copy(*pair, sems.at[i]) for i, pair in enumerate(zip(sources, staged))]
    for copy in copies:
        copy.start()
    modes, channels = decay_ref.shape
    tokens = x_ref.shape[0]
    chunks = tokens // (SUB * SUB)
    span = chunks * SUB
    closing, opening, grad = (segment.at[pl.ds(i * modes, modes)] for i in range(3))
    order = token_order(tokens)
    for copy in copies:
        copy.wait()
    xf[...] = jnp.dot(order, x_ref[...], preferred_element_type=F32)
    gf[...] = jnp.dot(order, g_ref[...], preferred_element_type=F32)

    def tile_step(tile):
        lanes = pl.ds(tile * LANES, LANES)
        pw, ends, starts, inner, before = (ref.at[tile % 2] for ref in scratch)
        decay = decay_ref[:, lanes]
        powers(decay, pw)
        xs = read_tokens(xf, chunks, lanes)
        for m in range(modes):
            held = held_states(m, xs, pw)
            ends[pl.ds(m * SUB, SUB), :] = held[-1]
            for p in range(chunks - 1):
                before[m, p] = held[p]
        gs = read_tokens(gf, chunks, lanes)
        for m in range(modes):
            back, opens = back_states(m, gs, pw)
            rows = pl.ds(m * SUB, SUB)
            starts[rows, :] = back[0]
            inner[rows, :] = sum(opens[p] * before[m, p - 1] for p in range(1, chunks))
        lagged = [0.0] * SUB
        for p in range(chunks):
            xs, gs = read_chunk(xf, p, lanes), read_chunk(gf, p, lanes)
            for lag in range(SUB):
                lagged[lag] = lagged[lag] + sum(gs[r] * xs[r - lag] for r in range(lag, SUB))
        lagged = [jnp.sum(total, axis=0, keepdims=True) for total in lagged]
        for half in range(modes // SUB):
            some = pl.ds(half * SUB, SUB)
            a = pw[0, some, :]
            across = jnp.exp(-decay[half * SUB:(half + 1) * SUB] * span)
            arriving = jnp.zeros((SUB, LANES), F32)
            cross = jnp.zeros((SUB, LANES), F32)
            for j in range(SUB):
                cross = cross + (by_span(inner, half, j) + by_span(starts, half, j) * arriving)
                arriving = arriving * across + by_span(ends, half, j)
            leaving = horner([by_span(starts, half, j) for j in reversed(range(SUB))], across)
            near = horner([jnp.broadcast_to(v, (SUB, LANES)) for v in reversed(lagged)], a)
            closing[some, lanes] = arriving
            opening[some, lanes] = leaving
            grad[some, lanes] = near + a * cross

    for tile in range(channels // LANES):
        tile_step(tile)

    own_high = owns_high()
    half = modes // 2
    for i in range(3):
        low, high = segment[pl.ds(i * modes, half)], segment[pl.ds(i * modes + half, half)]
        message[pl.ds(i * half, half)] = jnp.where(own_high, low, high)


def on_second():
    return lax.rem(lax.axis_index("ctx"), 2) == 1


def owns_high():
    place, group = lax.axis_index("ctx"), lax.axis_index("ch")
    bits = place ^ group
    for shift in (16, 8, 4, 2, 1):
        bits = bits ^ lax.shift_right_logical(bits, jnp.int32(shift))
    return lax.rem(bits, 2) == 1


def own_half(high, values):
    half = values.shape[0] // 2
    return jnp.where(high, values[half:], values[:half])


def in_order(second, own, other):
    return jnp.where(second, other, own), jnp.where(second, own, other)


def local_kernel(tiles, xf, gf, residue_ref, decay_ref, _, out_ref, back_ref,
                 pw, ends, starts, before, after, arrive, leave):
    modes, channels = decay_ref.shape
    chunks = xf.shape[0] // (SUB * SUB)
    span = chunks * SUB

    def tile_step(tile, _):
        lanes = pl.ds(pl.multiple_of(tile * LANES, LANES), LANES)
        decay = decay_ref[:, lanes]
        residue = residue_ref[:, lanes]
        powers(decay, pw)
        pw[2] = residue * pw[0]
        xs, gs = read_tokens(xf, chunks, lanes), read_tokens(gf, chunks, lanes)
        for m in range(modes):
            held, (back, _) = held_states(m, xs, pw), back_states(m, gs, pw)
            rows = pl.ds(m * SUB, SUB)
            ends[rows, :] = held[-1]
            starts[rows, :] = back[0]
            for p in range(1, chunks):
                before[m, p - 1] = held[p - 1]
                after[m, p - 1] = back[p]
        for half in range(modes // SUB):
            across = jnp.exp(-decay[half * SUB:(half + 1) * SUB] * span)
            for target, source, order in ((arrive, ends, range(SUB)), (leave, starts, range(SUB - 1, -1, -1))):
                running = jnp.zeros((SUB, LANES), F32)
                for j in order:
                    target[pl.ds(half * SUB * SUB + j, SUB, stride=SUB), :] = running
                    running = running * across + by_span(source, half, j)
        taps = []
        weight = residue
        for lag in range(SUB):
            taps.append(jnp.broadcast_to(jnp.sum(weight, axis=0, keepdims=True), (SUB, LANES)))
            weight = weight * pw[0]
        for values, carried, inside, target, forward in (
            (xs, arrive, before, out_ref, True), (gs, leave, after, back_ref, False)
        ):
            order = range(SUB) if forward else range(SUB - 1, -1, -1)
            totals = []
            for p in range(chunks):
                seq = [values[p][r] for r in order]
                totals.append([sum(taps[lag] * seq[r - lag] for lag in range(r + 1)) for r in range(SUB)])
            for m in range(modes):
                a, a8, first = (row(pw, i, pl.ds(m, 1)) for i in range(3))
                edge = carried[pl.ds(m * SUB, SUB), :]
                for q in range(chunks):
                    p = q if forward else chunks - 1 - q
                    if q == 0:
                        state = edge
                    else:
                        edge = edge * a8
                        state = edge + inside[m, p - 1 if forward else p]
                    wave = state * first
                    for r in range(SUB):
                        totals[p][r] = totals[p][r] + wave
                        if r < SUB - 1:
                            wave = wave * a
            for p in range(chunks):
                for r, at in enumerate(order):
                    target[tile - tiles[0], p * SUB + at] = totals[p][r]
        return 0

    lax.fori_loop(tiles[0], tiles[1], tile_step, 0)


def join_chip_kernel(tokens, segment, other, decay_ref, _, joined, core):
    modes = decay_ref.shape[0]
    half = modes // 2
    high = owns_high()
    decay = own_half(high, decay_ref[...])
    mine = [own_half(high, segment[i * modes:(i + 1) * modes]) for i in range(3)]
    theirs = [other[i * half:(i + 1) * half] for i in range(3)]
    (close0, close1), (open0, open1), _ = (in_order(on_second(), a, b) for a, b in zip(mine, theirs))
    block = jnp.exp(decay * (-1.0 * tokens))
    joined[0:half] = block * close0 + close1
    joined[half:2 * half] = open0 + block * open1
    joined[2 * half:] = (mine[2] + theirs[2]) + jnp.exp(-decay) * open1 * close0
    core[0:half] = close0
    core[half:] = open1


def join_kernel(tokens, size, masks, last, *refs):
    count = len(masks)
    segments = refs[:count]
    core, decay_ref, carried, _ = refs[count:count + 4]
    *outs, ordered = refs[count + 4:]
    second = on_second()
    decay = own_half(owns_high(), decay_ref[...])
    half = decay.shape[0]
    chip = lax.div(lax.axis_index("ctx"), 2)
    place = lax.rem(lax.div(chip, size), count)
    for mask, segment in zip(masks, segments):
        ordered[place ^ mask] = segment[...]
    block = jnp.exp(decay * (-2.0 * size * tokens))
    zero = jnp.zeros_like(decay)
    close, cross, grad, incoming = zero, zero, zero, zero
    for k in range(count):
        grad = grad + ordered[k, 2 * half:]
        if k:
            cross = cross + ordered[k, half:2 * half] * close
            incoming = jnp.where(place == k, close, incoming)
        close = close * block + ordered[k, 0:half]
    begin, outgoing = zero, zero
    for k in reversed(range(count)):
        outgoing = jnp.where(place == k, begin, outgoing)
        begin = begin * block + ordered[k, half:2 * half]
    grad = grad + jnp.exp(-decay) * cross
    if size > 1:
        inside = lax.rem(chip, size)
        incoming = carried[0:half] + incoming * jnp.exp(decay * (inside * (-2 * tokens)).astype(F32))
        outgoing = carried[half:] + outgoing * jnp.exp(decay * ((size - 1 - inside) * (-2 * tokens)).astype(F32))
    if not last:
        joined, arrivals = outs
        joined[0:half] = close
        joined[half:2 * half] = begin
        joined[2 * half:] = grad
        arrivals[0:half] = incoming
        arrivals[half:] = outgoing
        return
    total, own, message = outs
    total[...] = grad
    block = jnp.exp(decay * (-1.0 * tokens))
    into = incoming, block * incoming + core[0:half]
    out = block * outgoing + core[half:], outgoing
    own[0:half] = jnp.where(second, into[1], into[0])
    own[half:] = jnp.where(second, out[1], out[0])
    message[0:half] = jnp.where(second, into[0], into[1])
    message[half:] = jnp.where(second, out[0], out[1])


def finish_kernel(tiles, residue_ref, decay_ref, own, other, near_out, near_back, *refs):
    out_hbm, back_hbm, finished, out_ref, back_ref, result, pw, arrive, leave, sems = refs[-10:]
    modes, channels = decay_ref.shape
    half = modes // 2
    chunks = near_out.shape[1] // SUB
    span = chunks * SUB
    own_high = owns_high()
    first = residue_ref[...] * jnp.exp(-decay_ref[...])
    for target, rows in ((arrive, slice(0, half)), (leave, slice(half, modes))):
        low, high = in_order(own_high, own[rows], other[rows])
        target[0:half] = low * first[0:half]
        target[half:] = high * first[half:]

    def copy_out(tile, which):
        lanes = pl.ds(pl.multiple_of(tile * LANES, LANES), LANES)
        source, target = ((out_ref, out_hbm), (back_ref, back_hbm))[which]
        return pltpu.make_async_copy(source.at[:, lanes], target.at[:, lanes], sems.at[which, tile])

    def tile_step(tile, _):
        lanes = pl.ds(pl.multiple_of(tile * LANES, LANES), LANES)
        decay = decay_ref[:, lanes]
        powers(decay, pw)
        pw[2] = decay * (-1.0 * span)
        pw[3] = arrive[:, lanes]
        pw[4] = leave[:, lanes]
        level = lax.broadcasted_iota(jnp.int32, (SUB, LANES), 0).astype(F32)
        for near, target, forward in ((near_out, out_ref, True), (near_back, back_ref, False)):
            order = range(SUB) if forward else range(SUB - 1, -1, -1)
            spans = level if forward else SUB - 1.0 - level
            totals = [[near[tile - tiles[0], p * SUB + r] for r in range(SUB)] for p in range(chunks)]
            for m in range(modes):
                a, a8, rate = (row(pw, i, pl.ds(m, 1)) for i in range(3))
                state = row(pw, 3 if forward else 4, pl.ds(m, 1)) * jnp.exp(rate * spans)
                for q in range(chunks):
                    p = q if forward else chunks - 1 - q
                    wave = state
                    for r in order:
                        totals[p][r] = totals[p][r] + wave
                        wave = wave * a
                    if q < chunks - 1:
                        state = state * a8
            for p in range(chunks):
                for r in range(SUB):
                    result[pl.ds(p * SUB + r, SUB, stride=span), :] = totals[p][r]
            target[:, lanes] = result[...].astype(target.dtype)
            copy_out(tile, 0 if forward else 1).start()
        return 0

    lax.fori_loop(*tiles, tile_step, 0)
    for tile in range(*tiles):
        for which in range(2):
            copy_out(tile, which).wait()
    finished[...] = jnp.zeros(finished.shape, F32)


def sum_kernel(own, other, *refs):
    refs[-1][...] = own[...] + other[...]


def assemble_kernel(scale, own, other, out_ref):
    half = own.shape[0]
    low, high = in_order(owns_high(), own[...], other[...])
    out_ref[0:half] = low * scale
    out_ref[half:] = high * scale


def vmem(*shape):
    return pltpu.VMEM(shape, F32)


def shaped(*shape):
    return jax.ShapeDtypeStruct(shape, F32)


def cost(flops, transcendentals, nbytes):
    return pl.CostEstimate(flops=flops, transcendentals=transcendentals, bytes_accessed=nbytes)


PARAMS = pltpu.CompilerParams(vmem_limit_bytes=32 * 1024 * 1024)
WHOLE = pl.BlockSpec(memory_space=pltpu.VMEM)
HBM = pl.BlockSpec(memory_space=pltpu.HBM)


UNREAD = pl.BlockSpec(memory_space=pl.ANY)


def body(signal, cotangent, residue, decay):
    tokens, channels = signal.shape
    modes = decay.shape[0]
    half = modes // 2
    n, groups = lax.axis_size("ctx"), lax.axis_size("ch")
    chunks = tokens // (SUB * SUB)
    elements = tokens * channels
    spans = vmem(modes * SUB, LANES)
    tiles = channels // LANES
    quarter = tiles // 4
    ranges = [(0, quarter), (quarter, tiles)]
    small = dict(compiler_params=PARAMS, cost_estimate=cost(elements, modes * channels, modes * channels * 32))

    def swap(x, ctx_mask, ch_mask=0):
        if ctx_mask != 1:
            ctx_mask |= (ctx_mask.bit_count() + ch_mask.bit_count()) % 2
        mask = ctx_mask * groups + ch_mask
        return lax.ppermute(x, ("ctx", "ch"), [(i, i ^ mask) for i in range(n * groups)])

    def near_part(part, after):
        first, last = ranges[part]
        share = elements * modes * (last - first) // tiles
        return pl.pallas_call(
            functools.partial(local_kernel, ranges[part]),
            out_shape=[shaped(last - first, chunks * SUB, SUB, LANES)] * 2,
            in_specs=[WHOLE] * 4 + [UNREAD],
            scratch_shapes=[vmem(3, modes, LANES), spans, spans]
            + [vmem(modes, chunks - 1, SUB, LANES)] * 2
            + [spans, spans],
            compiler_params=PARAMS,
            cost_estimate=cost(share * 400, 0, share),
            name="local_convolutions",
        )(*inputs, after)

    values = shaped(tokens, channels)
    *inputs, segment, message = pl.pallas_call(
        gather_kernel,
        out_shape=[values, values]
        + [shaped(modes, channels)] * 2
        + [shaped(3 * modes, channels), shaped(3 * half, channels)],
        in_specs=[HBM] * 4,
        scratch_shapes=[vmem(2, 2, modes, LANES)]
        + [vmem(2, modes * SUB, LANES)] * 3
        + [vmem(2, modes, chunks - 1, SUB, LANES)]
        + [pltpu.VMEM(signal.shape, signal.dtype)] * 2
        + [pltpu.SemaphoreType.DMA((4,))],
        compiler_params=PARAMS,
        cost_estimate=cost(elements * modes * 5, modes * channels * 3, elements * 6),
        name="block_states",
    )(*(pltpu.with_memory_space_constraint(a, pltpu.HBM) for a in (signal, cotangent, residue, decay)))
    residue, decay = inputs[2:]

    other = swap(message, 1)
    near = near_part(0, segment)
    joined, core = pl.pallas_call(
        functools.partial(join_chip_kernel, tokens),
        out_shape=[shaped(3 * half, channels), shaped(2 * half, channels)],
        in_specs=[WHOLE] * 3 + [UNREAD],
        name="join_chip",
        **small,
    )(segment, other, decay, near[0])

    chips = n // 2
    size = 1
    carried = core
    while size < chips:
        count = min(4, chips // size)
        last = size * count == chips
        masks = [2, 1, 3] if count == 4 else [1]
        others = [swap(joined, 2 * size * m) for m in masks]
        if last:
            near = near + near_part(1, joined)
        rows = [half, 2 * half, 2 * half] if last else [3 * half, 2 * half]
        joined, carried, *message = pl.pallas_call(
            functools.partial(join_kernel, tokens, size, [0] + masks, last),
            out_shape=[shaped(r, channels) for r in rows],
            in_specs=[WHOLE] * (count + 3) + [UNREAD],
            scratch_shapes=[vmem(count, 3 * half, channels)],
            name="join_chips",
            **small,
        )(joined, *others, core, decay, carried, near[-1])
        size *= count

    def finish_part(part, after, written):
        return pl.pallas_call(
            functools.partial(finish_kernel, ranges[part]),
            out_shape=[jax.ShapeDtypeStruct((tokens, channels), jnp.bfloat16)] * 2 + [shaped(SUB, LANES)],
            in_specs=[WHOLE] * 6 + [UNREAD] + [HBM] * len(written),
            out_specs=[HBM] * 2 + [WHOLE],
            input_output_aliases={7 + i: i for i in range(len(written))},
            scratch_shapes=[pltpu.VMEM((tokens, channels), jnp.bfloat16)] * 2
            + [vmem(tokens, LANES), vmem(5, modes, LANES)]
            + [vmem(modes, channels)] * 2
            + [pltpu.SemaphoreType.DMA((2, tiles))],
            compiler_params=PARAMS,
            cost_estimate=cost(elements * modes * 300, 0, elements * 6),
            name="add_arrivals",
        )(residue, decay, carried, received, *near[2 * part:2 * part + 2], after, *written)

    received = swap(message[0], 1)
    grad = joined
    written = []
    stride = groups // 2
    while stride:
        other = swap(grad, 0, stride)
        pinned = []
        if stride == groups // 2:
            *written, finished = finish_part(0, grad, written)
            pinned = [finished]
        if stride == 1:
            *written, finished = finish_part(1, grad, written)
            pinned = [finished]
        grad = pl.pallas_call(
            sum_kernel,
            out_shape=shaped(half, channels),
            in_specs=[WHOLE] * 2 + [UNREAD] * len(pinned),
            name="sum_groups",
            **small,
        )(grad, other, *pinned)
        stride //= 2
    residue_grad = pl.pallas_call(
        functools.partial(assemble_kernel, 1.0 / (tokens * n)),
        out_shape=shaped(modes, channels),
        name="assemble_gradient",
        **small,
    )(grad, swap(grad, 1))
    return *written, residue_grad


def solution(mesh):
    return jax.shard_map(
        body,
        mesh=mesh,
        in_specs=(P("ctx", "ch"), P("ctx", "ch"), P(), P()),
        out_specs=(P("ctx", "ch"), P("ctx", "ch"), P()),
        check_vma=False,
    )
```

```python
import functools

import jax
import jax.numpy as jnp
from jax import lax
from jax.experimental import pallas as pl
from jax.experimental.pallas import tpu as pltpu
from jax.sharding import PartitionSpec as P

SUB = 8
LANES = 128
F32 = jnp.float32


def row(ref, *index):
    return jnp.broadcast_to(ref[index], (SUB, LANES))


def token_order(tokens):
    rows = lax.broadcasted_iota(jnp.int32, (tokens, tokens), 0)
    columns = lax.broadcasted_iota(jnp.int32, (tokens, tokens), 1)
    wanted = lax.rem(rows, SUB) * (tokens // SUB) + lax.div(rows, SUB)
    return jnp.where(columns == wanted, 1.0, 0.0).astype(jnp.bfloat16)


def read_chunk(ref, p, lanes):
    return [ref[pl.ds((p * SUB + r) * SUB, SUB), lanes] for r in range(SUB)]


def read_tokens(ref, chunks, lanes):
    return [read_chunk(ref, p, lanes) for p in range(chunks)]


def powers(decay, pw):
    pw[0] = jnp.exp(-decay)
    pw[1] = jnp.exp(-decay * SUB)


def horner(terms, factor):
    total = terms[0]
    for term in terms[1:]:
        total = total * factor + term
    return total


def held_states(m, xs, pw):
    a, a8 = row(pw, 0, pl.ds(m, 1)), row(pw, 1, pl.ds(m, 1))
    held = []
    for chunk in xs:
        own = horner(chunk, a)
        held.append(held[-1] * a8 + own if held else own)
    return held


def back_states(m, gs, pw):
    a, a8 = row(pw, 0, pl.ds(m, 1)), row(pw, 1, pl.ds(m, 1))
    opens = [horner(chunk[::-1], a) for chunk in gs]
    back = opens[-1:]
    for own in reversed(opens[:-1]):
        back.insert(0, back[0] * a8 + own)
    return back, opens


def by_span(scratch, half, j):
    return scratch[pl.ds(half * SUB * SUB + j, SUB, stride=SUB), :]


def gather_kernel(*refs):
    sources = refs[:4]
    xf, gf, residue_ref, decay_ref, segment, message, *scratch, x_ref, g_ref, sems = refs[4:]
    staged = x_ref, g_ref, residue_ref, decay_ref
    copies = [pltpu.make_async_copy(*pair, sems.at[i]) for i, pair in enumerate(zip(sources, staged))]
    for copy in copies:
        copy.start()
    modes, channels = decay_ref.shape
    tokens = x_ref.shape[0]
    chunks = tokens // (SUB * SUB)
    span = chunks * SUB
    closing, opening, grad = (segment.at[pl.ds(i * modes, modes)] for i in range(3))
    order = token_order(tokens)
    for copy in copies:
        copy.wait()
    xf[...] = jnp.dot(order, x_ref[...], preferred_element_type=F32)
    gf[...] = jnp.dot(order, g_ref[...], preferred_element_type=F32)

    def tile_step(tile):
        lanes = pl.ds(tile * LANES, LANES)
        pw, ends, starts, inner, before = (ref.at[tile % 2] for ref in scratch)
        decay = decay_ref[:, lanes]
        powers(decay, pw)
        xs = read_tokens(xf, chunks, lanes)
        for m in range(modes):
            held = held_states(m, xs, pw)
            ends[pl.ds(m * SUB, SUB), :] = held[-1]
            for p in range(chunks - 1):
                before[m, p] = held[p]
        gs = read_tokens(gf, chunks, lanes)
        for m in range(modes):
            back, opens = back_states(m, gs, pw)
            rows = pl.ds(m * SUB, SUB)
            starts[rows, :] = back[0]
            inner[rows, :] = sum(opens[p] * before[m, p - 1] for p in range(1, chunks))
        lagged = [0.0] * SUB
        for p in range(chunks):
            xs, gs = read_chunk(xf, p, lanes), read_chunk(gf, p, lanes)
            for lag in range(SUB):
                lagged[lag] = lagged[lag] + sum(gs[r] * xs[r - lag] for r in range(lag, SUB))
        lagged = [jnp.sum(total, axis=0, keepdims=True) for total in lagged]
        for half in range(modes // SUB):
            some = pl.ds(half * SUB, SUB)
            a = pw[0, some, :]
            across = jnp.exp(-decay[half * SUB:(half + 1) * SUB] * span)
            arriving = jnp.zeros((SUB, LANES), F32)
            cross = jnp.zeros((SUB, LANES), F32)
            for j in range(SUB):
                cross = cross + (by_span(inner, half, j) + by_span(starts, half, j) * arriving)
                arriving = arriving * across + by_span(ends, half, j)
            leaving = horner([by_span(starts, half, j) for j in reversed(range(SUB))], across)
            near = horner([jnp.broadcast_to(v, (SUB, LANES)) for v in reversed(lagged)], a)
            closing[some, lanes] = arriving
            opening[some, lanes] = leaving
            grad[some, lanes] = near + a * cross

    for tile in range(channels // LANES):
        tile_step(tile)

    own_high = owns_high()
    half = modes // 2
    for i in range(3):
        low, high = segment[pl.ds(i * modes, half)], segment[pl.ds(i * modes + half, half)]
        message[pl.ds(i * half, half)] = jnp.where(own_high, low, high)


def on_second():
    return lax.rem(lax.axis_index("ctx"), 2) == 1


def owns_high():
    place, group = lax.axis_index("ctx"), lax.axis_index("ch")
    bits = place ^ group
    for shift in (16, 8, 4, 2, 1):
        bits = bits ^ lax.shift_right_logical(bits, jnp.int32(shift))
    return lax.rem(bits, 2) == 1


def own_half(high, values):
    half = values.shape[0] // 2
    return jnp.where(high, values[half:], values[:half])


def in_order(second, own, other):
    return jnp.where(second, other, own), jnp.where(second, own, other)


def local_kernel(tiles, xf, gf, residue_ref, decay_ref, _, out_ref, back_ref,
                 pw, ends, starts, before, after, arrive, leave):
    modes, channels = decay_ref.shape
    chunks = xf.shape[0] // (SUB * SUB)
    span = chunks * SUB

    def tile_step(tile, _):
        lanes = pl.ds(pl.multiple_of(tile * LANES, LANES), LANES)
        decay = decay_ref[:, lanes]
        residue = residue_ref[:, lanes]
        powers(decay, pw)
        pw[2] = residue * pw[0]
        xs, gs = read_tokens(xf, chunks, lanes), read_tokens(gf, chunks, lanes)
        for m in range(modes):
            held, (back, _) = held_states(m, xs, pw), back_states(m, gs, pw)
            rows = pl.ds(m * SUB, SUB)
            ends[rows, :] = held[-1]
            starts[rows, :] = back[0]
            for p in range(1, chunks):
                before[m, p - 1] = held[p - 1]
                after[m, p - 1] = back[p]
        for half in range(modes // SUB):
            across = jnp.exp(-decay[half * SUB:(half + 1) * SUB] * span)
            for target, source, order in ((arrive, ends, range(SUB)), (leave, starts, range(SUB - 1, -1, -1))):
                running = jnp.zeros((SUB, LANES), F32)
                for j in order:
                    target[pl.ds(half * SUB * SUB + j, SUB, stride=SUB), :] = running
                    running = running * across + by_span(source, half, j)
        taps = []
        weight = residue
        for lag in range(SUB):
            taps.append(jnp.broadcast_to(jnp.sum(weight, axis=0, keepdims=True), (SUB, LANES)))
            weight = weight * pw[0]
        for values, carried, inside, target, forward in (
            (xs, arrive, before, out_ref, True), (gs, leave, after, back_ref, False)
        ):
            order = range(SUB) if forward else range(SUB - 1, -1, -1)
            totals = []
            for p in range(chunks):
                seq = [values[p][r] for r in order]
                totals.append([sum(taps[lag] * seq[r - lag] for lag in range(r + 1)) for r in range(SUB)])
            for m in range(modes):
                a, a8, first = (row(pw, i, pl.ds(m, 1)) for i in range(3))
                edge = carried[pl.ds(m * SUB, SUB), :]
                for q in range(chunks):
                    p = q if forward else chunks - 1 - q
                    if q == 0:
                        state = edge
                    else:
                        edge = edge * a8
                        state = edge + inside[m, p - 1 if forward else p]
                    wave = state * first
                    for r in range(SUB):
                        totals[p][r] = totals[p][r] + wave
                        if r < SUB - 1:
                            wave = wave * a
            for p in range(chunks):
                for r, at in enumerate(order):
                    target[tile - tiles[0], p * SUB + at] = totals[p][r]
        return 0

    lax.fori_loop(tiles[0], tiles[1], tile_step, 0)


def join_chip_kernel(tokens, segment, other, decay_ref, _, joined, core):
    modes = decay_ref.shape[0]
    half = modes // 2
    high = owns_high()
    decay = own_half(high, decay_ref[...])
    mine = [own_half(high, segment[i * modes:(i + 1) * modes]) for i in range(3)]
    theirs = [other[i * half:(i + 1) * half] for i in range(3)]
    (close0, close1), (open0, open1), _ = (in_order(on_second(), a, b) for a, b in zip(mine, theirs))
    block = jnp.exp(decay * (-1.0 * tokens))
    joined[0:half] = block * close0 + close1
    joined[half:2 * half] = open0 + block * open1
    joined[2 * half:] = (mine[2] + theirs[2]) + jnp.exp(-decay) * open1 * close0
    core[0:half] = close0
    core[half:] = open1


def join_kernel(tokens, size, masks, last, *refs):
    count = len(masks)
    segments = refs[:count]
    core, decay_ref, carried, _ = refs[count:count + 4]
    *outs, ordered = refs[count + 4:]
    second = on_second()
    decay = own_half(owns_high(), decay_ref[...])
    half = decay.shape[0]
    chip = lax.div(lax.axis_index("ctx"), 2)
    place = lax.rem(lax.div(chip, size), count)
    for mask, segment in zip(masks, segments):
        ordered[place ^ mask] = segment[...]
    block = jnp.exp(decay * (-2.0 * size * tokens))
    zero = jnp.zeros_like(decay)
    close, cross, grad, incoming = zero, zero, zero, zero
    for k in range(count):
        grad = grad + ordered[k, 2 * half:]
        if k:
            cross = cross + ordered[k, half:2 * half] * close
            incoming = jnp.where(place == k, close, incoming)
        close = close * block + ordered[k, 0:half]
    begin, outgoing = zero, zero
    for k in reversed(range(count)):
        outgoing = jnp.where(place == k, begin, outgoing)
        begin = begin * block + ordered[k, half:2 * half]
    grad = grad + jnp.exp(-decay) * cross
    if size > 1:
        inside = lax.rem(chip, size)
        incoming = carried[0:half] + incoming * jnp.exp(decay * (inside * (-2 * tokens)).astype(F32))
        outgoing = carried[half:] + outgoing * jnp.exp(decay * ((size - 1 - inside) * (-2 * tokens)).astype(F32))
    if not last:
        joined, arrivals = outs
        joined[0:half] = close
        joined[half:2 * half] = begin
        joined[2 * half:] = grad
        arrivals[0:half] = incoming
        arrivals[half:] = outgoing
        return
    total, own, message = outs
    total[...] = grad
    block = jnp.exp(decay * (-1.0 * tokens))
    into = incoming, block * incoming + core[0:half]
    out = block * outgoing + core[half:], outgoing
    own[0:half] = jnp.where(second, into[1], into[0])
    own[half:] = jnp.where(second, out[1], out[0])
    message[0:half] = jnp.where(second, into[0], into[1])
    message[half:] = jnp.where(second, out[0], out[1])


def finish_kernel(tiles, residue_ref, decay_ref, own, other, near_out, near_back, *refs):
    out_hbm, back_hbm, finished, out_ref, back_ref, result, pw, arrive, leave, sems = refs[-10:]
    modes, channels = decay_ref.shape
    half = modes // 2
    chunks = near_out.shape[1] // SUB
    span = chunks * SUB
    own_high = owns_high()
    first = residue_ref[...] * jnp.exp(-decay_ref[...])
    for target, rows in ((arrive, slice(0, half)), (leave, slice(half, modes))):
        low, high = in_order(own_high, own[rows], other[rows])
        target[0:half] = low * first[0:half]
        target[half:] = high * first[half:]

    def copy_out(tile, which):
        lanes = pl.ds(pl.multiple_of(tile * LANES, LANES), LANES)
        source, target = ((out_ref, out_hbm), (back_ref, back_hbm))[which]
        return pltpu.make_async_copy(source.at[:, lanes], target.at[:, lanes], sems.at[which, tile])

    def tile_step(tile, _):
        lanes = pl.ds(pl.multiple_of(tile * LANES, LANES), LANES)
        decay = decay_ref[:, lanes]
        powers(decay, pw)
        pw[2] = decay * (-1.0 * span)
        pw[3] = arrive[:, lanes]
        pw[4] = leave[:, lanes]
        level = lax.broadcasted_iota(jnp.int32, (SUB, LANES), 0).astype(F32)
        for near, target, forward in ((near_out, out_ref, True), (near_back, back_ref, False)):
            order = range(SUB) if forward else range(SUB - 1, -1, -1)
            spans = level if forward else SUB - 1.0 - level
            totals = [[near[tile - tiles[0], p * SUB + r] for r in range(SUB)] for p in range(chunks)]
            for m in range(modes):
                a, a8, rate = (row(pw, i, pl.ds(m, 1)) for i in range(3))
                state = row(pw, 3 if forward else 4, pl.ds(m, 1)) * jnp.exp(rate * spans)
                for q in range(chunks):
                    p = q if forward else chunks - 1 - q
                    wave = state
                    for r in order:
                        totals[p][r] = totals[p][r] + wave
                        wave = wave * a
                    if q < chunks - 1:
                        state = state * a8
            for p in range(chunks):
                for r in range(SUB):
                    result[pl.ds(p * SUB + r, SUB, stride=span), :] = totals[p][r]
            target[:, lanes] = result[...].astype(target.dtype)
            copy_out(tile, 0 if forward else 1).start()
        return 0

    lax.fori_loop(*tiles, tile_step, 0)
    for tile in range(*tiles):
        for which in range(2):
            copy_out(tile, which).wait()
    finished[...] = jnp.zeros(finished.shape, F32)


def sum_kernel(own, other, *refs):
    refs[-1][...] = own[...] + other[...]


def assemble_kernel(scale, own, same, across, beside, _, out_ref):
    half = own.shape[0]
    low, high = in_order(owns_high(), own[...] + same[...], beside[...] + across[...])
    out_ref[0:half] = low * scale
    out_ref[half:] = high * scale


def vmem(*shape):
    return pltpu.VMEM(shape, F32)


def shaped(*shape):
    return jax.ShapeDtypeStruct(shape, F32)


def cost(flops, transcendentals, nbytes):
    return pl.CostEstimate(flops=flops, transcendentals=transcendentals, bytes_accessed=nbytes)


PARAMS = pltpu.CompilerParams(vmem_limit_bytes=32 * 1024 * 1024)
WHOLE = pl.BlockSpec(memory_space=pltpu.VMEM)
HBM = pl.BlockSpec(memory_space=pltpu.HBM)


UNREAD = pl.BlockSpec(memory_space=pl.ANY)


def body(signal, cotangent, residue, decay):
    tokens, channels = signal.shape
    modes = decay.shape[0]
    half = modes // 2
    n, groups = lax.axis_size("ctx"), lax.axis_size("ch")
    chunks = tokens // (SUB * SUB)
    elements = tokens * channels
    spans = vmem(modes * SUB, LANES)
    tiles = channels // LANES
    quarter = tiles // 4
    ranges = [(0, quarter), (quarter, tiles)]
    small = dict(compiler_params=PARAMS, cost_estimate=cost(elements, modes * channels, modes * channels * 32))

    def swap(x, ctx_mask, ch_mask=0):
        mask = ctx_mask * groups + ch_mask
        return lax.ppermute(x, ("ctx", "ch"), [(i, i ^ mask) for i in range(n * groups)])

    def swap_halves(x, ctx_mask, ch_mask=0):
        return swap(x, ctx_mask | (ctx_mask.bit_count() + ch_mask.bit_count()) % 2, ch_mask)

    def near_part(part, after):
        first, last = ranges[part]
        share = elements * modes * (last - first) // tiles
        return pl.pallas_call(
            functools.partial(local_kernel, ranges[part]),
            out_shape=[shaped(last - first, chunks * SUB, SUB, LANES)] * 2,
            in_specs=[WHOLE] * 4 + [UNREAD],
            scratch_shapes=[vmem(3, modes, LANES), spans, spans]
            + [vmem(modes, chunks - 1, SUB, LANES)] * 2
            + [spans, spans],
            compiler_params=PARAMS,
            cost_estimate=cost(share * 400, 0, share),
            name="local_convolutions",
        )(*inputs, after)

    values = shaped(tokens, channels)
    *inputs, segment, message = pl.pallas_call(
        gather_kernel,
        out_shape=[values, values]
        + [shaped(modes, channels)] * 2
        + [shaped(3 * modes, channels), shaped(3 * half, channels)],
        in_specs=[HBM] * 4,
        scratch_shapes=[vmem(2, 2, modes, LANES)]
        + [vmem(2, modes * SUB, LANES)] * 3
        + [vmem(2, modes, chunks - 1, SUB, LANES)]
        + [pltpu.VMEM(signal.shape, signal.dtype)] * 2
        + [pltpu.SemaphoreType.DMA((4,))],
        compiler_params=PARAMS,
        cost_estimate=cost(elements * modes * 5, modes * channels * 3, elements * 6),
        name="block_states",
    )(*(pltpu.with_memory_space_constraint(a, pltpu.HBM) for a in (signal, cotangent, residue, decay)))
    residue, decay = inputs[2:]

    other = swap(message, 1)
    near = near_part(0, segment)
    joined, core = pl.pallas_call(
        functools.partial(join_chip_kernel, tokens),
        out_shape=[shaped(3 * half, channels), shaped(2 * half, channels)],
        in_specs=[WHOLE] * 3 + [UNREAD],
        name="join_chip",
        **small,
    )(segment, other, decay, near[0])

    chips = n // 2
    size = 1
    carried = core
    while size < chips:
        count = min(4, chips // size)
        last = size * count == chips
        masks = [2, 1, 3] if count == 4 else [1]
        others = [swap_halves(joined, 2 * size * m) for m in masks]
        if last:
            near = near + near_part(1, joined)
        rows = [half, 2 * half, 2 * half] if last else [3 * half, 2 * half]
        joined, carried, *message = pl.pallas_call(
            functools.partial(join_kernel, tokens, size, [0] + masks, last),
            out_shape=[shaped(r, channels) for r in rows],
            in_specs=[WHOLE] * (count + 3) + [UNREAD],
            scratch_shapes=[vmem(count, 3 * half, channels)],
            name="join_chips",
            **small,
        )(joined, *others, core, decay, carried, near[-1])
        size *= count

    def finish_part(part, after, written):
        return pl.pallas_call(
            functools.partial(finish_kernel, ranges[part]),
            out_shape=[jax.ShapeDtypeStruct((tokens, channels), jnp.bfloat16)] * 2 + [shaped(SUB, LANES)],
            in_specs=[WHOLE] * 6 + [UNREAD] + [HBM] * len(written),
            out_specs=[HBM] * 2 + [WHOLE],
            input_output_aliases={7 + i: i for i in range(len(written))},
            scratch_shapes=[pltpu.VMEM((tokens, channels), jnp.bfloat16)] * 2
            + [vmem(tokens, LANES), vmem(5, modes, LANES)]
            + [vmem(modes, channels)] * 2
            + [pltpu.SemaphoreType.DMA((2, tiles))],
            compiler_params=PARAMS,
            cost_estimate=cost(elements * modes * 300, 0, elements * 6),
            name="add_arrivals",
        )(residue, decay, carried, received, *near[2 * part:2 * part + 2], after, *written)

    received = swap(message[0], 1)
    grad = joined
    written = []
    stride = groups // 2
    while stride > 1:
        other = swap_halves(grad, 0, stride)
        pinned = []
        if not written:
            *written, finished = finish_part(0, grad, written)
            pinned = [finished]
        grad = pl.pallas_call(
            sum_kernel,
            out_shape=shaped(half, channels),
            in_specs=[WHOLE] * 2 + [UNREAD] * len(pinned),
            name="sum_groups",
            **small,
        )(grad, other, *pinned)
        stride //= 2

    if not written:
        *written, finished = finish_part(0, grad, written)
    same, across, beside = swap_halves(grad, 0, 1), swap(grad, 0, 1), swap(grad, 1)
    *written, finished = finish_part(1, grad, written)
    residue_grad = pl.pallas_call(
        functools.partial(assemble_kernel, 1.0 / (tokens * n)),
        out_shape=shaped(modes, channels),
        in_specs=[WHOLE] * 4 + [UNREAD],
        name="assemble_gradient",
        **small,
    )(grad, same, across, beside, finished)
    return *written, residue_grad


def solution(mesh):
    return jax.shard_map(
        body,
        mesh=mesh,
        in_specs=(P("ctx", "ch"), P("ctx", "ch"), P(), P()),
        out_specs=(P("ctx", "ch"), P("ctx", "ch"), P()),
        check_vma=False,
    )
```

```python
import functools

import jax
import jax.numpy as jnp
from jax import lax
from jax.experimental import pallas as pl
from jax.experimental.pallas import tpu as pltpu
from jax.sharding import PartitionSpec as P

SUB = 8
LANES = 128
F32 = jnp.float32


def row(ref, *index):
    return jnp.broadcast_to(ref[index], (SUB, LANES))


def token_order(tokens):
    rows = lax.broadcasted_iota(jnp.int32, (tokens, tokens), 0)
    columns = lax.broadcasted_iota(jnp.int32, (tokens, tokens), 1)
    wanted = lax.rem(rows, SUB) * (tokens // SUB) + lax.div(rows, SUB)
    return jnp.where(columns == wanted, 1.0, 0.0).astype(jnp.bfloat16)


def read_chunk(ref, p, lanes):
    return [ref[pl.ds((p * SUB + r) * SUB, SUB), lanes] for r in range(SUB)]


def read_tokens(ref, chunks, lanes):
    return [read_chunk(ref, p, lanes) for p in range(chunks)]


def powers(decay, pw):
    pw[0] = jnp.exp(-decay)
    pw[1] = jnp.exp(-decay * SUB)


def horner(terms, factor):
    total = terms[0]
    for term in terms[1:]:
        total = total * factor + term
    return total


def held_states(m, xs, pw):
    a, a8 = row(pw, 0, pl.ds(m, 1)), row(pw, 1, pl.ds(m, 1))
    held = []
    for chunk in xs:
        own = horner(chunk, a)
        held.append(held[-1] * a8 + own if held else own)
    return held


def back_states(m, gs, pw):
    a, a8 = row(pw, 0, pl.ds(m, 1)), row(pw, 1, pl.ds(m, 1))
    opens = [horner(chunk[::-1], a) for chunk in gs]
    back = opens[-1:]
    for own in reversed(opens[:-1]):
        back.insert(0, back[0] * a8 + own)
    return back, opens


def by_span(scratch, half, j):
    return scratch[pl.ds(half * SUB * SUB + j, SUB, stride=SUB), :]


def gather_kernel(*refs):
    sources = refs[:4]
    xf, gf, residue_ref, decay_ref, segment, message, *scratch, x_ref, g_ref, sems = refs[4:]
    staged = x_ref, g_ref, residue_ref, decay_ref
    copies = [pltpu.make_async_copy(*pair, sems.at[i]) for i, pair in enumerate(zip(sources, staged))]
    for copy in copies:
        copy.start()
    modes, channels = decay_ref.shape
    tokens = x_ref.shape[0]
    chunks = tokens // (SUB * SUB)
    span = chunks * SUB
    closing, opening, grad = (segment.at[pl.ds(i * modes, modes)] for i in range(3))
    order = token_order(tokens)
    copies[0].wait()
    xf[...] = jnp.dot(order, x_ref[...], preferred_element_type=F32)
    copies[1].wait()
    gf[...] = jnp.dot(order, g_ref[...], preferred_element_type=F32)
    copies[3].wait()

    def tile_step(tile):
        lanes = pl.ds(tile * LANES, LANES)
        pw, ends, starts, inner, before = (ref.at[tile % 2] for ref in scratch)
        decay = decay_ref[:, lanes]
        powers(decay, pw)
        xs = read_tokens(xf, chunks, lanes)
        for m in range(modes):
            held = held_states(m, xs, pw)
            ends[pl.ds(m * SUB, SUB), :] = held[-1]
            for p in range(chunks - 1):
                before[m, p] = held[p]
        gs = read_tokens(gf, chunks, lanes)
        for m in range(modes):
            back, opens = back_states(m, gs, pw)
            rows = pl.ds(m * SUB, SUB)
            starts[rows, :] = back[0]
            inner[rows, :] = sum(opens[p] * before[m, p - 1] for p in range(1, chunks))
        lagged = [0.0] * SUB
        for p in range(chunks):
            xs, gs = read_chunk(xf, p, lanes), read_chunk(gf, p, lanes)
            for lag in range(SUB):
                lagged[lag] = lagged[lag] + sum(gs[r] * xs[r - lag] for r in range(lag, SUB))
        lagged = [jnp.sum(total, axis=0, keepdims=True) for total in lagged]
        for half in range(modes // SUB):
            some = pl.ds(half * SUB, SUB)
            a = pw[0, some, :]
            across = jnp.exp(-decay[half * SUB:(half + 1) * SUB] * span)
            arriving = jnp.zeros((SUB, LANES), F32)
            cross = jnp.zeros((SUB, LANES), F32)
            for j in range(SUB):
                cross = cross + (by_span(inner, half, j) + by_span(starts, half, j) * arriving)
                arriving = arriving * across + by_span(ends, half, j)
            leaving = horner([by_span(starts, half, j) for j in reversed(range(SUB))], across)
            near = horner([jnp.broadcast_to(v, (SUB, LANES)) for v in reversed(lagged)], a)
            closing[some, lanes] = arriving
            opening[some, lanes] = leaving
            grad[some, lanes] = near + a * cross

    for tile in range(channels // LANES):
        tile_step(tile)
    copies[2].wait()

    own_high = owns_high()
    half = modes // 2
    for i in range(3):
        low, high = segment[pl.ds(i * modes, half)], segment[pl.ds(i * modes + half, half)]
        message[pl.ds(i * half, half)] = jnp.where(own_high, low, high)


def on_second():
    return lax.rem(lax.axis_index("ctx"), 2) == 1


def owns_high():
    place, group = lax.axis_index("ctx"), lax.axis_index("ch")
    bits = place ^ group
    for shift in (16, 8, 4, 2, 1):
        bits = bits ^ lax.shift_right_logical(bits, jnp.int32(shift))
    return lax.rem(bits, 2) == 1


def own_half(high, values):
    half = values.shape[0] // 2
    return jnp.where(high, values[half:], values[:half])


def in_order(second, own, other):
    return jnp.where(second, other, own), jnp.where(second, own, other)


def local_kernel(tiles, xf, gf, residue_ref, decay_ref, _, out_ref, back_ref,
                 pw, ends, starts, before, after, arrive, leave):
    modes, channels = decay_ref.shape
    chunks = xf.shape[0] // (SUB * SUB)
    span = chunks * SUB

    def tile_step(tile, _):
        lanes = pl.ds(pl.multiple_of(tile * LANES, LANES), LANES)
        decay = decay_ref[:, lanes]
        residue = residue_ref[:, lanes]
        powers(decay, pw)
        pw[2] = residue * pw[0]
        xs, gs = read_tokens(xf, chunks, lanes), read_tokens(gf, chunks, lanes)
        for m in range(modes):
            held, (back, _) = held_states(m, xs, pw), back_states(m, gs, pw)
            rows = pl.ds(m * SUB, SUB)
            ends[rows, :] = held[-1]
            starts[rows, :] = back[0]
            for p in range(1, chunks):
                before[m, p - 1] = held[p - 1]
                after[m, p - 1] = back[p]
        for half in range(modes // SUB):
            across = jnp.exp(-decay[half * SUB:(half + 1) * SUB] * span)
            for target, source, order in ((arrive, ends, range(SUB)), (leave, starts, range(SUB - 1, -1, -1))):
                running = jnp.zeros((SUB, LANES), F32)
                for j in order:
                    target[pl.ds(half * SUB * SUB + j, SUB, stride=SUB), :] = running
                    running = running * across + by_span(source, half, j)
        taps = []
        weight = residue
        for lag in range(SUB):
            taps.append(jnp.broadcast_to(jnp.sum(weight, axis=0, keepdims=True), (SUB, LANES)))
            weight = weight * pw[0]
        for values, carried, inside, target, forward in (
            (xs, arrive, before, out_ref, True), (gs, leave, after, back_ref, False)
        ):
            order = range(SUB) if forward else range(SUB - 1, -1, -1)
            totals = []
            for p in range(chunks):
                seq = [values[p][r] for r in order]
                totals.append([sum(taps[lag] * seq[r - lag] for lag in range(r + 1)) for r in range(SUB)])
            for m in range(modes):
                a, a8, first = (row(pw, i, pl.ds(m, 1)) for i in range(3))
                edge = carried[pl.ds(m * SUB, SUB), :]
                for q in range(chunks):
                    p = q if forward else chunks - 1 - q
                    if q == 0:
                        state = edge
                    else:
                        edge = edge * a8
                        state = edge + inside[m, p - 1 if forward else p]
                    wave = state * first
                    for r in range(SUB):
                        totals[p][r] = totals[p][r] + wave
                        if r < SUB - 1:
                            wave = wave * a
            for p in range(chunks):
                for r, at in enumerate(order):
                    target[tile - tiles[0], p * SUB + at] = totals[p][r]
        return 0

    lax.fori_loop(tiles[0], tiles[1], tile_step, 0)


def join_chip_kernel(tokens, segment, other, decay_ref, _, joined, core):
    modes = decay_ref.shape[0]
    half = modes // 2
    high = owns_high()
    decay = own_half(high, decay_ref[...])
    mine = [own_half(high, segment[i * modes:(i + 1) * modes]) for i in range(3)]
    theirs = [other[i * half:(i + 1) * half] for i in range(3)]
    (close0, close1), (open0, open1), _ = (in_order(on_second(), a, b) for a, b in zip(mine, theirs))
    block = jnp.exp(decay * (-1.0 * tokens))
    joined[0:half] = block * close0 + close1
    joined[half:2 * half] = open0 + block * open1
    joined[2 * half:] = (mine[2] + theirs[2]) + jnp.exp(-decay) * open1 * close0
    core[0:half] = close0
    core[half:] = open1


def join_kernel(tokens, size, masks, last, *refs):
    count = len(masks)
    segments = refs[:count]
    core, decay_ref, carried, _ = refs[count:count + 4]
    *outs, ordered = refs[count + 4:]
    second = on_second()
    decay = own_half(owns_high(), decay_ref[...])
    half = decay.shape[0]
    chip = lax.div(lax.axis_index("ctx"), 2)
    place = lax.rem(lax.div(chip, size), count)
    for mask, segment in zip(masks, segments):
        ordered[place ^ mask] = segment[...]
    block = jnp.exp(decay * (-2.0 * size * tokens))
    zero = jnp.zeros_like(decay)
    close, cross, grad, incoming = zero, zero, zero, zero
    for k in range(count):
        grad = grad + ordered[k, 2 * half:]
        if k:
            cross = cross + ordered[k, half:2 * half] * close
            incoming = jnp.where(place == k, close, incoming)
        close = close * block + ordered[k, 0:half]
    begin, outgoing = zero, zero
    for k in reversed(range(count)):
        outgoing = jnp.where(place == k, begin, outgoing)
        begin = begin * block + ordered[k, half:2 * half]
    grad = grad + jnp.exp(-decay) * cross
    if size > 1:
        inside = lax.rem(chip, size)
        incoming = carried[0:half] + incoming * jnp.exp(decay * (inside * (-2 * tokens)).astype(F32))
        outgoing = carried[half:] + outgoing * jnp.exp(decay * ((size - 1 - inside) * (-2 * tokens)).astype(F32))
    if not last:
        joined, arrivals = outs
        joined[0:half] = close
        joined[half:2 * half] = begin
        joined[2 * half:] = grad
        arrivals[0:half] = incoming
        arrivals[half:] = outgoing
        return
    total, own, message = outs
    total[...] = grad
    block = jnp.exp(decay * (-1.0 * tokens))
    into = incoming, block * incoming + core[0:half]
    out = block * outgoing + core[half:], outgoing
    own[0:half] = jnp.where(second, into[1], into[0])
    own[half:] = jnp.where(second, out[1], out[0])
    message[0:half] = jnp.where(second, into[0], into[1])
    message[half:] = jnp.where(second, out[0], out[1])


def finish_kernel(tiles, ranges, residue_ref, decay_ref, own, other, *refs):
    nears = refs[:2 * len(ranges)]
    out_hbm, back_hbm, finished, out_ref, back_ref, results, pws, arrive, leave, sems = refs[-10:]
    modes, channels = decay_ref.shape
    half = modes // 2
    chunks = nears[0].shape[1] // SUB
    span = chunks * SUB
    own_high = owns_high()
    first = residue_ref[...] * jnp.exp(-decay_ref[...])
    for target, rows in ((arrive, slice(0, half)), (leave, slice(half, modes))):
        low, high = in_order(own_high, own[rows], other[rows])
        target[0:half] = low * first[0:half]
        target[half:] = high * first[half:]

    def copy_out(tile, which):
        lanes = pl.ds(tile * LANES, LANES)
        source, target = ((out_ref, out_hbm), (back_ref, back_hbm))[which]
        return pltpu.make_async_copy(source.at[:, lanes], target.at[:, lanes], sems.at[which, tile])

    def tile_step(tile):
        part, = [i for i, (first, last) in enumerate(ranges) if first <= tile < last]
        near_out, near_back = (near.at[tile - ranges[part][0]] for near in nears[2 * part:2 * part + 2])
        pw = pws.at[tile % 2]
        lanes = pl.ds(tile * LANES, LANES)
        decay = decay_ref[:, lanes]
        powers(decay, pw)
        pw[2] = decay * (-1.0 * span)
        pw[3] = arrive[:, lanes]
        pw[4] = leave[:, lanes]
        level = lax.broadcasted_iota(jnp.int32, (SUB, LANES), 0).astype(F32)
        for near, target, forward in ((near_out, out_ref, True), (near_back, back_ref, False)):
            result = results.at[2 * (tile % 2) + forward]
            order = range(SUB) if forward else range(SUB - 1, -1, -1)
            spans = level if forward else SUB - 1.0 - level
            totals = [[near[p * SUB + r] for r in range(SUB)] for p in range(chunks)]
            for m in range(modes):
                a, a8, rate = (row(pw, i, pl.ds(m, 1)) for i in range(3))
                state = row(pw, 3 if forward else 4, pl.ds(m, 1)) * jnp.exp(rate * spans)
                for q in range(chunks):
                    p = q if forward else chunks - 1 - q
                    wave = state
                    for r in order:
                        totals[p][r] = totals[p][r] + wave
                        wave = wave * a
                    if q < chunks - 1:
                        state = state * a8
            for p in range(chunks):
                for r in range(SUB):
                    result[pl.ds(p * SUB + r, SUB, stride=span), :] = totals[p][r]
            target[:, lanes] = result[...].astype(target.dtype)
            copy_out(tile, 0 if forward else 1).start()

    for tile in range(*tiles):
        tile_step(tile)
    for tile in range(*tiles):
        for which in range(2):
            copy_out(tile, which).wait()
    finished[...] = jnp.zeros(finished.shape, F32)


def sum_kernel(own, other, *refs):
    refs[-1][...] = own[...] + other[...]


def assemble_kernel(scale, own, other, out_ref):
    half = own.shape[0]
    low, high = in_order(owns_high(), own[...], other[...])
    out_ref[0:half] = low * scale
    out_ref[half:] = high * scale


def vmem(*shape):
    return pltpu.VMEM(shape, F32)


def shaped(*shape):
    return jax.ShapeDtypeStruct(shape, F32)


def cost(flops, transcendentals, nbytes):
    return pl.CostEstimate(flops=flops, transcendentals=transcendentals, bytes_accessed=nbytes)


PARAMS = pltpu.CompilerParams(vmem_limit_bytes=32 * 1024 * 1024)
WHOLE = pl.BlockSpec(memory_space=pltpu.VMEM)
HBM = pl.BlockSpec(memory_space=pltpu.HBM)


UNREAD = pl.BlockSpec(memory_space=pl.ANY)


def body(signal, cotangent, residue, decay):
    tokens, channels = signal.shape
    modes = decay.shape[0]
    half = modes // 2
    n, groups = lax.axis_size("ctx"), lax.axis_size("ch")
    chunks = tokens // (SUB * SUB)
    elements = tokens * channels
    spans = vmem(modes * SUB, LANES)
    tiles = channels // LANES
    quarter = tiles // 4
    ranges = [(0, quarter), (quarter, tiles)]
    small = dict(compiler_params=PARAMS, cost_estimate=cost(elements, modes * channels, modes * channels * 32))

    def swap(x, ctx_mask, ch_mask=0):
        if ctx_mask != 1:
            ctx_mask |= (ctx_mask.bit_count() + ch_mask.bit_count()) % 2
        mask = ctx_mask * groups + ch_mask
        return lax.ppermute(x, ("ctx", "ch"), [(i, i ^ mask) for i in range(n * groups)])

    def near_part(part, after):
        first, last = ranges[part]
        share = elements * modes * (last - first) // tiles
        return pl.pallas_call(
            functools.partial(local_kernel, ranges[part]),
            out_shape=[shaped(last - first, chunks * SUB, SUB, LANES)] * 2,
            in_specs=[WHOLE] * 4 + [UNREAD],
            scratch_shapes=[vmem(3, modes, LANES), spans, spans]
            + [vmem(modes, chunks - 1, SUB, LANES)] * 2
            + [spans, spans],
            compiler_params=PARAMS,
            cost_estimate=cost(share * 400, 0, share),
            name="local_convolutions",
        )(*inputs, after)

    values = shaped(tokens, channels)
    *inputs, segment, message = pl.pallas_call(
        gather_kernel,
        out_shape=[values, values]
        + [shaped(modes, channels)] * 2
        + [shaped(3 * modes, channels), shaped(3 * half, channels)],
        in_specs=[HBM] * 4,
        scratch_shapes=[vmem(2, 2, modes, LANES)]
        + [vmem(2, modes * SUB, LANES)] * 3
        + [vmem(2, modes, chunks - 1, SUB, LANES)]
        + [pltpu.VMEM(signal.shape, signal.dtype)] * 2
        + [pltpu.SemaphoreType.DMA((4,))],
        compiler_params=PARAMS,
        cost_estimate=cost(elements * modes * 5, modes * channels * 3, elements * 6),
        name="block_states",
    )(*(pltpu.with_memory_space_constraint(a, pltpu.HBM) for a in (signal, cotangent, residue, decay)))
    residue, decay = inputs[2:]

    other = swap(message, 1)
    near = near_part(0, segment)
    joined, core = pl.pallas_call(
        functools.partial(join_chip_kernel, tokens),
        out_shape=[shaped(3 * half, channels), shaped(2 * half, channels)],
        in_specs=[WHOLE] * 3 + [UNREAD],
        name="join_chip",
        **small,
    )(segment, other, decay, near[0])

    chips = n // 2
    size = 1
    carried = core
    while size < chips:
        count = min(4, chips // size)
        last = size * count == chips
        masks = [2, 1, 3] if count == 4 else [1]
        others = [swap(joined, 2 * size * m) for m in masks]
        if last:
            near = near + near_part(1, joined)
        rows = [half, 2 * half, 2 * half] if last else [3 * half, 2 * half]
        joined, carried, *message = pl.pallas_call(
            functools.partial(join_kernel, tokens, size, [0] + masks, last),
            out_shape=[shaped(r, channels) for r in rows],
            in_specs=[WHOLE] * (count + 3) + [UNREAD],
            scratch_shapes=[vmem(count, 3 * half, channels)],
            name="join_chips",
            **small,
        )(joined, *others, core, decay, carried, near[-1])
        size *= count

    def finish_part(part, after, written):
        return pl.pallas_call(
            functools.partial(finish_kernel, (part * tiles // 2, (part + 1) * tiles // 2), ranges),
            out_shape=[jax.ShapeDtypeStruct((tokens, channels), jnp.bfloat16)] * 2 + [shaped(SUB, LANES)],
            in_specs=[WHOLE] * (4 + len(near)) + [UNREAD] + [HBM] * len(written),
            out_specs=[HBM] * 2 + [WHOLE],
            input_output_aliases={5 + len(near) + i: i for i in range(len(written))},
            scratch_shapes=[pltpu.VMEM((tokens, channels), jnp.bfloat16)] * 2
            + [vmem(4, tokens, LANES), vmem(2, 5, modes, LANES)]
            + [vmem(modes, channels)] * 2
            + [pltpu.SemaphoreType.DMA((2, tiles))],
            compiler_params=PARAMS,
            cost_estimate=cost(elements * modes * 300, 0, elements * 6),
            name="add_arrivals",
        )(residue, decay, carried, received, *near, after, *written)

    received = swap(message[0], 1)
    grad = joined
    written = []
    stride = groups // 2
    while stride:
        other = swap(grad, 0, stride)
        pinned = []
        if stride == groups // 2:
            *written, finished = finish_part(0, grad, written)
            pinned = [finished]
        if stride == 1:
            *written, finished = finish_part(1, grad, written)
            pinned = [finished]
        grad = pl.pallas_call(
            sum_kernel,
            out_shape=shaped(half, channels),
            in_specs=[WHOLE] * 2 + [UNREAD] * len(pinned),
            name="sum_groups",
            **small,
        )(grad, other, *pinned)
        stride //= 2
    residue_grad = pl.pallas_call(
        functools.partial(assemble_kernel, 1.0 / (tokens * n)),
        out_shape=shaped(modes, channels),
        name="assemble_gradient",
        **small,
    )(grad, swap(grad, 1))
    return *written, residue_grad


def solution(mesh):
    return jax.shard_map(
        body,
        mesh=mesh,
        in_specs=(P("ctx", "ch"), P("ctx", "ch"), P(), P()),
        out_specs=(P("ctx", "ch"), P("ctx", "ch"), P()),
        check_vma=False,
    )
```

```python
import functools

import jax
import jax.numpy as jnp
from jax import lax
from jax.experimental import pallas as pl
from jax.experimental.pallas import tpu as pltpu
from jax.sharding import PartitionSpec as P

SUB = 8
LANES = 128
F32 = jnp.float32


def row(ref, *index):
    return jnp.broadcast_to(ref[index], (SUB, LANES))


def token_order(tokens):
    rows = lax.broadcasted_iota(jnp.int32, (tokens, tokens), 0)
    columns = lax.broadcasted_iota(jnp.int32, (tokens, tokens), 1)
    wanted = lax.rem(rows, SUB) * (tokens // SUB) + lax.div(rows, SUB)
    return jnp.where(columns == wanted, 1.0, 0.0).astype(jnp.bfloat16)


def read_chunk(ref, p, lanes):
    return [ref[pl.ds((p * SUB + r) * SUB, SUB), lanes] for r in range(SUB)]


def read_tokens(ref, chunks, lanes):
    return [read_chunk(ref, p, lanes) for p in range(chunks)]


def powers(decay, pw):
    pw[0] = jnp.exp(-decay)
    pw[1] = jnp.exp(-decay * SUB)


def horner(terms, factor):
    total = terms[0]
    for term in terms[1:]:
        total = total * factor + term
    return total


def held_states(m, xs, pw):
    a, a8 = row(pw, 0, pl.ds(m, 1)), row(pw, 1, pl.ds(m, 1))
    held = []
    for chunk in xs:
        own = horner(chunk, a)
        held.append(held[-1] * a8 + own if held else own)
    return held


def back_states(m, gs, pw):
    a, a8 = row(pw, 0, pl.ds(m, 1)), row(pw, 1, pl.ds(m, 1))
    opens = [horner(chunk[::-1], a) for chunk in gs]
    back = opens[-1:]
    for own in reversed(opens[:-1]):
        back.insert(0, back[0] * a8 + own)
    return back, opens


def by_span(scratch, half, j):
    return scratch[pl.ds(half * SUB * SUB + j, SUB, stride=SUB), :]


def gather_kernel(*refs):
    sources = refs[:4]
    xf, gf, residue_ref, decay_ref, segment, message, *scratch, x_ref, g_ref, sems = refs[4:]
    staged = x_ref, g_ref, residue_ref, decay_ref
    copies = [pltpu.make_async_copy(*pair, sems.at[i]) for i, pair in enumerate(zip(sources, staged))]
    for copy in copies:
        copy.start()
    modes, channels = decay_ref.shape
    tokens = x_ref.shape[0]
    chunks = tokens // (SUB * SUB)
    span = chunks * SUB
    closing, opening, grad = (segment.at[pl.ds(i * modes, modes)] for i in range(3))
    order = token_order(tokens)
    for copy in copies:
        copy.wait()
    xf[...] = jnp.dot(order, x_ref[...], preferred_element_type=F32)
    gf[...] = jnp.dot(order, g_ref[...], preferred_element_type=F32)

    def tile_step(tile):
        lanes = pl.ds(tile * LANES, LANES)
        pw, ends, starts, inner, before = (ref.at[tile % 2] for ref in scratch)
        decay = decay_ref[:, lanes]
        powers(decay, pw)
        xs = read_tokens(xf, chunks, lanes)
        for m in range(modes):
            held = held_states(m, xs, pw)
            ends[pl.ds(m * SUB, SUB), :] = held[-1]
            for p in range(chunks - 1):
                before[m, p] = held[p]
        gs = read_tokens(gf, chunks, lanes)
        for m in range(modes):
            back, opens = back_states(m, gs, pw)
            rows = pl.ds(m * SUB, SUB)
            starts[rows, :] = back[0]
            inner[rows, :] = sum(opens[p] * before[m, p - 1] for p in range(1, chunks))
        lagged = [0.0] * SUB
        for p in range(chunks):
            xs, gs = read_chunk(xf, p, lanes), read_chunk(gf, p, lanes)
            for lag in range(SUB):
                lagged[lag] = lagged[lag] + sum(gs[r] * xs[r - lag] for r in range(lag, SUB))
        lagged = [jnp.sum(total, axis=0, keepdims=True) for total in lagged]
        for half in range(modes // SUB):
            some = pl.ds(half * SUB, SUB)
            a = pw[0, some, :]
            across = jnp.exp(-decay[half * SUB:(half + 1) * SUB] * span)
            arriving = jnp.zeros((SUB, LANES), F32)
            cross = jnp.zeros((SUB, LANES), F32)
            for j in range(SUB):
                cross = cross + (by_span(inner, half, j) + by_span(starts, half, j) * arriving)
                arriving = arriving * across + by_span(ends, half, j)
            leaving = horner([by_span(starts, half, j) for j in reversed(range(SUB))], across)
            near = horner([jnp.broadcast_to(v, (SUB, LANES)) for v in reversed(lagged)], a)
            closing[some, lanes] = arriving
            opening[some, lanes] = leaving
            grad[some, lanes] = near + a * cross

    for tile in range(channels // LANES):
        tile_step(tile)

    own_high = owns_high()
    half = modes // 2
    for i in range(3):
        low, high = segment[pl.ds(i * modes, half)], segment[pl.ds(i * modes + half, half)]
        message[pl.ds(i * half, half)] = jnp.where(own_high, low, high)


def on_second():
    return lax.rem(lax.axis_index("ctx"), 2) == 1


def owns_high():
    place, group = lax.axis_index("ctx"), lax.axis_index("ch")
    bits = place ^ group
    for shift in (16, 8, 4, 2, 1):
        bits = bits ^ lax.shift_right_logical(bits, jnp.int32(shift))
    return lax.rem(bits, 2) == 1


def own_half(high, values):
    half = values.shape[0] // 2
    return jnp.where(high, values[half:], values[:half])


def in_order(second, own, other):
    return jnp.where(second, other, own), jnp.where(second, own, other)


def local_kernel(tiles, xf, gf, residue_ref, decay_ref, _, out_ref, back_ref,
                 pw, ends, starts, before, after, arrive, leave):
    modes, channels = decay_ref.shape
    chunks = xf.shape[0] // (SUB * SUB)
    span = chunks * SUB

    def tile_step(tile, _):
        lanes = pl.ds(pl.multiple_of(tile * LANES, LANES), LANES)
        decay = decay_ref[:, lanes]
        residue = residue_ref[:, lanes]
        powers(decay, pw)
        pw[2] = residue * pw[0]
        xs, gs = read_tokens(xf, chunks, lanes), read_tokens(gf, chunks, lanes)
        for m in range(modes):
            held, (back, _) = held_states(m, xs, pw), back_states(m, gs, pw)
            rows = pl.ds(m * SUB, SUB)
            ends[rows, :] = held[-1]
            starts[rows, :] = back[0]
            for p in range(1, chunks):
                before[m, p - 1] = held[p - 1]
                after[m, p - 1] = back[p]
        for half in range(modes // SUB):
            across = jnp.exp(-decay[half * SUB:(half + 1) * SUB] * span)
            for target, source, order in ((arrive, ends, range(SUB)), (leave, starts, range(SUB - 1, -1, -1))):
                running = jnp.zeros((SUB, LANES), F32)
                for j in order:
                    target[pl.ds(half * SUB * SUB + j, SUB, stride=SUB), :] = running
                    running = running * across + by_span(source, half, j)
        taps = []
        weight = residue
        for lag in range(SUB):
            taps.append(jnp.broadcast_to(jnp.sum(weight, axis=0, keepdims=True), (SUB, LANES)))
            weight = weight * pw[0]
        for values, carried, inside, target, forward in (
            (xs, arrive, before, out_ref, True), (gs, leave, after, back_ref, False)
        ):
            order = range(SUB) if forward else range(SUB - 1, -1, -1)
            totals = []
            for p in range(chunks):
                seq = [values[p][r] for r in order]
                totals.append([sum(taps[lag] * seq[r - lag] for lag in range(r + 1)) for r in range(SUB)])
            for m in range(modes):
                a, a8, first = (row(pw, i, pl.ds(m, 1)) for i in range(3))
                edge = carried[pl.ds(m * SUB, SUB), :]
                for q in range(chunks):
                    p = q if forward else chunks - 1 - q
                    if q == 0:
                        state = edge
                    else:
                        edge = edge * a8
                        state = edge + inside[m, p - 1 if forward else p]
                    wave = state * first
                    for r in range(SUB):
                        totals[p][r] = totals[p][r] + wave
                        if r < SUB - 1:
                            wave = wave * a
            for p in range(chunks):
                for r, at in enumerate(order):
                    target[tile - tiles[0], p * SUB + at] = totals[p][r]
        return 0

    lax.fori_loop(tiles[0], tiles[1], tile_step, 0)


def join_chip_kernel(tokens, segment, other, decay_ref, _, joined, core):
    modes = decay_ref.shape[0]
    half = modes // 2
    high = owns_high()
    decay = own_half(high, decay_ref[...])
    mine = [own_half(high, segment[i * modes:(i + 1) * modes]) for i in range(3)]
    theirs = [other[i * half:(i + 1) * half] for i in range(3)]
    (close0, close1), (open0, open1), _ = (in_order(on_second(), a, b) for a, b in zip(mine, theirs))
    block = jnp.exp(decay * (-1.0 * tokens))
    joined[0:half] = block * close0 + close1
    joined[half:2 * half] = open0 + block * open1
    joined[2 * half:] = (mine[2] + theirs[2]) + jnp.exp(-decay) * open1 * close0
    core[0:half] = close0
    core[half:] = open1


def join_kernel(tokens, size, masks, last, *refs):
    count = len(masks)
    segments = refs[:count]
    core, decay_ref, carried, _ = refs[count:count + 4]
    *outs, ordered = refs[count + 4:]
    second = on_second()
    decay = own_half(owns_high(), decay_ref[...])
    half = decay.shape[0]
    chip = lax.div(lax.axis_index("ctx"), 2)
    place = lax.rem(lax.div(chip, size), count)
    for mask, segment in zip(masks, segments):
        ordered[place ^ mask] = segment[...]
    block = jnp.exp(decay * (-2.0 * size * tokens))
    zero = jnp.zeros_like(decay)
    close, cross, grad, incoming = zero, zero, zero, zero
    for k in range(count):
        grad = grad + ordered[k, 2 * half:]
        if k:
            cross = cross + ordered[k, half:2 * half] * close
            incoming = jnp.where(place == k, close, incoming)
        close = close * block + ordered[k, 0:half]
    begin, outgoing = zero, zero
    for k in reversed(range(count)):
        outgoing = jnp.where(place == k, begin, outgoing)
        begin = begin * block + ordered[k, half:2 * half]
    grad = grad + jnp.exp(-decay) * cross
    if size > 1:
        inside = lax.rem(chip, size)
        incoming = carried[0:half] + incoming * jnp.exp(decay * (inside * (-2 * tokens)).astype(F32))
        outgoing = carried[half:] + outgoing * jnp.exp(decay * ((size - 1 - inside) * (-2 * tokens)).astype(F32))
    if not last:
        joined, arrivals = outs
        joined[0:half] = close
        joined[half:2 * half] = begin
        joined[2 * half:] = grad
        arrivals[0:half] = incoming
        arrivals[half:] = outgoing
        return
    total, own, message = outs
    total[...] = grad
    block = jnp.exp(decay * (-1.0 * tokens))
    into = incoming, block * incoming + core[0:half]
    out = block * outgoing + core[half:], outgoing
    own[0:half] = jnp.where(second, into[1], into[0])
    own[half:] = jnp.where(second, out[1], out[0])
    message[0:half] = jnp.where(second, into[0], into[1])
    message[half:] = jnp.where(second, out[0], out[1])


def finish_kernel(tiles, ranges, residue_ref, decay_ref, own, other, *refs):
    nears = refs[:2 * len(ranges)]
    out_hbm, back_hbm, finished, out_ref, back_ref, results, pws, arrive, leave, sems = refs[-10:]
    modes, channels = decay_ref.shape
    half = modes // 2
    chunks = nears[0].shape[1] // SUB
    span = chunks * SUB
    own_high = owns_high()
    first = residue_ref[...] * jnp.exp(-decay_ref[...])
    for target, rows in ((arrive, slice(0, half)), (leave, slice(half, modes))):
        low, high = in_order(own_high, own[rows], other[rows])
        target[0:half] = low * first[0:half]
        target[half:] = high * first[half:]

    def copy_out(tile, which):
        lanes = pl.ds(tile * LANES, LANES)
        source, target = ((out_ref, out_hbm), (back_ref, back_hbm))[which]
        return pltpu.make_async_copy(source.at[:, lanes], target.at[:, lanes], sems.at[which, tile])

    def tile_step(tile):
        part, = [i for i, (first, last) in enumerate(ranges) if first <= tile < last]
        near_out, near_back = (near.at[tile - ranges[part][0]] for near in nears[2 * part:2 * part + 2])
        pw = pws.at[tile % 2]
        lanes = pl.ds(tile * LANES, LANES)
        decay = decay_ref[:, lanes]
        powers(decay, pw)
        pw[2] = decay * (-1.0 * span)
        pw[3] = arrive[:, lanes]
        pw[4] = leave[:, lanes]
        level = lax.broadcasted_iota(jnp.int32, (SUB, LANES), 0).astype(F32)
        for near, target, forward in ((near_out, out_ref, True), (near_back, back_ref, False)):
            result = results.at[2 * (tile % 2) + forward]
            order = range(SUB) if forward else range(SUB - 1, -1, -1)
            spans = level if forward else SUB - 1.0 - level
            totals = [[near[p * SUB + r] for r in range(SUB)] for p in range(chunks)]
            for m in range(modes):
                a, a8, rate = (row(pw, i, pl.ds(m, 1)) for i in range(3))
                state = row(pw, 3 if forward else 4, pl.ds(m, 1)) * jnp.exp(rate * spans)
                for q in range(chunks):
                    p = q if forward else chunks - 1 - q
                    wave = state
                    for r in order:
                        totals[p][r] = totals[p][r] + wave
                        wave = wave * a
                    if q < chunks - 1:
                        state = state * a8
            for p in range(chunks):
                for r in range(SUB):
                    result[pl.ds(p * SUB + r, SUB, stride=span), :] = totals[p][r]
            target[:, lanes] = result[...].astype(target.dtype)
            copy_out(tile, 0 if forward else 1).start()

    for tile in range(*tiles):
        tile_step(tile)
    for tile in range(*tiles):
        for which in range(2):
            copy_out(tile, which).wait()
    finished[...] = jnp.zeros(finished.shape, F32)


def sum_kernel(own, other, *refs):
    refs[-1][...] = own[...] + other[...]


def assemble_kernel(scale, own, other, out_ref):
    half = own.shape[0]
    low, high = in_order(owns_high(), own[...], other[...])
    out_ref[0:half] = low * scale
    out_ref[half:] = high * scale


def vmem(*shape):
    return pltpu.VMEM(shape, F32)


def shaped(*shape):
    return jax.ShapeDtypeStruct(shape, F32)


def cost(flops, transcendentals, nbytes):
    return pl.CostEstimate(flops=flops, transcendentals=transcendentals, bytes_accessed=nbytes)


PARAMS = pltpu.CompilerParams(vmem_limit_bytes=32 * 1024 * 1024)
WHOLE = pl.BlockSpec(memory_space=pltpu.VMEM)
HBM = pl.BlockSpec(memory_space=pltpu.HBM)


UNREAD = pl.BlockSpec(memory_space=pl.ANY)


def body(signal, cotangent, residue, decay):
    tokens, channels = signal.shape
    modes = decay.shape[0]
    half = modes // 2
    n, groups = lax.axis_size("ctx"), lax.axis_size("ch")
    chunks = tokens // (SUB * SUB)
    elements = tokens * channels
    spans = vmem(modes * SUB, LANES)
    tiles = channels // LANES
    quarter = tiles // 4
    ranges = [(0, quarter), (quarter, tiles)]
    small = dict(compiler_params=PARAMS, cost_estimate=cost(elements, modes * channels, modes * channels * 32))

    def swap(x, ctx_mask, ch_mask=0):
        if ctx_mask != 1:
            ctx_mask |= (ctx_mask.bit_count() + ch_mask.bit_count()) % 2
        mask = ctx_mask * groups + ch_mask
        return lax.ppermute(x, ("ctx", "ch"), [(i, i ^ mask) for i in range(n * groups)])

    def near_part(part, after):
        first, last = ranges[part]
        share = elements * modes * (last - first) // tiles
        return pl.pallas_call(
            functools.partial(local_kernel, ranges[part]),
            out_shape=[shaped(last - first, chunks * SUB, SUB, LANES)] * 2,
            in_specs=[WHOLE] * 4 + [UNREAD],
            scratch_shapes=[vmem(3, modes, LANES), spans, spans]
            + [vmem(modes, chunks - 1, SUB, LANES)] * 2
            + [spans, spans],
            compiler_params=PARAMS,
            cost_estimate=cost(share * 400, 0, share),
            name="local_convolutions",
        )(*inputs, after)

    values = shaped(tokens, channels)
    *inputs, segment, message = pl.pallas_call(
        gather_kernel,
        out_shape=[values, values]
        + [shaped(modes, channels)] * 2
        + [shaped(3 * modes, channels), shaped(3 * half, channels)],
        in_specs=[HBM] * 4,
        scratch_shapes=[vmem(2, 2, modes, LANES)]
        + [vmem(2, modes * SUB, LANES)] * 3
        + [vmem(2, modes, chunks - 1, SUB, LANES)]
        + [pltpu.VMEM(signal.shape, signal.dtype)] * 2
        + [pltpu.SemaphoreType.DMA((4,))],
        compiler_params=PARAMS,
        cost_estimate=cost(elements * modes * 5, modes * channels * 3, elements * 6),
        name="block_states",
    )(*(pltpu.with_memory_space_constraint(a, pltpu.HBM) for a in (signal, cotangent, residue, decay)))
    residue, decay = inputs[2:]

    other = swap(message, 1)
    near = near_part(0, segment)
    joined, core = pl.pallas_call(
        functools.partial(join_chip_kernel, tokens),
        out_shape=[shaped(3 * half, channels), shaped(2 * half, channels)],
        in_specs=[WHOLE] * 3 + [UNREAD],
        name="join_chip",
        **small,
    )(segment, other, decay, near[0])

    chips = n // 2
    size = 1
    carried = core
    while size < chips:
        count = min(4, chips // size)
        last = size * count == chips
        masks = [2, 1, 3] if count == 4 else [1]
        others = [swap(joined, 2 * size * m) for m in masks]
        if last:
            near = near + near_part(1, joined)
        rows = [half, 2 * half, 2 * half] if last else [3 * half, 2 * half]
        joined, carried, *message = pl.pallas_call(
            functools.partial(join_kernel, tokens, size, [0] + masks, last),
            out_shape=[shaped(r, channels) for r in rows],
            in_specs=[WHOLE] * (count + 3) + [UNREAD],
            scratch_shapes=[vmem(count, 3 * half, channels)],
            name="join_chips",
            **small,
        )(joined, *others, core, decay, carried, near[-1])
        size *= count

    def finish_part(part, after, written):
        return pl.pallas_call(
            functools.partial(finish_kernel, ranges[part], ranges),
            out_shape=[jax.ShapeDtypeStruct((tokens, channels), jnp.bfloat16)] * 2 + [shaped(SUB, LANES)],
            in_specs=[WHOLE] * (4 + len(near)) + [UNREAD] + [HBM] * len(written),
            out_specs=[HBM] * 2 + [WHOLE],
            input_output_aliases={5 + len(near) + i: i for i in range(len(written))},
            scratch_shapes=[pltpu.VMEM((tokens, channels), jnp.bfloat16)] * 2
            + [vmem(4, tokens, LANES), vmem(2, 5, modes, LANES)]
            + [vmem(modes, channels)] * 2
            + [pltpu.SemaphoreType.DMA((2, tiles))],
            compiler_params=PARAMS,
            cost_estimate=cost(elements * modes * 300, 0, elements * 6),
            name="add_arrivals",
        )(residue, decay, carried, received, *near, after, *written)

    received = swap(message[0], 1)
    grad = joined
    written = []
    stride = groups // 2
    while stride:
        other = swap(grad, 0, stride)
        pinned = []
        if stride == groups // 2:
            *written, finished = finish_part(0, grad, written)
            pinned = [finished]
        if stride == 1:
            *written, finished = finish_part(1, grad, written)
            pinned = [finished]
        grad = pl.pallas_call(
            sum_kernel,
            out_shape=shaped(half, channels),
            in_specs=[WHOLE] * 2 + [UNREAD] * len(pinned),
            name="sum_groups",
            **small,
        )(grad, other, *pinned)
        stride //= 2
    residue_grad = pl.pallas_call(
        functools.partial(assemble_kernel, 1.0 / (tokens * n)),
        out_shape=shaped(modes, channels),
        name="assemble_gradient",
        **small,
    )(grad, swap(grad, 1))
    return *written, residue_grad


def solution(mesh):
    return jax.shard_map(
        body,
        mesh=mesh,
        in_specs=(P("ctx", "ch"), P("ctx", "ch"), P(), P()),
        out_specs=(P("ctx", "ch"), P("ctx", "ch"), P()),
        check_vma=False,
    )
```

```python
import functools

import jax
import jax.numpy as jnp
from jax import lax
from jax.experimental import pallas as pl
from jax.experimental.pallas import tpu as pltpu
from jax.sharding import PartitionSpec as P

SUB = 8
LANES = 128
F32 = jnp.float32


def row(ref, *index):
    return jnp.broadcast_to(ref[index], (SUB, LANES))


def token_order(tokens):
    rows = lax.broadcasted_iota(jnp.int32, (tokens, tokens), 0)
    columns = lax.broadcasted_iota(jnp.int32, (tokens, tokens), 1)
    wanted = lax.rem(rows, SUB) * (tokens // SUB) + lax.div(rows, SUB)
    return jnp.where(columns == wanted, 1.0, 0.0).astype(jnp.bfloat16)


def read_chunk(ref, p, lanes):
    return [ref[pl.ds((p * SUB + r) * SUB, SUB), lanes] for r in range(SUB)]


def read_tokens(ref, chunks, lanes):
    return [read_chunk(ref, p, lanes) for p in range(chunks)]


def powers(decay, pw):
    pw[0] = jnp.exp(-decay)
    pw[1] = jnp.exp(-decay * SUB)


def horner(terms, factor):
    total = terms[0]
    for term in terms[1:]:
        total = total * factor + term
    return total


def held_states(m, xs, pw):
    a, a8 = row(pw, 0, pl.ds(m, 1)), row(pw, 1, pl.ds(m, 1))
    held = []
    for chunk in xs:
        own = horner(chunk, a)
        held.append(held[-1] * a8 + own if held else own)
    return held


def back_states(m, gs, pw):
    a, a8 = row(pw, 0, pl.ds(m, 1)), row(pw, 1, pl.ds(m, 1))
    opens = [horner(chunk[::-1], a) for chunk in gs]
    back = opens[-1:]
    for own in reversed(opens[:-1]):
        back.insert(0, back[0] * a8 + own)
    return back, opens


def by_span(scratch, half, j):
    return scratch[pl.ds(half * SUB * SUB + j, SUB, stride=SUB), :]


def gather_kernel(*refs):
    sources = refs[:4]
    xf, gf, residue_ref, decay_ref, segment, message, *scratch, x_ref, g_ref, sems = refs[4:]
    staged = x_ref, g_ref, residue_ref, decay_ref
    copies = [pltpu.make_async_copy(*pair, sems.at[i]) for i, pair in enumerate(zip(sources, staged))]
    for copy in copies:
        copy.start()
    modes, channels = decay_ref.shape
    tokens = x_ref.shape[0]
    chunks = tokens // (SUB * SUB)
    span = chunks * SUB
    closing, opening, grad = (segment.at[pl.ds(i * modes, modes)] for i in range(3))
    order = token_order(tokens)
    for copy in copies:
        copy.wait()
    xf[...] = jnp.dot(order, x_ref[...], preferred_element_type=F32)
    gf[...] = jnp.dot(order, g_ref[...], preferred_element_type=F32)

    def tile_step(tile):
        lanes = pl.ds(tile * LANES, LANES)
        pw, ends, starts, inner, before = (ref.at[tile % 2] for ref in scratch)
        decay = decay_ref[:, lanes]
        powers(decay, pw)
        xs = read_tokens(xf, chunks, lanes)
        for m in range(modes):
            held = held_states(m, xs, pw)
            ends[pl.ds(m * SUB, SUB), :] = held[-1]
            for p in range(chunks - 1):
                before[m, p] = held[p]
        gs = read_tokens(gf, chunks, lanes)
        for m in range(modes):
            back, opens = back_states(m, gs, pw)
            rows = pl.ds(m * SUB, SUB)
            starts[rows, :] = back[0]
            inner[rows, :] = sum(opens[p] * before[m, p - 1] for p in range(1, chunks))
        lagged = [0.0] * SUB
        for p in range(chunks):
            xs, gs = read_chunk(xf, p, lanes), read_chunk(gf, p, lanes)
            for lag in range(SUB):
                lagged[lag] = lagged[lag] + sum(gs[r] * xs[r - lag] for r in range(lag, SUB))
        lagged = [jnp.sum(total, axis=0, keepdims=True) for total in lagged]
        for half in range(modes // SUB):
            some = pl.ds(half * SUB, SUB)
            a = pw[0, some, :]
            across = jnp.exp(-decay[half * SUB:(half + 1) * SUB] * span)
            arriving = jnp.zeros((SUB, LANES), F32)
            cross = jnp.zeros((SUB, LANES), F32)
            for j in range(SUB):
                cross = cross + (by_span(inner, half, j) + by_span(starts, half, j) * arriving)
                arriving = arriving * across + by_span(ends, half, j)
            leaving = horner([by_span(starts, half, j) for j in reversed(range(SUB))], across)
            near = horner([jnp.broadcast_to(v, (SUB, LANES)) for v in reversed(lagged)], a)
            closing[some, lanes] = arriving
            opening[some, lanes] = leaving
            grad[some, lanes] = near + a * cross

    for tile in range(channels // LANES):
        tile_step(tile)

    own_high = owns_high()
    half = modes // 2
    for i in range(3):
        low, high = segment[pl.ds(i * modes, half)], segment[pl.ds(i * modes + half, half)]
        message[pl.ds(i * half, half)] = jnp.where(own_high, low, high)


def on_second():
    return lax.rem(lax.axis_index("ctx"), 2) == 1


def owns_high():
    place, group = lax.axis_index("ctx"), lax.axis_index("ch")
    bits = place ^ group
    for shift in (16, 8, 4, 2, 1):
        bits = bits ^ lax.shift_right_logical(bits, jnp.int32(shift))
    return lax.rem(bits, 2) == 1


def own_half(high, values):
    half = values.shape[0] // 2
    return jnp.where(high, values[half:], values[:half])


def in_order(second, own, other):
    return jnp.where(second, other, own), jnp.where(second, own, other)


def local_kernel(tiles, xf, gf, residue_ref, decay_ref, _, out_ref, back_ref,
                 pw, ends, starts, before, after, arrive, leave):
    modes, channels = decay_ref.shape
    chunks = xf.shape[0] // (SUB * SUB)
    span = chunks * SUB

    def tile_step(tile, _):
        lanes = pl.ds(pl.multiple_of(tile * LANES, LANES), LANES)
        decay = decay_ref[:, lanes]
        residue = residue_ref[:, lanes]
        powers(decay, pw)
        pw[2] = residue * pw[0]
        xs, gs = read_tokens(xf, chunks, lanes), read_tokens(gf, chunks, lanes)
        for m in range(modes):
            held, (back, _) = held_states(m, xs, pw), back_states(m, gs, pw)
            rows = pl.ds(m * SUB, SUB)
            ends[rows, :] = held[-1]
            starts[rows, :] = back[0]
            for p in range(1, chunks):
                before[m, p - 1] = held[p - 1]
                after[m, p - 1] = back[p]
        for half in range(modes // SUB):
            across = jnp.exp(-decay[half * SUB:(half + 1) * SUB] * span)
            for target, source, order in ((arrive, ends, range(SUB)), (leave, starts, range(SUB - 1, -1, -1))):
                running = jnp.zeros((SUB, LANES), F32)
                for j in order:
                    target[pl.ds(half * SUB * SUB + j, SUB, stride=SUB), :] = running
                    running = running * across + by_span(source, half, j)
        taps = []
        weight = residue
        for lag in range(SUB):
            taps.append(jnp.broadcast_to(jnp.sum(weight, axis=0, keepdims=True), (SUB, LANES)))
            weight = weight * pw[0]
        for values, carried, inside, target, forward in (
            (xs, arrive, before, out_ref, True), (gs, leave, after, back_ref, False)
        ):
            order = range(SUB) if forward else range(SUB - 1, -1, -1)
            totals = []
            for p in range(chunks):
                seq = [values[p][r] for r in order]
                totals.append([sum(taps[lag] * seq[r - lag] for lag in range(r + 1)) for r in range(SUB)])
            for m in range(modes):
                a, a8, first = (row(pw, i, pl.ds(m, 1)) for i in range(3))
                edge = carried[pl.ds(m * SUB, SUB), :]
                for q in range(chunks):
                    p = q if forward else chunks - 1 - q
                    if q == 0:
                        state = edge
                    else:
                        edge = edge * a8
                        state = edge + inside[m, p - 1 if forward else p]
                    wave = state * first
                    for r in range(SUB):
                        totals[p][r] = totals[p][r] + wave
                        if r < SUB - 1:
                            wave = wave * a
            for p in range(chunks):
                for r, at in enumerate(order):
                    target[tile - tiles[0], p * SUB + at] = totals[p][r]
        return 0

    lax.fori_loop(tiles[0], tiles[1], tile_step, 0)


def join_chip_kernel(tokens, segment, other, decay_ref, _, joined, core):
    modes = decay_ref.shape[0]
    half = modes // 2
    high = owns_high()
    decay = own_half(high, decay_ref[...])
    mine = [own_half(high, segment[i * modes:(i + 1) * modes]) for i in range(3)]
    theirs = [other[i * half:(i + 1) * half] for i in range(3)]
    (close0, close1), (open0, open1), _ = (in_order(on_second(), a, b) for a, b in zip(mine, theirs))
    block = jnp.exp(decay * (-1.0 * tokens))
    joined[0:half] = block * close0 + close1
    joined[half:2 * half] = open0 + block * open1
    joined[2 * half:] = (mine[2] + theirs[2]) + jnp.exp(-decay) * open1 * close0
    core[0:half] = close0
    core[half:] = open1


def join_kernel(tokens, size, masks, last, *refs):
    count = len(masks)
    segments = refs[:count]
    core, decay_ref, carried, _ = refs[count:count + 4]
    *outs, ordered = refs[count + 4:]
    second = on_second()
    decay = own_half(owns_high(), decay_ref[...])
    half = decay.shape[0]
    chip = lax.div(lax.axis_index("ctx"), 2)
    place = lax.rem(lax.div(chip, size), count)
    for mask, segment in zip(masks, segments):
        ordered[place ^ mask] = segment[...]
    block = jnp.exp(decay * (-2.0 * size * tokens))
    zero = jnp.zeros_like(decay)
    close, cross, grad, incoming = zero, zero, zero, zero
    for k in range(count):
        grad = grad + ordered[k, 2 * half:]
        if k:
            cross = cross + ordered[k, half:2 * half] * close
            incoming = jnp.where(place == k, close, incoming)
        close = close * block + ordered[k, 0:half]
    begin, outgoing = zero, zero
    for k in reversed(range(count)):
        outgoing = jnp.where(place == k, begin, outgoing)
        begin = begin * block + ordered[k, half:2 * half]
    grad = grad + jnp.exp(-decay) * cross
    if size > 1:
        inside = lax.rem(chip, size)
        incoming = carried[0:half] + incoming * jnp.exp(decay * (inside * (-2 * tokens)).astype(F32))
        outgoing = carried[half:] + outgoing * jnp.exp(decay * ((size - 1 - inside) * (-2 * tokens)).astype(F32))
    if not last:
        joined, arrivals = outs
        joined[0:half] = close
        joined[half:2 * half] = begin
        joined[2 * half:] = grad
        arrivals[0:half] = incoming
        arrivals[half:] = outgoing
        return
    total, own, message = outs
    total[...] = grad
    block = jnp.exp(decay * (-1.0 * tokens))
    into = incoming, block * incoming + core[0:half]
    out = block * outgoing + core[half:], outgoing
    own[0:half] = jnp.where(second, into[1], into[0])
    own[half:] = jnp.where(second, out[1], out[0])
    message[0:half] = jnp.where(second, into[0], into[1])
    message[half:] = jnp.where(second, out[0], out[1])


def finish_kernel(tiles, ranges, residue_ref, decay_ref, own, other, *refs):
    nears = refs[:2 * len(ranges)]
    out_hbm, back_hbm, finished, out_ref, back_ref, results, pws, arrive, leave, sems = refs[-10:]
    modes, channels = decay_ref.shape
    half = modes // 2
    chunks = nears[0].shape[1] // SUB
    span = chunks * SUB
    own_high = owns_high()
    first = residue_ref[...] * jnp.exp(-decay_ref[...])
    for target, rows in ((arrive, slice(0, half)), (leave, slice(half, modes))):
        low, high = in_order(own_high, own[rows], other[rows])
        target[0:half] = low * first[0:half]
        target[half:] = high * first[half:]

    def copy_out(tile, which):
        lanes = pl.ds(tile * LANES, LANES)
        source, target = ((out_ref, out_hbm), (back_ref, back_hbm))[which]
        return pltpu.make_async_copy(source.at[:, lanes], target.at[:, lanes], sems.at[which, tile])

    def tile_step(tile):
        part, = [i for i, (first, last) in enumerate(ranges) if first <= tile < last]
        near_out, near_back = (near.at[tile - ranges[part][0]] for near in nears[2 * part:2 * part + 2])
        pw = pws.at[tile % 2]
        lanes = pl.ds(tile * LANES, LANES)
        decay = decay_ref[:, lanes]
        powers(decay, pw)
        pw[2] = decay * (-1.0 * span)
        pw[3] = arrive[:, lanes]
        pw[4] = leave[:, lanes]
        level = lax.broadcasted_iota(jnp.int32, (SUB, LANES), 0).astype(F32)
        for near, target, forward in ((near_out, out_ref, True), (near_back, back_ref, False)):
            result = results.at[2 * (tile % 2) + forward]
            order = range(SUB) if forward else range(SUB - 1, -1, -1)
            spans = level if forward else SUB - 1.0 - level
            totals = [[near[p * SUB + r] for r in range(SUB)] for p in range(chunks)]
            for m in range(modes):
                a, a8, rate = (row(pw, i, pl.ds(m, 1)) for i in range(3))
                state = row(pw, 3 if forward else 4, pl.ds(m, 1)) * jnp.exp(rate * spans)
                for q in range(chunks):
                    p = q if forward else chunks - 1 - q
                    wave = state
                    for r in order:
                        totals[p][r] = totals[p][r] + wave
                        wave = wave * a
                    if q < chunks - 1:
                        state = state * a8
            for p in range(chunks):
                for r in range(SUB):
                    result[pl.ds(p * SUB + r, SUB, stride=span), :] = totals[p][r]
            target[:, lanes] = result[...].astype(target.dtype)
            copy_out(tile, 0 if forward else 1).start()

    for tile in range(*tiles):
        tile_step(tile)
    for tile in range(*tiles):
        for which in range(2):
            copy_out(tile, which).wait()
    finished[...] = jnp.zeros(finished.shape, F32)


def sum_kernel(own, other, *refs):
    refs[-1][...] = own[...] + other[...]


def assemble_kernel(scale, own, other, out_ref):
    half = own.shape[0]
    low, high = in_order(owns_high(), own[...], other[...])
    out_ref[0:half] = low * scale
    out_ref[half:] = high * scale


def vmem(*shape):
    return pltpu.VMEM(shape, F32)


def shaped(*shape):
    return jax.ShapeDtypeStruct(shape, F32)


def cost(flops, transcendentals, nbytes):
    return pl.CostEstimate(flops=flops, transcendentals=transcendentals, bytes_accessed=nbytes)


PARAMS = pltpu.CompilerParams(vmem_limit_bytes=32 * 1024 * 1024)
WHOLE = pl.BlockSpec(memory_space=pltpu.VMEM)
HBM = pl.BlockSpec(memory_space=pltpu.HBM)


UNREAD = pl.BlockSpec(memory_space=pl.ANY)


def body(signal, cotangent, residue, decay):
    tokens, channels = signal.shape
    modes = decay.shape[0]
    half = modes // 2
    n, groups = lax.axis_size("ctx"), lax.axis_size("ch")
    chunks = tokens // (SUB * SUB)
    elements = tokens * channels
    spans = vmem(modes * SUB, LANES)
    tiles = channels // LANES
    quarter = tiles // 4
    ranges = [(0, quarter), (quarter, tiles)]
    small = dict(compiler_params=PARAMS, cost_estimate=cost(elements, modes * channels, modes * channels * 32))

    def swap(x, ctx_mask, ch_mask=0):
        if ctx_mask != 1:
            ctx_mask |= (ctx_mask.bit_count() + ch_mask.bit_count()) % 2
        mask = ctx_mask * groups + ch_mask
        return lax.ppermute(x, ("ctx", "ch"), [(i, i ^ mask) for i in range(n * groups)])

    def near_part(part, after):
        first, last = ranges[part]
        share = elements * modes * (last - first) // tiles
        return pl.pallas_call(
            functools.partial(local_kernel, ranges[part]),
            out_shape=[shaped(last - first, chunks * SUB, SUB, LANES)] * 2,
            in_specs=[WHOLE] * 4 + [UNREAD],
            scratch_shapes=[vmem(3, modes, LANES), spans, spans]
            + [vmem(modes, chunks - 1, SUB, LANES)] * 2
            + [spans, spans],
            compiler_params=PARAMS,
            cost_estimate=cost(share * 400, 0, share),
            name="local_convolutions",
        )(*inputs, after)

    values = shaped(tokens, channels)
    *inputs, segment, message = pl.pallas_call(
        gather_kernel,
        out_shape=[values, values]
        + [shaped(modes, channels)] * 2
        + [shaped(3 * modes, channels), shaped(3 * half, channels)],
        in_specs=[HBM] * 4,
        scratch_shapes=[vmem(2, 2, modes, LANES)]
        + [vmem(2, modes * SUB, LANES)] * 3
        + [vmem(2, modes, chunks - 1, SUB, LANES)]
        + [pltpu.VMEM(signal.shape, signal.dtype)] * 2
        + [pltpu.SemaphoreType.DMA((4,))],
        compiler_params=PARAMS,
        cost_estimate=cost(elements * modes * 5, modes * channels * 3, elements * 6),
        name="block_states",
    )(*(pltpu.with_memory_space_constraint(a, pltpu.HBM) for a in (signal, cotangent, residue, decay)))
    residue, decay = inputs[2:]

    other = swap(message, 1)
    near = near_part(0, segment)
    joined, core = pl.pallas_call(
        functools.partial(join_chip_kernel, tokens),
        out_shape=[shaped(3 * half, channels), shaped(2 * half, channels)],
        in_specs=[WHOLE] * 3 + [UNREAD],
        name="join_chip",
        **small,
    )(segment, other, decay, near[0])

    chips = n // 2
    size = 1
    carried = core
    while size < chips:
        count = min(4, chips // size)
        last = size * count == chips
        masks = [2, 1, 3] if count == 4 else [1]
        others = [swap(joined, 2 * size * m) for m in masks]
        if last:
            near = near + near_part(1, joined)
        rows = [half, 2 * half, 2 * half] if last else [3 * half, 2 * half]
        joined, carried, *message = pl.pallas_call(
            functools.partial(join_kernel, tokens, size, [0] + masks, last),
            out_shape=[shaped(r, channels) for r in rows],
            in_specs=[WHOLE] * (count + 3) + [UNREAD],
            scratch_shapes=[vmem(count, 3 * half, channels)],
            name="join_chips",
            **small,
        )(joined, *others, core, decay, carried, near[-1])
        size *= count

    def finish_part(part, after, written):
        return pl.pallas_call(
            functools.partial(finish_kernel, (part * tiles // 2, (part + 1) * tiles // 2), ranges),
            out_shape=[jax.ShapeDtypeStruct((tokens, channels), jnp.bfloat16)] * 2 + [shaped(SUB, LANES)],
            in_specs=[WHOLE] * (4 + len(near)) + [UNREAD] + [HBM] * len(written),
            out_specs=[HBM] * 2 + [WHOLE],
            input_output_aliases={5 + len(near) + i: i for i in range(len(written))},
            scratch_shapes=[pltpu.VMEM((tokens, channels), jnp.bfloat16)] * 2
            + [vmem(4, tokens, LANES), vmem(2, 5, modes, LANES)]
            + [vmem(modes, channels)] * 2
            + [pltpu.SemaphoreType.DMA((2, tiles))],
            compiler_params=PARAMS,
            cost_estimate=cost(elements * modes * 300, 0, elements * 6),
            name="add_arrivals",
        )(residue, decay, carried, received, *near, after, *written)

    received = swap(message[0], 1)
    grad = joined
    written = []
    stride = groups // 2
    while stride:
        other = swap(grad, 0, stride)
        pinned = []
        if stride == groups // 2:
            *written, finished = finish_part(0, grad, written)
            pinned = [finished]
        if stride == 1:
            *written, finished = finish_part(1, grad, written)
            pinned = [finished]
        grad = pl.pallas_call(
            sum_kernel,
            out_shape=shaped(half, channels),
            in_specs=[WHOLE] * 2 + [UNREAD] * len(pinned),
            name="sum_groups",
            **small,
        )(grad, other, *pinned)
        stride //= 2
    residue_grad = pl.pallas_call(
        functools.partial(assemble_kernel, 1.0 / (tokens * n)),
        out_shape=shaped(modes, channels),
        name="assemble_gradient",
        **small,
    )(grad, swap(grad, 1))
    return *written, residue_grad


def solution(mesh):
    return jax.shard_map(
        body,
        mesh=mesh,
        in_specs=(P("ctx", "ch"), P("ctx", "ch"), P(), P()),
        out_specs=(P("ctx", "ch"), P("ctx", "ch"), P()),
        check_vma=False,
    )
```
